32 devices in a mesh: groups: 2 (over y), pipe: 4 (over z), hour: 2 (over x), seg: 2 (over core).
Axes of the slice: x: 2, y: 2, z: 4, core: 2. Of those that a mesh axis runs over, the one named last changes fastest.
Arguments:
- segment_flow: float32 [16, 64, 1024], P(('groups', 'hour'), 'seg', 'pipe'), parts along dimension 0, may hold values from -4 to 4
- linepack: float32 [16, 64, 1024], P(('groups', 'hour'), 'seg', 'pipe'), parts along dimension 0, may hold values from 0.2 to 2.4
- mass_dual: float32 [16, 64, 1024], P(('groups', 'hour'), 'seg', 'pipe'), parts along dimension 0, may hold values from -3 to 3
- momentum_dual: float32 [16, 64, 1024], P(('groups', 'hour'), 'seg', 'pipe'), parts along dimension 0, may hold values from -3 to 3
- contract_dual: float32 [16, 2, 32, 128], P(('groups', 'hour'), 'seg', 'pipe'), parts along dimension 0, may hold values from -3 to 3
- flow_cost: float32 [16, 64, 1024], P(('groups', 'hour'), 'seg', 'pipe'), parts along dimension 0, may hold values from -24 to 24
- injection: float32 [16, 64, 1024], P(('groups', 'hour'), 'seg', 'pipe'), parts along dimension 0, may hold values from -3 to 3
- contract_target: float32 [16, 2, 32, 128], P(('groups', 'hour'), 'seg', 'pipe'), parts along dimension 0, may hold values from 0.4 to 2
- friction_table: float32 [16], replicated, may hold values from 0.3 to 3
- friction_class: int32 [64, 2048], P('seg', ('groups', 'pipe')), parts along dimension 1, may hold values from 0 to 15
- matching: int32 [2048], P('groups'), parts along dimension 0, may hold values from 0 to 1023, as said below
- contract_map: int32 [16, 1024], P(('groups', 'hour')), parts along dimension 0, may hold values from 0 to 127
Outputs:
- flow_final: float32 [16, 64, 1024], P(('groups', 'hour'), 'seg', 'pipe'), parts along dimension 0
- linepack_final: float32 [16, 64, 1024], P(('groups', 'hour'), 'seg', 'pipe'), parts along dimension 0
- mass_dual_final: float32 [16, 64, 1024], P(('groups', 'hour'), 'seg', 'pipe'), parts along dimension 0
- momentum_dual_final: float32 [16, 64, 1024], P(('groups', 'hour'), 'seg', 'pipe'), parts along dimension 0
- contract_dual_final: float32 [16, 2, 32, 128], P(('groups', 'hour'), 'seg', 'pipe'), parts along dimension 0
- primal_weight: float32 [2], P('groups'), parts along dimension 0
The draws below stay inside these ranges and needn't reach their ends.
There are 2 independent parts, one for each index of `groups`. The reference program is written for one: setup_inputs(seed, part) draws one part's arguments, and reference() takes and returns one part's arrays. A program takes and returns all parts, laid end to end along the dimension named above; an argument that names none is the same for every part. Nothing has to cross between parts.
Inputs may be any that keep to these rules, and one draw needn't show every extreme that they name: `matching`: every pipe's inlet is fed by the outlet of exactly one pipe: each number of 0 to 1023 appears once; for any two blocks of 256 consecutive pipes, exactly 64 pipes of the first are fed from outlets of the second.
All inputs are finite; a program needn't handle non-finite values.
Results may differ from the reference program's by a relative error of at most 0.0001.
Values sent between devices are 32-bit elements; how exact they have to be, the bound alone decides.
No kernel may reach another device: no remote copies, remote signals or barrier semaphores. Data moves between devices by JAX's collectives and lax.ppermute only.
A program may use at most 64 MiB of HBM per device.

```python
import math
import jax
import jax.numpy as jnp

PIPE_DEV = 256
SEGS = 64
NC = 128
NCLS = 16
ITERS = 2
PIPES = 1024
HOURS = 8
SEG_PARTS = 2
SEG_BLOCK = 32


def draw_flow_cost(key, part):
    normal_key = jax.random.fold_in(jax.random.fold_in(key, 17), 0)
    pipe_rank = jnp.arange(PIPES, dtype=jnp.float32) / PIPES
    pipe_scale = 0.3 * 10.0 ** pipe_rank
    normal_part = jnp.clip(jax.random.normal(normal_key, (HOURS, SEGS, PIPES), jnp.float32), -4.0, 4.0)
    return normal_part * pipe_scale


def draw_matching(key, part):
    base_key = jax.random.fold_in(key, 29)
    block_count = PIPES // PIPE_DEV
    per_peer = PIPE_DEV // block_count
    dest_keys = jax.random.split(jax.random.fold_in(base_key, 1), block_count)
    source_keys = jax.random.split(jax.random.fold_in(base_key, 2), block_count)
    dest_order = jax.vmap(lambda one_key: jax.random.permutation(one_key, PIPE_DEV))(dest_keys).astype(jnp.int32)
    source_order = jax.vmap(lambda one_key: jax.random.permutation(one_key, PIPE_DEV))(source_keys).astype(jnp.int32)
    offsets = jax.random.permutation(jax.random.fold_in(base_key, 3), block_count).astype(jnp.int32)
    blocks = jnp.arange(block_count, dtype=jnp.int32)[:, None]
    group_index = dest_order // per_peer
    slot_index = dest_order % per_peer
    offset_used = jnp.take(offsets, group_index, axis=0)
    source_block = (blocks + offset_used) % block_count
    local_index = source_order[source_block, offset_used * per_peer + slot_index]
    return (source_block * PIPE_DEV + local_index).reshape(-1).astype(jnp.int32)


def place_ends(drawn, rng, least, high):
    longest = drawn.shape.index(max(drawn.shape))
    spots = []
    for shift in (0, 1):
        where = [jax.random.randint(jax.random.fold_in(rng, axis), (), 0, length) for axis, length in enumerate(drawn.shape)]
        where[longest] = (where[longest] + shift) % drawn.shape[longest]
        spots.append(tuple(where))
    return drawn.at[spots[0]].set(least).at[spots[1]].set(high)


def shard_levels(stream_key, shape, cuts, smallest, high):
    gain, own = 1.0, jax.random.fold_in(stream_key, 6)
    for position, shards_of in cuts:
        steps = jnp.exp(jax.random.uniform(jax.random.fold_in(own, position), (shards_of,), jnp.float32, smallest / len(cuts), high / len(cuts)))
        gain = gain * jnp.repeat(steps, shape[position] // shards_of).reshape([-1 if axis == position else 1 for axis in range(len(shape))])
    return gain


def centred(key, shape, scale, reach, pieces=(), kind=jnp.bfloat16):
    array = jax.random.normal(key, shape, jnp.float32) * scale
    if len(pieces) > 0:
        array = shard_levels(key, shape, pieces, -0.22, 0.18) * array
    return jnp.clip(array, min=-reach, max=reach).astype(kind)


def setup_inputs(seed: int = 0, part: int = 0) -> dict:
    seeds = jax.random.split(jax.random.key(seed), 13)
    part_splits = jax.random.split(jax.random.fold_in(seeds[12], part), 13)
    return {
        "segment_flow": centred(part_splits[0], (HOURS, SEGS, PIPES), 1.0, 4.0, ((0, 2), (1, 2), (2, 4)), jnp.float32),
        "linepack": jnp.clip(0.2 + 2.2 * jax.random.uniform(part_splits[1], (HOURS, SEGS, PIPES), jnp.float32) ** shard_levels(part_splits[1], (HOURS, SEGS, PIPES), ((0, 2), (1, 2), (2, 4)), -0.2, 0.2), 0.2, 2.4),
        "mass_dual": centred(part_splits[2], (HOURS, SEGS, PIPES), 0.5, 3.0, ((0, 2), (1, 2), (2, 4)), jnp.float32),
        "momentum_dual": centred(part_splits[3], (HOURS, SEGS, PIPES), 0.5, 3.0, ((0, 2), (1, 2), (2, 4)), jnp.float32),
        "contract_dual": centred(part_splits[4], (HOURS, SEG_PARTS, SEG_BLOCK, NC), 0.5, 3.0, ((0, 2), (1, 2), (2, 4)), jnp.float32),
        "flow_cost": draw_flow_cost(jax.random.fold_in(jax.random.fold_in(seeds[12], part), 71), part),
        "injection": centred(part_splits[6], (HOURS, SEGS, PIPES), 0.5, 3.0, ((0, 2), (1, 2), (2, 4)), jnp.float32),
        "contract_target": jnp.clip(0.4 + 1.6 * jax.random.uniform(part_splits[7], (HOURS, SEG_PARTS, SEG_BLOCK, NC), jnp.float32) ** shard_levels(part_splits[7], (HOURS, SEG_PARTS, SEG_BLOCK, NC), ((0, 2), (1, 2), (2, 4)), -0.2, 0.2), 0.4, 2.0),
        "friction_table": jnp.clip(jnp.exp(jax.random.uniform(seeds[8], (NCLS,), jnp.float32, math.log(0.3), math.log(3.0))), 0.3, 3.0),
        "friction_class": place_ends(jax.random.randint(part_splits[9], (SEGS, PIPES), 0, NCLS), jax.random.fold_in(part_splits[9], 1), 0, NCLS - 1).astype(jnp.int32),
        "matching": draw_matching(jax.random.fold_in(jax.random.fold_in(seeds[12], part), 71), part),
        "contract_map": place_ends(jax.random.randint(part_splits[11], (HOURS, PIPES), 0, NC), jax.random.fold_in(part_splits[11], 1), 0, NC - 1).astype(jnp.int32),
    }


FLOW_CAP = 1.5
PACK_CAP = 2.5
STEP_SCALE = 0.25
NORM_EPS = 1e-06

def contract_sums(linepack, contract_map):
    hour_count, seg_count, pipe_count = linepack.shape
    offsets = contract_map + NC * jnp.arange(hour_count, dtype=jnp.int32)[:, None]
    flattened = jnp.transpose(linepack, (0, 2, 1)).reshape(hour_count * pipe_count, seg_count)
    summed = jax.ops.segment_sum(flattened, offsets.reshape(-1), num_segments=hour_count * NC)
    return jnp.transpose(summed.reshape(hour_count, NC, seg_count), (0, 2, 1))

def contract_spread(duals, contract_map, seg_count):
    pick_index = jnp.broadcast_to(contract_map[:, None, :], (contract_map.shape[0], seg_count, contract_map.shape[1]))
    return jnp.take_along_axis(duals, pick_index, axis=2)

def forward(flow_bar, pack_bar, friction, matching, contract_map, share_scale):
    far_rows = jnp.take(flow_bar[:, -1, :], matching, axis=1)
    upstream = jnp.concatenate([far_rows[:, None, :], flow_bar[:, :-1, :]], axis=1)
    earlier = jnp.concatenate([jnp.zeros_like(pack_bar[:1]), pack_bar[:-1]], axis=0)
    after_seg = jnp.concatenate([pack_bar[:, 1:, :], jnp.zeros_like(pack_bar[:, :1])], axis=1)
    mass_rows = pack_bar - earlier + flow_bar - upstream
    momentum = friction * flow_bar - (pack_bar - after_seg)
    totals = share_scale * contract_sums(pack_bar, contract_map)
    return (mass_rows, momentum, totals)

def backward(mass_now, momentum_now, contract_now, friction, matching, contract_map, share_scale):
    returned = jnp.zeros_like(mass_now[:, 0, :]).at[:, matching].add(mass_now[:, 0, :])
    next_seg = jnp.concatenate([mass_now[:, 1:, :], returned[:, None, :]], axis=1)
    grad_flow = mass_now - next_seg + friction * momentum_now
    later_hour = jnp.concatenate([mass_now[1:], jnp.zeros_like(mass_now[:1])], axis=0)
    before_seg = jnp.concatenate([jnp.zeros_like(momentum_now[:, :1]), momentum_now[:, :-1]], axis=1)
    spread = contract_spread(contract_now, contract_map, SEGS)
    grad_pack = mass_now - later_hour - momentum_now + before_seg + share_scale * spread
    return (grad_flow, grad_pack)

def reference(segment_flow, linepack, mass_dual, momentum_dual, contract_dual, flow_cost, injection, contract_target, friction_table, friction_class, matching, contract_map):
    friction = jnp.take(friction_table, friction_class, axis=0)[None]
    share_scale = NC / PIPES
    target_now = contract_target.reshape(HOURS, SEGS, NC)
    contract_now = contract_dual.reshape(HOURS, SEGS, NC)
    weight = jnp.float32(1.0)
    for iteration in range(ITERS):
        primal_step = STEP_SCALE / weight
        dual_step = STEP_SCALE * weight
        grad_flow, grad_pack = backward(mass_dual, momentum_dual, contract_now, friction, matching, contract_map, share_scale)
        flow_next = jnp.clip(segment_flow - primal_step * (flow_cost - grad_flow), -FLOW_CAP, FLOW_CAP)
        pack_next = jnp.clip(linepack + primal_step * grad_pack, 0.0, PACK_CAP)
        mass_rows, momentum, totals = forward(2.0 * flow_next - segment_flow, 2.0 * pack_next - linepack, friction, matching, contract_map, share_scale)
        mass_next = mass_dual + dual_step * (injection - mass_rows)
        momentum_next = momentum_dual - dual_step * momentum
        contract_next = contract_now + dual_step * (target_now - totals)
        primal_sq = jnp.sum((flow_next - segment_flow) ** 2) + jnp.sum((pack_next - linepack) ** 2)
        dual_sq = jnp.sum((mass_next - mass_dual) ** 2) + jnp.sum((momentum_next - momentum_dual) ** 2) + jnp.sum((contract_next - contract_now) ** 2)
        weight = jnp.sqrt(weight * jnp.sqrt((dual_sq + NORM_EPS) / (primal_sq + NORM_EPS)))
        segment_flow, linepack = (flow_next, pack_next)
        mass_dual, momentum_dual, contract_now = (mass_next, momentum_next, contract_next)
    return (segment_flow, linepack, mass_dual, momentum_dual, contract_now.reshape(HOURS, SEG_PARTS, SEG_BLOCK, NC), weight.reshape(1))
```

```python
import functools

import jax
import jax.numpy as jnp
from jax import lax
from jax.experimental import pallas as pl
from jax.experimental.pallas import tpu as pltpu
from jax.sharding import PartitionSpec as P

ITERS = 2

FLOW_CAP = 1.5
PACK_CAP = 2.5
STEP_SCALE = 0.25
NORM_EPS = 1e-06

LANES = 128
SUBLANES = 8
VMEM_LIMIT = 8 * 1024 * 1024
NT = (((1,), (1,)), ((), ()))
NN = (((1,), (0,)), ((), ()))


def rounded_up(count):
    return -(-count // SUBLANES) * SUBLANES


def local_call(body, outs, args):
    specs = [
        pl.BlockSpec(memory_space=pltpu.SMEM if space == "smem" else pltpu.VMEM)
        for space, _ in args
    ]
    results = pl.pallas_call(
        body,
        out_shape=[jax.ShapeDtypeStruct(shape, jnp.float32) for shape in outs],
        in_specs=specs,
        out_specs=[pl.BlockSpec(memory_space=pltpu.VMEM) for _ in outs],
        compiler_params=pltpu.CompilerParams(vmem_limit_bytes=VMEM_LIMIT),
    )(*[array for _, array in args])
    return list(results)


def vmem(*arrays):
    return [("vmem", array) for array in arrays]


def parts_of(values):
    high = values.astype(jnp.bfloat16).astype(jnp.float32)
    rest = values - high
    middle = rest.astype(jnp.bfloat16).astype(jnp.float32)
    return jnp.concatenate([high, middle, rest - middle], axis=0).astype(jnp.bfloat16)


def exact_product(values, onehot, dims):
    rows = values.shape[0]
    product = lax.dot_general(
        parts_of(values), onehot, dims, preferred_element_type=jnp.float32
    )
    return product[:rows] + product[rows : 2 * rows] + product[2 * rows :]


def as_onehot(mask):
    return jnp.where(mask, 1.0, 0.0).astype(jnp.bfloat16)


def contract_onehot(map_row, class_count):
    shape = (class_count, map_row.shape[1])
    return as_onehot(lax.broadcasted_iota(jnp.int32, shape, 0) == map_row)


def friction_of(classes, table_ref, levels):
    friction = jnp.zeros(classes.shape, jnp.float32)
    for level in range(levels):
        friction = jnp.where(classes == level, table_ref[level], friction)
    return friction


def folded(values):
    rows, width = values.shape
    total = values[:SUBLANES]
    for start in range(SUBLANES, rows, SUBLANES):
        total = total + values[start : start + SUBLANES]
    result = total[:, :LANES]
    for start in range(LANES, width, LANES):
        result = result + total[:, start : start + LANES]
    return result


def tree_sum(terms):
    while len(terms) > 1:
        terms = [a + b for a, b in zip(terms[0::2], terms[1::2])]
    return terms[0]


def swapped(message, axes, distance):
    count = lax.axis_size(axes)
    return lax.ppermute(message, axes, [(i, i ^ distance) for i in range(count)])


class Sizes:
    def __init__(self, hours, segs, pipes, chunk, classes, levels):
        self.hours, self.segs, self.pipes = hours, segs, pipes
        self.chunk, self.classes, self.levels = chunk, classes, levels
        self.blocks = lax.axis_size("pipe")
        self.hour_parts = lax.axis_size("hour")
        self.share = classes / (pipes * self.blocks)
        self.halves = pipes // LANES
        self.end_rows = 2 * hours
        self.end_packed = self.end_rows * self.halves
        self.sums = hours * segs
        self.paired = self.hour_parts == 2


def write_ends(sz, message, start, rows):
    for index, row in enumerate(rows):
        for half in range(sz.halves):
            at = start + half * sz.end_rows + index
            message[at : at + 1, :] = row[:, half * LANES : (half + 1) * LANES]


def read_ends(sz, message, start):
    pieces = [
        message[start + half * sz.end_rows : start + (half + 1) * sz.end_rows, :]
        for half in range(sz.halves)
    ]
    return jnp.concatenate(pieces, axis=1)


def end_rows(sz, first_seg, mass, flow, outflow):
    firsts = [mass[t, 0:1, :] for t in range(sz.hours)]
    lasts = [flow[t, sz.segs - 1 : sz.segs, :] for t in range(sz.hours)]
    return [
        jnp.where(first_seg, a, b) for a, b in zip(firsts + firsts, lasts + outflow)
    ]


def start_kernel(
    sz, table, flow, mass, momentum, cost, classes, duals, message, friction
):
    first_seg = lax.axis_index("seg") == 0
    friction[...] = friction_of(classes[...], table, sz.levels)
    last = sz.segs - 1
    outflow = [
        cost[t, last : last + 1, :]
        - mass[t, last : last + 1, :]
        - friction[last : last + 1, :] * momentum[t, last : last + 1, :]
        for t in range(sz.hours)
    ]
    duals_rows = sz.hours * sz.chunk
    for t in range(sz.hours):
        message[t * sz.chunk : (t + 1) * sz.chunk, :] = duals[t]
    write_ends(
        sz, message, rounded_up(duals_rows), end_rows(sz, first_seg, mass, flow, outflow)
    )


def spread_kernel(sz, first, *refs):
    refs = list(refs)
    take = lambda count: [refs.pop(0) for _ in range(count)]
    flow, pack, mass, momentum, cost, friction, contract_map, matching = take(8)
    messages = take(sz.blocks)
    if not first:
        old_duals, old_weight = take(2)
    seg_message = take(1)[0]
    hour_messages = take(1 if sz.paired else 2)
    corner_message, duals, spread = take(3)
    scalars = None if first else take(1)[0]
    if first:
        temp = None
    first_seg = lax.axis_index("seg") == 0
    first_hour = lax.axis_index("hour") == 0
    block = lax.axis_index("pipe")
    hours, segs, pipes = sz.hours, sz.segs, sz.pipes
    last = segs - 1

    if first:
        ends_at = rounded_up(hours * sz.chunk)
        for distance in range(sz.blocks):
            owner = lax.bitwise_xor(block, distance)
            for t in range(hours):
                rows = pl.ds(pl.multiple_of(owner * sz.chunk, sz.chunk), sz.chunk)
                duals[t, rows, :] = messages[distance][t * sz.chunk : (t + 1) * sz.chunk, :]
    else:
        ends_at = sz.sums
        dual_step = STEP_SCALE * old_weight[...]
        dual_sq = jnp.zeros((SUBLANES, LANES), jnp.float32)
        for t in range(hours):
            totals = tree_sum([ref[t * segs : (t + 1) * segs, :] for ref in messages])
            change = dual_step * totals
            duals[t] = old_duals[t] - change
            dual_sq = dual_sq + folded(change * change)
        squares_at = sz.sums + sz.end_packed
        primal_sq = tree_sum(
            [ref[squares_at : squares_at + SUBLANES, :] for ref in messages]
        )
        dual_sq = dual_sq + tree_sum(
            [
                ref[squares_at + SUBLANES : squares_at + 2 * SUBLANES, :]
                for ref in messages
            ]
        )
        scalars[:, :LANES] = primal_sq
        scalars[:, LANES : 2 * LANES] = dual_sq

    own_pipes = pl.ds(pl.multiple_of(block * pipes, LANES), pipes)
    for t in range(hours):
        onehot = contract_onehot(contract_map[t : t + 1, own_pipes], sz.classes)
        spread[t] = sz.share * exact_product(duals[t], onehot, NN)

    own_match = matching[0:1, own_pipes]
    ends = [read_ends(sz, ref, ends_at) for ref in messages]
    matched_at = 3 * hours

    def put_rows(start, rows):
        for index, row in enumerate(rows):
            seg_message[start + index : start + index + 1, :] = row

    seg_message[...] = jnp.zeros(seg_message.shape, jnp.float32)

    @pl.when(first_seg)
    def _():
        returned = jnp.zeros((hours, pipes), jnp.float32)
        found = jnp.zeros((sz.end_rows, pipes), jnp.float32)
        for distance in range(sz.blocks):
            owner = lax.bitwise_xor(block, distance)
            feeds = matching[0:1, pl.ds(pl.multiple_of(owner * pipes, LANES), pipes)]
            here = lax.broadcasted_iota(jnp.int32, (pipes, pipes), 0) + block * pipes
            found = found + exact_product(ends[distance], as_onehot(here == feeds), NT)
        returned = found[:hours]
        seg_message[0:hours, :] = returned
        put_rows(hours, [momentum[t, last : last + 1, :] for t in range(hours)])
        put_rows(2 * hours, [flow[t, last : last + 1, :] for t in range(hours)])
        put_rows(
            3 * hours,
            [
                cost[t, last : last + 1, :]
                - mass[t, last : last + 1, :]
                - friction[last : last + 1, :] * momentum[t, last : last + 1, :]
                for t in range(hours)
            ],
        )

    @pl.when(jnp.logical_not(first_seg))
    def _():
        found = jnp.zeros((sz.end_rows, pipes), jnp.float32)
        for distance in range(sz.blocks):
            owner = lax.bitwise_xor(block, distance)
            there = lax.broadcasted_iota(jnp.int32, (pipes, pipes), 0) + owner * pipes
            found = found + exact_product(ends[distance], as_onehot(there == own_match), NN)
        put_rows(0, [mass[t, 0:1, :] for t in range(hours)])
        put_rows(hours, [pack[t, 0:1, :] for t in range(hours)])
        put_rows(
            2 * hours,
            [
                mass[t, 0:1, :] - momentum[t, 0:1, :] + spread[t, 0:1, :]
                for t in range(hours)
            ],
        )
        seg_message[matched_at : matched_at + sz.end_rows, :] = found

    end = hours - 1
    row_index = lax.broadcasted_iota(jnp.int32, (segs, pipes), 0)
    before = jnp.where(row_index == 0, 0.0, pltpu.roll(momentum[end], 1, 0))
    gradient = mass[end] - momentum[end] + before + spread[end]
    if sz.paired:
        hour_message = hour_messages[0]
        hour_message[0:segs, :] = jnp.where(first_hour, pack[end], mass[0])
        hour_message[segs : 2 * segs, :] = gradient
    else:
        hour_messages[0][0:segs, :] = pack[end]
        hour_messages[0][segs : 2 * segs, :] = gradient
        hour_messages[1][...] = mass[0]
    corner_message[...] = jnp.zeros(corner_message.shape, jnp.float32)
    corner_message[0:1, :] = jnp.where(
        first_seg, momentum[end, last : last + 1, :], mass[0, 0:1, :]
    )
    if not first and sz.paired:
        for ref in (seg_message, hour_messages[0], corner_message):
            tail = ref.shape[0] - SUBLANES
            ref[tail:, :LANES] = primal_sq
            ref[tail:, LANES : 2 * LANES] = dual_sq


def new_weight(weight, total):
    primal = jnp.sum(total[:, :LANES], axis=(0, 1), keepdims=True)
    dual = jnp.sum(total[:, LANES : 2 * LANES], axis=(0, 1), keepdims=True)
    return jnp.sqrt(weight * jnp.sqrt((dual + NORM_EPS) / (primal + NORM_EPS)))


def tail_of(ref):
    return ref[ref.shape[0] - SUBLANES :, : 2 * LANES]


def step_kernel(sz, first, final, *refs):
    refs = list(refs)
    take = lambda count: [refs.pop(0) for _ in range(count)]
    flow, pack, mass, momentum, cost, injection, friction, spread = take(8)
    contract_map, target, seg_in = take(3)
    hours_in = take(1 if sz.paired else 2)
    corner_in = take(1)[0]
    if not first:
        old_weight, scalars = take(2)
    flow_out, pack_out, mass_out, momentum_out, message, weight_out = take(6)
    first_seg = lax.axis_index("seg") == 0
    hour_index = lax.axis_index("hour")
    has_earlier = hour_index > 0
    has_later = hour_index < sz.hour_parts - 1
    block = lax.axis_index("pipe")
    hours, segs, pipes = sz.hours, sz.segs, sz.pipes
    last = segs - 1
    end = hours - 1
    earlier_in, later_in = hours_in[0], hours_in[-1]

    if first:
        weight = jnp.ones((1, 1), jnp.float32)
    else:
        if sz.paired:
            total = tree_sum(
                [scalars[...], tail_of(seg_in), tail_of(hours_in[0]), tail_of(corner_in)]
            )
        else:
            total = scalars[...]
        weight = new_weight(old_weight[...], total)
    weight_out[...] = weight
    primal_step = STEP_SCALE / weight
    dual_step = STEP_SCALE * weight

    row_index = lax.broadcasted_iota(jnp.int32, (segs, pipes), 0)
    top, bottom = row_index == 0, row_index == last

    def from_above(values, row):
        return jnp.where(top, row, pltpu.roll(values, 1, 0))

    def from_below(values, row):
        return jnp.where(bottom, row, pltpu.roll(values, segs - 1, 0))

    def seg_row(slot, t):
        at = slot * hours + t
        return seg_in[at : at + 1, :]

    def new_flow(start, gap):
        return jnp.clip(start - primal_step * gap, -FLOW_CAP, FLOW_CAP)

    def new_pack(start, gradient):
        return jnp.clip(start + primal_step * gradient, 0.0, PACK_CAP)

    corner = corner_in[0:1, :]
    earlier_pack = earlier_in[0:segs, :]
    earlier_gradient = (
        earlier_in[segs : 2 * segs, :]
        + jnp.where(top, jnp.where(first_seg, 0.0, corner), 0.0)
        - mass[0]
    )
    earlier_bar = jnp.where(
        has_earlier, 2.0 * new_pack(earlier_pack, earlier_gradient) - earlier_pack, 0.0
    )
    later_mass = jnp.where(has_later, later_in[0:segs, :], 0.0)
    later_corner = jnp.where(has_later, corner, 0.0)
    resistance = friction[...]
    primal_sq = jnp.zeros((SUBLANES, LANES), jnp.float32)
    dual_sq = jnp.zeros((SUBLANES, LANES), jnp.float32)
    outflow = []
    for t in range(hours):
        mass_now, momentum_now = mass[t], momentum[t]
        flow_now, pack_now = flow[t], pack[t]
        below_mass = seg_row(0, t)
        next_mass = mass[t + 1] if t < end else later_mass
        gap = cost[t] - (
            mass_now - from_below(mass_now, below_mass) + resistance * momentum_now
        )
        flow_next = new_flow(flow_now, gap)
        above_momentum = jnp.where(first_seg, 0.0, seg_row(1, t))
        gradient = (
            mass_now
            - next_mass
            - momentum_now
            + from_above(momentum_now, above_momentum)
            + spread[t]
        )
        pack_next = new_pack(pack_now, gradient)
        flow_bar = 2.0 * flow_next - flow_now
        pack_bar = 2.0 * pack_next - pack_now

        edge_flow = jnp.where(first_seg, seg_row(3, t), seg_row(2, t))
        edge_gap = jnp.where(first_seg, seg_row(4, t), seg_row(3, t)) + mass_now[0:1, :]
        edge_flow_bar = 2.0 * new_flow(edge_flow, edge_gap) - edge_flow
        edge_pack = seg_row(1, t)
        edge_later = seg_row(0, t + 1) if t < end else later_corner
        edge_gradient = seg_row(2, t) + momentum_now[last : last + 1, :] - edge_later
        edge_pack_bar = jnp.where(
            first_seg, 2.0 * new_pack(edge_pack, edge_gradient) - edge_pack, 0.0
        )

        mass_rows = pack_bar - earlier_bar + flow_bar - from_above(flow_bar, edge_flow_bar)
        momentum_rows = resistance * flow_bar - (pack_bar - from_below(pack_bar, edge_pack_bar))
        mass_change = dual_step * (injection[t] - mass_rows)
        momentum_change = dual_step * momentum_rows
        mass_next = mass_now + mass_change
        momentum_next = momentum_now - momentum_change
        flow_out[t] = flow_next
        pack_out[t] = pack_next
        mass_out[t] = mass_next
        momentum_out[t] = momentum_next
        flow_change, pack_change = flow_next - flow_now, pack_next - pack_now
        primal_sq = primal_sq + folded(flow_change * flow_change + pack_change * pack_change)
        dual_sq = dual_sq + folded(
            mass_change * mass_change + momentum_change * momentum_change
        )
        own_pipes = pl.ds(pl.multiple_of(block * pipes, LANES), pipes)
        onehot = contract_onehot(contract_map[t : t + 1, own_pipes], sz.classes)
        message[t * segs : (t + 1) * segs, :] = sz.share * exact_product(pack_bar, onehot, NT)
        rows = pl.ds(pl.multiple_of(t * segs + block * sz.chunk, sz.chunk), sz.chunk)
        message[rows, :] = message[rows, :] - target[t]
        outflow.append(
            cost[t, last : last + 1, :]
            - mass_next[last : last + 1, :]
            - resistance[last : last + 1, :] * momentum_next[last : last + 1, :]
        )
        earlier_bar = pack_bar

    squares_at = sz.sums
    if not final:
        squares_at += sz.end_packed
        write_ends(sz, message, sz.sums, end_rows(sz, first_seg, mass_out, flow_out, outflow))
    message[squares_at : squares_at + SUBLANES, :] = primal_sq
    message[squares_at + SUBLANES : squares_at + 2 * SUBLANES, :] = dual_sq


def close_kernel(sz, *refs):
    refs = list(refs)
    messages = [refs.pop(0) for _ in range(sz.blocks)]
    old_duals, weight, duals, scalars = refs
    block = lax.axis_index("pipe")
    segs = sz.segs
    dual_step = STEP_SCALE * weight[...]
    dual_sq = jnp.zeros((SUBLANES, LANES), jnp.float32)
    for t in range(sz.hours):
        totals = tree_sum([ref[t * segs : (t + 1) * segs, :] for ref in messages])
        change = dual_step * totals
        dual_sq = dual_sq + folded(change * change)
        start = block * sz.chunk
        own = pl.ds(pl.multiple_of(start, sz.chunk), sz.chunk)
        rows = pl.ds(pl.multiple_of(t * segs + start, sz.chunk), sz.chunk)
        own_totals = tree_sum([ref[rows, :] for ref in messages])
        duals[t] = old_duals[t, own, :] - dual_step * own_totals
    at = sz.sums
    scalars[:, :LANES] = tree_sum([ref[at : at + SUBLANES, :] for ref in messages])
    scalars[:, LANES : 2 * LANES] = dual_sq + tree_sum(
        [ref[at + SUBLANES : at + 2 * SUBLANES, :] for ref in messages]
    )


def weight_kernel(weight, *refs):
    *scalars, result = refs
    result[...] = new_weight(weight[...], tree_sum([ref[...] for ref in scalars]))


def gathered(message):
    count = lax.axis_size("pipe")
    return [message] + [swapped(message, "pipe", k) for k in range(1, count)]


def exchanged(sz, seg_message, hour_messages, corner_message):
    seg_in = swapped(seg_message, "seg", 1)
    if sz.paired:
        hours_in = [swapped(hour_messages[0], "hour", 1)]
        corner_in = swapped(corner_message, ("hour", "seg"), 3)
    else:
        steps = range(sz.hour_parts - 1)
        hours_in = [
            lax.ppermute(hour_messages[0], "hour", [(i, i + 1) for i in steps]),
            lax.ppermute(hour_messages[1], "hour", [(i + 1, i) for i in steps]),
        ]
        corner_in = lax.ppermute(
            corner_message,
            ("hour", "seg"),
            [(2 * i, 2 * i + 3) for i in steps] + [(2 * i + 3, 2 * i) for i in steps],
        )
    return seg_in, hours_in, corner_in


def on_device(
    segment_flow,
    linepack,
    mass_dual,
    momentum_dual,
    contract_dual,
    flow_cost,
    injection,
    contract_target,
    friction_table,
    friction_class,
    matching,
    contract_map,
):
    hours, segs, pipes = segment_flow.shape
    chunk, classes = contract_dual.shape[2:]
    sz = Sizes(hours, segs, pipes, chunk, classes, friction_table.shape[0])
    duals_now = contract_dual.reshape(hours, chunk, classes)
    target_now = contract_target.reshape(hours, chunk, classes)
    matching = matching.reshape(1, matching.shape[0])
    cells = (hours, segs, pipes)
    seg_rows = rounded_up(5 * hours) + SUBLANES
    hour_shapes = [(2 * segs + SUBLANES, pipes)]
    if not sz.paired:
        hour_shapes = [(2 * segs, pipes), (segs, pipes)]
    square_shape = (SUBLANES, 2 * LANES)

    state = [segment_flow, linepack, mass_dual, momentum_dual]
    message, friction = local_call(
        functools.partial(start_kernel, sz),
        [(rounded_up(hours * chunk) + sz.end_packed, classes), (segs, pipes)],
        [("smem", friction_table)]
        + vmem(segment_flow, mass_dual, momentum_dual, flow_cost, friction_class, duals_now),
    )
    duals, weight = None, None
    for iteration in range(ITERS):
        first, final = iteration == 0, iteration == ITERS - 1
        args = vmem(*state, flow_cost, friction, contract_map, matching, *gathered(message))
        outs = [(seg_rows, pipes), *hour_shapes, (2 * SUBLANES, pipes)]
        outs += [(hours, segs, classes), cells]
        if not first:
            args += vmem(duals, weight)
            outs += [square_shape]
        results = local_call(functools.partial(spread_kernel, sz, first), outs, args)
        scalars = None if first else results.pop()
        *messages, duals, spread = results
        seg_in, hours_in, corner_in = exchanged(
            sz, messages[0], messages[1:-1], messages[-1]
        )
        if not first and not sz.paired:
            scalars = lax.psum(scalars, ("hour", "seg"))
        args = vmem(*state, flow_cost, injection, friction, spread, contract_map, target_now)
        args += vmem(seg_in, *hours_in, corner_in)
        if not first:
            args += vmem(weight, scalars)
        rows = sz.sums + 2 * SUBLANES + (0 if final else sz.end_packed)
        *state, message, weight = local_call(
            functools.partial(step_kernel, sz, first, final),
            [cells] * 4 + [(rows, classes), (1, 1)],
            args,
        )
    contract_out, scalars = local_call(
        functools.partial(close_kernel, sz),
        [(hours, chunk, classes), square_shape],
        vmem(*gathered(message), duals, weight),
    )
    if sz.paired:
        squares = [scalars] + [swapped(scalars, ("hour", "seg"), k) for k in (1, 2, 3)]
    else:
        squares = [lax.psum(scalars, ("hour", "seg"))]
    (weight,) = local_call(weight_kernel, [(1, 1)], vmem(weight, *squares))
    return (
        *state,
        contract_out.reshape(contract_dual.shape),
        weight.reshape(1),
    )


def solution(mesh):
    cells = P(("groups", "hour"), "seg", "pipe")
    contracts = P(("groups", "hour"), "seg", "pipe", None)
    return jax.shard_map(
        on_device,
        mesh=mesh,
        in_specs=(
            cells,
            cells,
            cells,
            cells,
            contracts,
            cells,
            cells,
            contracts,
            P(),
            P("seg", ("groups", "pipe")),
            P("groups"),
            P(("groups", "hour"), None),
        ),
        out_specs=(cells, cells, cells, cells, contracts, P("groups")),
        check_vma=False,
    )
```

```python
import functools

import jax
import jax.numpy as jnp
from jax import lax
from jax.experimental import pallas as pl
from jax.experimental.pallas import tpu as pltpu
from jax.sharding import PartitionSpec as P

ITERS = 2

FLOW_CAP = 1.5
PACK_CAP = 2.5
STEP_SCALE = 0.25
NORM_EPS = 1e-06

LANES = 128
SUBLANES = 8
VMEM_LIMIT = 8 * 1024 * 1024
SHIFTED = True
NT = (((1,), (1,)), ((), ()))
NN = (((1,), (0,)), ((), ()))


def rounded_up(count):
    return -(-count // SUBLANES) * SUBLANES


def local_call(body, outs, args, kept=False, scratch=()):
    spaces = {"smem": pltpu.SMEM, "vmem": pltpu.VMEM, "hbm": pltpu.HBM}
    shape_of = pltpu.VMEM if kept else jax.ShapeDtypeStruct
    results = pl.pallas_call(
        body,
        out_shape=[shape_of(shape, jnp.float32) for shape in outs],
        in_specs=[pl.BlockSpec(memory_space=spaces[space]) for space, _ in args],
        out_specs=[pl.BlockSpec(memory_space=pltpu.VMEM) for _ in outs],
        scratch_shapes=scratch,
        compiler_params=pltpu.CompilerParams(vmem_limit_bytes=VMEM_LIMIT),
    )(*[array for _, array in args])
    return list(results)


def vmem(*arrays):
    return [("vmem", array) for array in arrays]


def taker(refs):
    refs = list(refs)

    def take(count):
        return [refs.pop(0) for _ in range(count)]

    return take


def parts_of(values):
    high = values.astype(jnp.bfloat16).astype(jnp.float32)
    rest = values - high
    middle = rest.astype(jnp.bfloat16).astype(jnp.float32)
    return jnp.concatenate([high, middle, rest - middle], axis=0).astype(jnp.bfloat16)


def exact_product(values, onehot, dims):
    rows = values.shape[0]
    product = lax.dot_general(
        parts_of(values), onehot, dims, preferred_element_type=jnp.float32
    )
    return product[:rows] + product[rows : 2 * rows] + product[2 * rows :]


def as_onehot(mask):
    return jnp.where(mask, 1.0, 0.0).astype(jnp.bfloat16)


def contract_onehot(map_row, class_count):
    shape = (class_count, map_row.shape[1])
    return as_onehot(lax.broadcasted_iota(jnp.int32, shape, 0) == map_row)


def friction_of(classes, table_ref, levels):
    friction = jnp.zeros(classes.shape, jnp.float32)
    for level in range(levels):
        friction = jnp.where(classes == level, table_ref[level], friction)
    return friction


def folded(values):
    rows, width = values.shape
    total = values[:SUBLANES]
    for start in range(SUBLANES, rows, SUBLANES):
        total = total + values[start : start + SUBLANES]
    result = total[:, :LANES]
    for start in range(LANES, width, LANES):
        result = result + total[:, start : start + LANES]
    return result


def tree_sum(terms):
    while len(terms) > 1:
        terms = [a + b for a, b in zip(terms[0::2], terms[1::2])]
    return terms[0]


def swapped(message, axes, distance):
    count = lax.axis_size(axes)
    return lax.ppermute(message, axes, [(i, i ^ distance) for i in range(count)])


class Sizes:
    def __init__(self, hours, segs, pipes, chunk, classes, levels):
        self.hours, self.segs, self.pipes = hours, segs, pipes
        self.chunk, self.classes, self.levels = chunk, classes, levels
        self.blocks = lax.axis_size("pipe")
        self.hour_parts = lax.axis_size("hour")
        self.share = classes / (pipes * self.blocks)
        self.halves = pipes // LANES
        self.paired = self.hour_parts == 2
        self.shifted = SHIFTED and self.blocks == 4
        self.end_rows = 2 * hours
        self.end_packed = self.end_rows * self.halves
        self.sums = hours * segs
        self.halo_hour = rounded_up(hours * chunk)
        self.halo_seg = self.halo_hour + rounded_up(chunk)
        self.first_ends = self.halo_seg + rounded_up(hours)
        self.matched = 7 * hours
        self.seg_tail = rounded_up(9 * hours)

    def owner(self, block, index):
        if self.shifted:
            return lax.rem(block + (self.blocks - index), self.blocks)
        return lax.bitwise_xor(block, index)

    def added(self, block, terms):
        if self.shifted:
            even = lax.rem(block, 2) == 0
            one, two, three = terms[1:]
            terms = [terms[0], jnp.where(even, three, one), two, jnp.where(even, one, three)]
        return tree_sum(terms)

    def own_pipes(self, block):
        return pl.ds(pl.multiple_of(block * self.pipes, LANES), self.pipes)


def places():
    return lax.axis_index("pipe"), lax.axis_index("hour"), lax.axis_index("seg") == 0


def write_ends(sz, message, start, rows):
    for index, row in enumerate(rows):
        for half in range(sz.halves):
            at = start + half * sz.end_rows + index
            message[at : at + 1, :] = row[:, half * LANES : (half + 1) * LANES]


def read_ends(sz, message, start):
    pieces = [
        message[start + half * sz.end_rows : start + (half + 1) * sz.end_rows, :]
        for half in range(sz.halves)
    ]
    return jnp.concatenate(pieces, axis=1)


def write_edges(sz, message, first_rows, last_rows, resistance):
    for t in range(sz.hours):
        mass, pack, momentum = [ref(t) for ref in first_rows]
        last_mass, flow, last_momentum, cost = [ref(t) for ref in last_rows]
        gap = cost - last_mass - resistance * last_momentum
        rows = [mass, pack, mass - momentum, last_momentum, flow, gap]
        for slot, row in enumerate(rows):
            at = slot * sz.hours + t
            message[at : at + 1, :] = row


def write_layers(sz, outs, first_hour, pack, mass, momentum, first_mass):
    segs = sz.segs
    top = lax.broadcasted_iota(jnp.int32, (segs, sz.pipes), 0) == 0
    gradient = mass - momentum + jnp.where(top, 0.0, pltpu.roll(momentum, 1, 0))
    if sz.paired:
        outs[0][0:segs, :] = jnp.where(first_hour, pack, first_mass)
    else:
        outs[0][0:segs, :] = pack
        outs[1][...] = first_mass
    outs[0][segs : 2 * segs, :] = gradient
    outs[0][2 * segs : 2 * segs + SUBLANES, :] = jnp.zeros((SUBLANES, sz.pipes), jnp.float32)
    outs[0][2 * segs : 2 * segs + 1, :] = momentum[segs - 1 : segs, :]


def matched_rows(sz, block, inlet_side, ends, matching, found):
    shape = (sz.pipes, sz.pipes)
    row = lax.broadcasted_iota(jnp.int32, shape, 0)
    total = jnp.zeros((sz.end_rows, sz.pipes), jnp.float32)

    @pl.when(inlet_side)
    def _():
        own = matching[0:1, sz.own_pipes(block)]
        result = total
        for index, values in enumerate(ends):
            there = row + sz.owner(block, index) * sz.pipes
            result = result + exact_product(values, as_onehot(there == own), NN)
        found[...] = result

    @pl.when(jnp.logical_not(inlet_side))
    def _():
        here = row + block * sz.pipes
        result = total
        for index, values in enumerate(ends):
            feeds = matching[0:1, sz.own_pipes(sz.owner(block, index))]
            result = result + exact_product(values, as_onehot(here == feeds), NT)
        found[...] = result


def start_kernel(sz, table, *refs):
    take = taker(refs)
    flow, pack, mass, momentum, cost, classes, duals, contract_map = take(8)
    seg_message, *hour_messages = take(1 + (1 if sz.paired else 2))
    (flow_last, cost_last, mass_last, momentum_last) = take(4)
    (pack_first, mass_first, momentum_first, classes_last) = take(4)
    (pack_layer, mass_layer, momentum_layer, mass_start) = take(4)
    duals_own, map_own, arrived = take(3)
    block, hour, first_seg = places()
    hours, segs = sz.hours, sz.segs
    low, high = pl.ds(0, SUBLANES), pl.ds(segs - SUBLANES, SUBLANES)
    copies = [
        (flow.at[:, high], flow_last),
        (cost.at[:, high], cost_last),
        (mass.at[:, high], mass_last),
        (momentum.at[:, high], momentum_last),
        (pack.at[:, low], pack_first),
        (mass.at[:, low], mass_first),
        (momentum.at[:, low], momentum_first),
        (classes.at[high], classes_last),
        (pack.at[hours - 1], pack_layer),
        (mass.at[hours - 1], mass_layer),
        (momentum.at[hours - 1], momentum_layer),
        (mass.at[0], mass_start),
        (duals, duals_own),
        (contract_map.at[:, sz.own_pipes(block)], map_own),
    ]
    copies = [
        pltpu.make_async_copy(source, target, arrived.at[index])
        for index, (source, target) in enumerate(copies)
    ]
    for copy in copies:
        copy.start()
    seg_message[...] = jnp.zeros(seg_message.shape, jnp.float32)
    for copy in copies:
        copy.wait()
    end = SUBLANES - 1
    resistance = friction_of(classes_last[...], table, sz.levels)[end:]
    write_edges(
        sz,
        seg_message,
        [lambda t, ref=ref: ref[t, 0:1, :] for ref in (mass_first, pack_first, momentum_first)],
        [
            lambda t, ref=ref: ref[t, end : end + 1, :]
            for ref in (mass_last, flow_last, momentum_last, cost_last)
        ],
        resistance,
    )
    for t in range(hours):
        at = 6 * hours + t
        seg_message[at : at + 1, : sz.classes] = duals_own[t, 0:1, :]
    write_layers(
        sz,
        hour_messages,
        hour == 0,
        pack_layer[...],
        mass_layer[...],
        momentum_layer[...],
        mass_start[...],
    )
    up = hour_messages[0]
    up[2 * segs + 1 : 2 * segs + 2, :] = map_own[hours - 1 : hours, :].astype(jnp.float32)
    halo = 2 * segs + SUBLANES
    up[halo:, :] = jnp.zeros((up.shape[0] - halo, sz.pipes), jnp.float32)
    up[halo : halo + sz.chunk, : sz.classes] = duals_own[hours - 1]


def start_scratch(sz):
    ends = (sz.hours, SUBLANES, sz.pipes)
    layer = (sz.segs, sz.pipes)
    return (
        [pltpu.VMEM(ends, jnp.float32)] * 7
        + [pltpu.VMEM((SUBLANES, sz.pipes), jnp.int32)]
        + [pltpu.VMEM(layer, jnp.float32)] * 4
        + [
            pltpu.VMEM((sz.hours, sz.chunk, sz.classes), jnp.float32),
            pltpu.VMEM((sz.hours, sz.pipes), jnp.int32),
            pltpu.SemaphoreType.DMA((14,)),
        ]
    )


def relay_kernel(sz, *refs):
    take = taker(refs)
    duals, seg_in, *hours_in = take(2 + (1 if sz.paired else 2))
    message, corner = take(2)
    earlier_in, later_in = hours_in[0], hours_in[-1]
    block, hour, first_seg = places()
    hours, segs = sz.hours, sz.segs
    message[...] = jnp.zeros(message.shape, jnp.float32)
    for t in range(hours):
        message[t * sz.chunk : (t + 1) * sz.chunk, :] = duals[t]
    halo = 2 * segs + SUBLANES
    message[sz.halo_hour : sz.halo_hour + sz.chunk, :] = earlier_in[
        halo : halo + sz.chunk, : sz.classes
    ]
    message[sz.halo_seg : sz.halo_seg + hours, :] = seg_in[
        6 * hours : 7 * hours, : sz.classes
    ]
    rows = []
    for slot, mass_slot in ((4, 0), (5, 0)):
        for t in range(hours):
            outlet, inlet = slot * hours + t, mass_slot * hours + t
            rows.append(
                jnp.where(first_seg, seg_in[outlet : outlet + 1, :], seg_in[inlet : inlet + 1, :])
            )
    write_ends(sz, message, sz.first_ends, rows)
    corner[...] = jnp.zeros(corner.shape, jnp.float32)
    corner[0:1, :] = jnp.where(
        first_seg, earlier_in[2 * segs : 2 * segs + 1, :], later_in[0:1, :]
    )


def spread_kernel(sz, *refs):
    take = taker(refs)
    flow, pack, mass, momentum, cost, friction, contract_map, matching = take(8)
    messages = take(sz.blocks)
    hours_in = take(1 if sz.paired else 2)
    old_duals, old_weight = take(2)
    seg_message, hour_message, duals, spread, scalars, found = take(6)
    earlier_in, later_in = hours_in[0], hours_in[-1]
    block, hour, first_seg = places()
    hours, segs, pipes = sz.hours, sz.segs, sz.pipes
    last = segs - 1

    ends = [read_ends(sz, ref, sz.sums) for ref in messages]
    matched_rows(sz, block, jnp.logical_not(first_seg), ends, matching, found)

    dual_step = STEP_SCALE * old_weight[...]
    dual_sq = jnp.zeros((SUBLANES, LANES), jnp.float32)
    for t in range(hours):
        totals = sz.added(block, [ref[t * segs : (t + 1) * segs, :] for ref in messages])
        change = dual_step * totals
        duals[t] = old_duals[t] - change
        dual_sq = dual_sq + folded(change * change)
        onehot = contract_onehot(contract_map[t : t + 1, sz.own_pipes(block)], sz.classes)
        spread[t] = sz.share * exact_product(duals[t], onehot, NN)
    at = sz.sums + sz.end_packed
    write_squares(sz, block, [ref[at : at + SUBLANES, :] for ref in messages], dual_sq, scalars)

    seg_message[...] = jnp.zeros(seg_message.shape, jnp.float32)
    write_edges(
        sz,
        seg_message,
        [lambda t, ref=ref: ref[t, 0:1, :] for ref in (mass, pack, momentum)],
        [lambda t, ref=ref: ref[t, last:segs, :] for ref in (mass, flow, momentum, cost)],
        friction[last:segs, :],
    )
    for t in range(hours):
        at = 6 * hours + t
        seg_message[at : at + 1, :] = spread[t, 0:1, :]
    seg_message[sz.matched : sz.matched + sz.end_rows, :] = found[...]
    seg_message[sz.seg_tail : sz.seg_tail + 1, : 2 * LANES] = scalars[0:1, :]
    seg_message[sz.seg_tail + 1 : sz.seg_tail + 2, :] = jnp.where(
        first_seg, earlier_in[2 * segs : 2 * segs + 1, :], later_in[0:1, :]
    )
    hour_message[0:segs, :] = spread[hours - 1]
    if sz.paired:
        hour_message[segs:, :] = jnp.zeros((SUBLANES, pipes), jnp.float32)
        hour_message[segs : segs + 1, : 2 * LANES] = scalars[0:1, :]


def write_squares(sz, block, squares, dual_sq, scalars):
    total = sz.added(block, squares)
    scalars[...] = jnp.zeros(scalars.shape, jnp.float32)
    scalars[0:1, :LANES] = total[0:1]
    scalars[0:1, LANES:] = total[1:2] + jnp.sum(dual_sq, axis=0, keepdims=True)


def new_weight(weight, total):
    primal = jnp.sum(total[:, :LANES], axis=1, keepdims=True)
    dual = jnp.sum(total[:, LANES : 2 * LANES], axis=1, keepdims=True)
    return jnp.sqrt(weight * jnp.sqrt((dual + NORM_EPS) / (primal + NORM_EPS)))


def step(sz, block, hour, first_seg, weight, state, data, halo, spread_of, outs, message):
    flow, pack, mass, momentum = state
    cost, injection, resistance, contract_map, target = data
    flow_out, pack_out, mass_out, momentum_out = outs
    hours, segs, pipes = sz.hours, sz.segs, sz.pipes
    last, end = segs - 1, hours - 1
    has_earlier = hour > 0
    has_later = hour < sz.hour_parts - 1
    primal_step = STEP_SCALE / weight
    dual_step = STEP_SCALE * weight

    row_index = lax.broadcasted_iota(jnp.int32, (segs, pipes), 0)
    top, bottom = row_index == 0, row_index == last

    def from_above(values, row):
        return jnp.where(top, row, pltpu.roll(values, 1, 0))

    def from_below(values, row):
        return jnp.where(bottom, row, pltpu.roll(values, segs - 1, 0))

    def seg_row(slot, t):
        at = slot * hours + t
        return halo["seg"][at : at + 1, :]

    def matched_row(slot, t):
        at = halo["matched_at"] + slot * hours + t
        return halo["matched"][at : at + 1, :]

    def new_flow(start, gap):
        return jnp.clip(start - primal_step * gap, -FLOW_CAP, FLOW_CAP)

    def new_pack(start, gradient):
        return jnp.clip(start + primal_step * gradient, 0.0, PACK_CAP)

    corner = halo["corner"]
    earlier_pack = halo["earlier"][0:segs, :]
    earlier_gradient = (
        halo["earlier"][segs : 2 * segs, :]
        + halo["earlier_spread"]
        + jnp.where(top, jnp.where(first_seg, 0.0, corner), 0.0)
        - mass[0]
    )
    earlier_bar = jnp.where(
        has_earlier, 2.0 * new_pack(earlier_pack, earlier_gradient) - earlier_pack, 0.0
    )
    later_mass = jnp.where(has_later, halo["later"][0:segs, :], 0.0)
    later_corner = jnp.where(has_later, corner, 0.0)
    primal_sq = jnp.zeros((SUBLANES, LANES), jnp.float32)
    dual_sq = jnp.zeros((SUBLANES, LANES), jnp.float32)
    for t in range(hours):
        mass_now, momentum_now = mass[t], momentum[t]
        flow_now, pack_now = flow[t], pack[t]
        spread, edge_spread, onehot = spread_of(t)
        below_mass = jnp.where(first_seg, seg_row(0, t), matched_row(0, t))
        next_mass = mass[t + 1] if t < end else later_mass
        gap = cost[t] - (
            mass_now - from_below(mass_now, below_mass) + resistance * momentum_now
        )
        flow_next = new_flow(flow_now, gap)
        above_momentum = jnp.where(first_seg, 0.0, seg_row(3, t))
        gradient = (
            mass_now
            - next_mass
            - momentum_now
            + from_above(momentum_now, above_momentum)
            + spread
        )
        pack_next = new_pack(pack_now, gradient)
        flow_bar = 2.0 * flow_next - flow_now
        pack_bar = 2.0 * pack_next - pack_now

        edge_flow = jnp.where(first_seg, matched_row(0, t), seg_row(4, t))
        edge_gap = jnp.where(first_seg, matched_row(1, t), seg_row(5, t)) + mass_now[0:1, :]
        edge_flow_bar = 2.0 * new_flow(edge_flow, edge_gap) - edge_flow
        edge_pack = seg_row(1, t)
        edge_later = seg_row(0, t + 1) if t < end else later_corner
        edge_gradient = (
            seg_row(2, t) + edge_spread + momentum_now[last : last + 1, :] - edge_later
        )
        edge_pack_bar = jnp.where(
            first_seg, 2.0 * new_pack(edge_pack, edge_gradient) - edge_pack, 0.0
        )

        mass_rows = pack_bar - earlier_bar + flow_bar - from_above(flow_bar, edge_flow_bar)
        momentum_rows = resistance * flow_bar - (pack_bar - from_below(pack_bar, edge_pack_bar))
        mass_change = dual_step * (injection[t] - mass_rows)
        momentum_change = dual_step * momentum_rows
        flow_out[t] = flow_next
        pack_out[t] = pack_next
        mass_out[t] = mass_now + mass_change
        momentum_out[t] = momentum_now - momentum_change
        flow_change, pack_change = flow_next - flow_now, pack_next - pack_now
        primal_sq = primal_sq + folded(flow_change * flow_change + pack_change * pack_change)
        dual_sq = dual_sq + folded(
            mass_change * mass_change + momentum_change * momentum_change
        )
        message[t * segs : (t + 1) * segs, :] = sz.share * exact_product(pack_bar, onehot, NT)
        rows = pl.ds(pl.multiple_of(t * segs + block * sz.chunk, sz.chunk), sz.chunk)
        message[rows, :] = message[rows, :] - target[t]
        earlier_bar = pack_bar

    at = message.shape[0] - SUBLANES
    message[at:, :] = jnp.zeros((SUBLANES, LANES), jnp.float32)
    message[at : at + 1, :] = jnp.sum(primal_sq, axis=0, keepdims=True)
    message[at + 1 : at + 2, :] = jnp.sum(dual_sq, axis=0, keepdims=True)


def write_next(sz, hour, first_seg, outs, cost, resistance, message, hour_messages):
    flow, pack, mass, momentum = outs
    last = sz.segs - 1
    firsts = [mass[t, 0:1, :] for t in range(sz.hours)]
    lasts = [flow[t, last : last + 1, :] for t in range(sz.hours)]
    gaps = [
        cost[t, last : last + 1, :]
        - mass[t, last : last + 1, :]
        - resistance[last : last + 1, :] * momentum[t, last : last + 1, :]
        for t in range(sz.hours)
    ]
    rows = [jnp.where(first_seg, a, b) for a, b in zip(firsts + firsts, lasts + gaps)]
    write_ends(sz, message, sz.sums, rows)
    end = sz.hours - 1
    write_layers(sz, hour_messages, hour == 0, pack[end], mass[end], momentum[end], mass[0])


def first_kernel(sz, final, table, *refs):
    take = taker(refs)
    state, data = take(4), take(2)
    classes, contract_map, target, matching = take(4)
    messages, seg_in = take(sz.blocks), take(1)[0]
    hours_in, corner_in = take(1 if sz.paired else 2), take(1)[0]
    outs, message, duals, friction = take(4), *take(3)
    hour_messages = [] if final else take(1 if sz.paired else 2)
    halo_duals, found = take(2)
    block, hour, first_seg = places()
    hours, segs, chunk = sz.hours, sz.segs, sz.chunk
    friction[...] = friction_of(classes[...], table, sz.levels)
    edge_duals = jnp.zeros((hours, sz.classes), jnp.float32)
    for index, ref in enumerate(messages):
        owner = sz.owner(block, index)
        rows = pl.ds(pl.multiple_of(owner * chunk, chunk), chunk)
        for t in range(hours):
            duals[t, rows, :] = ref[t * chunk : (t + 1) * chunk, :]
        halo_duals[rows, :] = ref[sz.halo_hour : sz.halo_hour + chunk, :]
        edge_duals = jnp.where(
            owner == 0, ref[sz.halo_seg : sz.halo_seg + hours, :], edge_duals
        )
    ends = [read_ends(sz, ref, sz.first_ends) for ref in messages]
    matched_rows(sz, block, first_seg, ends, matching, found)
    map_row = hours_in[0][2 * segs + 1 : 2 * segs + 2, :].astype(jnp.int32)
    earlier_spread = sz.share * exact_product(
        halo_duals[...], contract_onehot(map_row, sz.classes), NN
    )

    def spread_of(t):
        onehot = contract_onehot(contract_map[t : t + 1, sz.own_pipes(block)], sz.classes)
        edge = jnp.broadcast_to(edge_duals[t : t + 1, :], (2 * SUBLANES, sz.classes))
        values = jnp.concatenate([duals[t], edge], axis=0)
        product = sz.share * exact_product(values, onehot, NN)
        return product[:segs], product[segs : segs + 1], onehot

    halo = {
        "seg": seg_in,
        "matched": found,
        "matched_at": 0,
        "corner": corner_in[0:1, :],
        "earlier": hours_in[0],
        "earlier_spread": earlier_spread,
        "later": hours_in[-1],
    }
    resistance = friction[...]
    data = [*data, resistance, contract_map, target]
    one = jnp.ones((1, 1), jnp.float32)
    step(sz, block, hour, first_seg, one, state, data, halo, spread_of, outs, message)
    if not final:
        write_next(sz, hour, first_seg, outs, data[0], resistance, message, hour_messages)


def later_kernel(sz, final, *refs):
    take = taker(refs)
    state, data = take(4), take(2)
    friction, contract_map, target, spread = take(4)
    seg_in, hours_in, spread_in = take(1)[0], take(1 if sz.paired else 2), take(1)[0]
    old_weight, scalars = take(2)
    corner_scalars = take(1) if sz.paired else []
    outs, message, weight_out = take(4), *take(2)
    hour_messages = [] if final else take(1 if sz.paired else 2)
    block, hour, first_seg = places()
    hours, segs = sz.hours, sz.segs
    total = scalars[0:1, :]
    if sz.paired:
        total = tree_sum(
            [
                total,
                seg_in[sz.seg_tail : sz.seg_tail + 1, : 2 * LANES],
                spread_in[segs : segs + 1, : 2 * LANES],
                corner_scalars[0][0:1, :],
            ]
        )
    weight = new_weight(old_weight[...], total)
    weight_out[...] = weight

    def spread_of(t):
        onehot = contract_onehot(contract_map[t : t + 1, sz.own_pipes(block)], sz.classes)
        at = 6 * hours + t
        return spread[t], seg_in[at : at + 1, :], onehot

    halo = {
        "seg": seg_in,
        "matched": seg_in,
        "matched_at": sz.matched,
        "corner": seg_in[sz.seg_tail + 1 : sz.seg_tail + 2, :],
        "earlier": hours_in[0],
        "earlier_spread": spread_in[0:segs, :],
        "later": hours_in[-1],
    }
    resistance = friction[...]
    data = [*data, resistance, contract_map, target]
    step(sz, block, hour, first_seg, weight, state, data, halo, spread_of, outs, message)
    if not final:
        write_next(sz, hour, first_seg, outs, data[0], resistance, message, hour_messages)


def close_kernel(sz, *refs):
    take = taker(refs)
    messages = take(sz.blocks)
    old_duals, weight, duals, scalars = take(4)
    block, hour, first_seg = places()
    segs = sz.segs
    dual_step = STEP_SCALE * weight[...]
    dual_sq = jnp.zeros((SUBLANES, LANES), jnp.float32)
    start = block * sz.chunk
    for t in range(sz.hours):
        totals = sz.added(block, [ref[t * segs : (t + 1) * segs, :] for ref in messages])
        change = dual_step * totals
        dual_sq = dual_sq + folded(change * change)
        own = pl.ds(pl.multiple_of(start, sz.chunk), sz.chunk)
        rows = pl.ds(pl.multiple_of(t * segs + start, sz.chunk), sz.chunk)
        own_totals = sz.added(block, [ref[rows, :] for ref in messages])
        duals[t] = old_duals[t, own, :] - dual_step * own_totals
    squares = [ref[sz.sums : sz.sums + SUBLANES, :] for ref in messages]
    write_squares(sz, block, squares, dual_sq, scalars)


def weight_kernel(weight, *refs):
    *scalars, result = refs
    result[...] = new_weight(weight[...], tree_sum([ref[0:1, :] for ref in scalars]))


def gathered(sz, message):
    if sz.shifted:
        ring = [
            [(i, (i + k) % sz.blocks) for i in range(sz.blocks)] for k in range(1, sz.blocks)
        ]
        return [message] + [lax.ppermute(message, "pipe", pairs) for pairs in ring]
    return [message] + [swapped(message, "pipe", k) for k in range(1, sz.blocks)]


def layers_exchanged(sz, hour_messages):
    if sz.paired:
        return [swapped(hour_messages[0], "hour", 1)]
    steps = range(sz.hour_parts - 1)
    return [
        lax.ppermute(hour_messages[0], "hour", [(i, i + 1) for i in steps]),
        lax.ppermute(hour_messages[1], "hour", [(i + 1, i) for i in steps]),
    ]


def on_device(
    segment_flow,
    linepack,
    mass_dual,
    momentum_dual,
    contract_dual,
    flow_cost,
    injection,
    contract_target,
    friction_table,
    friction_class,
    matching,
    contract_map,
):
    hours, segs, pipes = segment_flow.shape
    chunk, classes = contract_dual.shape[2:]
    sz = Sizes(hours, segs, pipes, chunk, classes, friction_table.shape[0])
    duals_now = contract_dual.reshape(hours, chunk, classes)
    target_now = contract_target.reshape(hours, chunk, classes)
    matching = matching.reshape(1, matching.shape[0])
    cells, contracts = (hours, segs, pipes), (hours, segs, classes)
    layer_shapes = [(2 * segs + SUBLANES, pipes)]
    raw_shapes = [(2 * segs + SUBLANES + rounded_up(chunk), pipes)]
    if not sz.paired:
        layer_shapes.append((segs, pipes))
        raw_shapes.append((segs, pipes))
    scalars_shape = (SUBLANES, 2 * LANES)
    found_scratch = [pltpu.VMEM((sz.end_rows, pipes), jnp.float32)]

    state = [segment_flow, linepack, mass_dual, momentum_dual]
    raw = [*state, flow_cost, friction_class, duals_now, contract_map]
    seg_message, *hour_messages = local_call(
        functools.partial(start_kernel, sz),
        [(rounded_up(7 * hours), pipes), *raw_shapes],
        [("smem", friction_table)] + [("hbm", array) for array in raw],
        scratch=start_scratch(sz),
    )
    seg_in = swapped(seg_message, "seg", 1)
    hours_in = layers_exchanged(sz, hour_messages)
    message, corner = local_call(
        functools.partial(relay_kernel, sz),
        [(sz.first_ends + sz.end_packed, classes), (SUBLANES, pipes)],
        vmem(duals_now, seg_in, *hours_in),
    )
    messages = gathered(sz, message)
    corner_in = swapped(corner, "seg", 1)

    def message_shape(final):
        return (sz.sums + SUBLANES + (0 if final else sz.end_packed), classes)

    final = ITERS == 1
    args = vmem(*state, flow_cost, injection, friction_class, contract_map, target_now)
    args += vmem(matching, *messages, seg_in, *hours_in, corner_in)
    results = local_call(
        functools.partial(first_kernel, sz, final),
        [cells] * 4
        + [message_shape(final), contracts, (segs, pipes)]
        + ([] if final else layer_shapes),
        [("smem", friction_table)] + args,
        kept=True,
        scratch=[pltpu.VMEM((segs, classes), jnp.float32)] + found_scratch,
    )
    state, message, duals, friction = results[:4], *results[4:7]
    hour_messages = results[7:]
    weight = jnp.ones((1, 1), jnp.float32)
    for iteration in range(1, ITERS):
        final = iteration == ITERS - 1
        messages = gathered(sz, message)
        hours_in = layers_exchanged(sz, hour_messages)
        args = vmem(*state, flow_cost, friction, contract_map, matching)
        args += vmem(*messages, *hours_in, duals, weight)
        spread_rows = segs + (SUBLANES if sz.paired else 0)
        seg_message, spread_message, duals, spread, scalars = local_call(
            functools.partial(spread_kernel, sz),
            [(sz.seg_tail + SUBLANES, pipes), (spread_rows, pipes), contracts, cells]
            + [scalars_shape],
            args,
            kept=True,
            scratch=found_scratch,
        )
        seg_in = swapped(seg_message, "seg", 1)
        if sz.paired:
            spread_in = swapped(spread_message, "hour", 1)
            sums = [scalars, swapped(scalars, ("hour", "seg"), 3)]
        else:
            steps = range(sz.hour_parts - 1)
            spread_in = lax.ppermute(spread_message, "hour", [(i, i + 1) for i in steps])
            sums = [lax.psum(scalars, ("hour", "seg"))]
        args = vmem(*state, flow_cost, injection, friction, contract_map, target_now, spread)
        args += vmem(seg_in, *hours_in, spread_in, weight, *sums)
        results = local_call(
            functools.partial(later_kernel, sz, final),
            [cells] * 4
            + [message_shape(final), (1, 1)]
            + ([] if final else layer_shapes),
            args,
            kept=True,
        )
        state, message, weight = results[:4], *results[4:6]
        hour_messages = results[6:]
    contract_out, scalars = local_call(
        functools.partial(close_kernel, sz),
        [(hours, chunk, classes), scalars_shape],
        vmem(*gathered(sz, message), duals, weight),
        kept=True,
    )
    if sz.paired:
        sums = [scalars] + [swapped(scalars, ("hour", "seg"), k) for k in (1, 2, 3)]
    else:
        sums = [lax.psum(scalars, ("hour", "seg"))]
    (weight,) = local_call(weight_kernel, [(1, 1)], vmem(weight, *sums), kept=True)
    return (
        *state,
        contract_out.reshape(contract_dual.shape),
        weight.reshape(1),
    )


def solution(mesh):
    cells = P(("groups", "hour"), "seg", "pipe")
    contracts = P(("groups", "hour"), "seg", "pipe", None)
    return jax.shard_map(
        on_device,
        mesh=mesh,
        in_specs=(
            cells,
            cells,
            cells,
            cells,
            contracts,
            cells,
            cells,
            contracts,
            P(),
            P("seg", ("groups", "pipe")),
            P("groups"),
            P(("groups", "hour"), None),
        ),
        out_specs=(cells, cells, cells, cells, contracts, P("groups")),
        check_vma=False,
    )
```

```python
import functools

import jax
import jax.numpy as jnp
from jax import lax
from jax.experimental import pallas as pl
from jax.experimental.pallas import tpu as pltpu
from jax.sharding import PartitionSpec as P

ITERS = 2

FLOW_CAP = 1.5
PACK_CAP = 2.5
STEP_SCALE = 0.25
NORM_EPS = 1e-06

LANES = 128
SUBLANES = 8
VMEM_LIMIT = 8 * 1024 * 1024
SHIFTED = True
NT = (((1,), (1,)), ((), ()))
NN = (((1,), (0,)), ((), ()))


def rounded_up(count):
    return -(-count // SUBLANES) * SUBLANES


def local_call(body, outs, args, kept=False, scratch=()):
    spaces = {"smem": pltpu.SMEM, "vmem": pltpu.VMEM, "hbm": pltpu.HBM}
    shape_of = pltpu.VMEM if kept else jax.ShapeDtypeStruct
    arrays = [
        pltpu.with_memory_space_constraint(array, pltpu.HBM) if space == "hbm" else array
        for space, array in args
    ]
    results = pl.pallas_call(
        body,
        out_shape=[shape_of(shape, jnp.float32) for shape in outs],
        in_specs=[pl.BlockSpec(memory_space=spaces[space]) for space, _ in args],
        out_specs=[pl.BlockSpec(memory_space=pltpu.VMEM) for _ in outs],
        scratch_shapes=scratch,
        compiler_params=pltpu.CompilerParams(vmem_limit_bytes=VMEM_LIMIT),
    )(*arrays)
    return list(results)


def vmem(*arrays):
    return [("vmem", array) for array in arrays]


def taker(refs):
    refs = list(refs)

    def take(count):
        return [refs.pop(0) for _ in range(count)]

    return take


def parts_of(values):
    high = values.astype(jnp.bfloat16).astype(jnp.float32)
    rest = values - high
    middle = rest.astype(jnp.bfloat16).astype(jnp.float32)
    return jnp.concatenate([high, middle, rest - middle], axis=0).astype(jnp.bfloat16)


def exact_product(values, onehot, dims):
    rows = values.shape[0]
    product = lax.dot_general(
        parts_of(values), onehot, dims, preferred_element_type=jnp.float32
    )
    return product[:rows] + product[rows : 2 * rows] + product[2 * rows :]


def as_onehot(mask):
    return jnp.where(mask, 1.0, 0.0).astype(jnp.bfloat16)


def contract_onehot(map_row, class_count):
    shape = (class_count, map_row.shape[1])
    return as_onehot(lax.broadcasted_iota(jnp.int32, shape, 0) == map_row)


def friction_of(classes, table_ref, levels):
    friction = jnp.zeros(classes.shape, jnp.float32)
    for level in range(levels):
        friction = jnp.where(classes == level, table_ref[level], friction)
    return friction


def folded(values):
    rows, width = values.shape
    total = values[:SUBLANES]
    for start in range(SUBLANES, rows, SUBLANES):
        total = total + values[start : start + SUBLANES]
    result = total[:, :LANES]
    for start in range(LANES, width, LANES):
        result = result + total[:, start : start + LANES]
    return result


def tree_sum(terms):
    while len(terms) > 1:
        terms = [a + b for a, b in zip(terms[0::2], terms[1::2])]
    return terms[0]


def swapped(message, axes, distance):
    count = lax.axis_size(axes)
    return lax.ppermute(message, axes, [(i, i ^ distance) for i in range(count)])


class Sizes:
    def __init__(self, hours, segs, pipes, chunk, classes, levels):
        self.hours, self.segs, self.pipes = hours, segs, pipes
        self.chunk, self.classes, self.levels = chunk, classes, levels
        self.blocks = lax.axis_size("pipe")
        self.hour_parts = lax.axis_size("hour")
        self.share = classes / (pipes * self.blocks)
        self.halves = pipes // LANES
        self.paired = self.hour_parts == 2
        self.shifted = SHIFTED and self.blocks == 4
        self.end_rows = 2 * hours
        self.end_packed = self.end_rows * self.halves
        self.sums = hours * segs
        self.halo_hour = rounded_up(hours * chunk)
        self.halo_seg = self.halo_hour + rounded_up(chunk)
        self.first_ends = self.halo_seg + rounded_up(hours)
        self.matched = 7 * hours
        self.seg_tail = rounded_up(9 * hours)

    def owner(self, block, index):
        if self.shifted:
            return lax.rem(block + (self.blocks - index), self.blocks)
        return lax.bitwise_xor(block, index)

    def added(self, block, terms):
        if self.shifted:
            even = lax.rem(block, 2) == 0
            one, two, three = terms[1:]
            terms = [terms[0], jnp.where(even, three, one), two, jnp.where(even, one, three)]
        return tree_sum(terms)

    def own_pipes(self, block):
        return pl.ds(pl.multiple_of(block * self.pipes, LANES), self.pipes)


def places():
    return lax.axis_index("pipe"), lax.axis_index("hour"), lax.axis_index("seg") == 0


def write_ends(sz, message, start, rows):
    for index, row in enumerate(rows):
        for half in range(sz.halves):
            at = start + half * sz.end_rows + index
            message[at : at + 1, :] = row[:, half * LANES : (half + 1) * LANES]


def read_ends(sz, message, start):
    pieces = [
        message[start + half * sz.end_rows : start + (half + 1) * sz.end_rows, :]
        for half in range(sz.halves)
    ]
    return jnp.concatenate(pieces, axis=1)


def write_edges(sz, message, first_rows, last_rows, resistance):
    for t in range(sz.hours):
        mass, pack, momentum = [ref(t) for ref in first_rows]
        last_mass, flow, last_momentum, cost = [ref(t) for ref in last_rows]
        gap = cost - last_mass - resistance * last_momentum
        rows = [mass, pack, mass - momentum, last_momentum, flow, gap]
        for slot, row in enumerate(rows):
            at = slot * sz.hours + t
            message[at : at + 1, :] = row


def write_layers(sz, outs, first_hour, pack, mass, momentum, first_mass):
    segs = sz.segs
    top = lax.broadcasted_iota(jnp.int32, (segs, sz.pipes), 0) == 0
    gradient = mass - momentum + jnp.where(top, 0.0, pltpu.roll(momentum, 1, 0))
    if sz.paired:
        outs[0][0:segs, :] = jnp.where(first_hour, pack, first_mass)
    else:
        outs[0][0:segs, :] = pack
        outs[1][...] = first_mass
    outs[0][segs : 2 * segs, :] = gradient
    outs[0][2 * segs : 2 * segs + SUBLANES, :] = jnp.zeros((SUBLANES, sz.pipes), jnp.float32)
    outs[0][2 * segs : 2 * segs + 1, :] = momentum[segs - 1 : segs, :]


def matched_rows(sz, block, inlet_side, ends, matching, found):
    shape = (sz.pipes, sz.pipes)
    row = lax.broadcasted_iota(jnp.int32, shape, 0)
    total = jnp.zeros((sz.end_rows, sz.pipes), jnp.float32)

    @pl.when(inlet_side)
    def _():
        own = matching[0:1, sz.own_pipes(block)]
        result = total
        for index, values in enumerate(ends):
            there = row + sz.owner(block, index) * sz.pipes
            result = result + exact_product(values, as_onehot(there == own), NN)
        found[...] = result

    @pl.when(jnp.logical_not(inlet_side))
    def _():
        here = row + block * sz.pipes
        result = total
        for index, values in enumerate(ends):
            feeds = matching[0:1, sz.own_pipes(sz.owner(block, index))]
            result = result + exact_product(values, as_onehot(here == feeds), NT)
        found[...] = result


def start_kernel(sz, *refs):
    take = taker(refs)
    flow, pack, mass, momentum, cost, classes, duals, contract_map, table_in = take(9)
    seg_message, duals_own, *hour_messages = take(2 + (1 if sz.paired else 2))
    (flow_last, cost_last, mass_last, momentum_last) = take(4)
    (pack_first, mass_first, momentum_first, classes_last) = take(4)
    (pack_layer, mass_layer, momentum_layer, mass_start) = take(4)
    map_own, table, arrived = take(3)
    block, hour, first_seg = places()
    hours, segs = sz.hours, sz.segs
    low, high = pl.ds(0, SUBLANES), pl.ds(segs - SUBLANES, SUBLANES)
    copies = [
        (flow.at[:, high], flow_last),
        (cost.at[:, high], cost_last),
        (mass.at[:, high], mass_last),
        (momentum.at[:, high], momentum_last),
        (pack.at[:, low], pack_first),
        (mass.at[:, low], mass_first),
        (momentum.at[:, low], momentum_first),
        (classes.at[high], classes_last),
        (pack.at[hours - 1], pack_layer),
        (mass.at[hours - 1], mass_layer),
        (momentum.at[hours - 1], momentum_layer),
        (mass.at[0], mass_start),
        (duals, duals_own),
        (contract_map.at[:, sz.own_pipes(block)], map_own),
        (table_in, table),
    ]
    copies = [
        pltpu.make_async_copy(source, target, arrived.at[index])
        for index, (source, target) in enumerate(copies)
    ]
    for copy in copies:
        copy.start()
    seg_message[...] = jnp.zeros(seg_message.shape, jnp.float32)
    for copy in copies:
        copy.wait()
    end = SUBLANES - 1
    resistance = friction_of(classes_last[...], table, sz.levels)[end:]
    write_edges(
        sz,
        seg_message,
        [lambda t, ref=ref: ref[t, 0:1, :] for ref in (mass_first, pack_first, momentum_first)],
        [
            lambda t, ref=ref: ref[t, end : end + 1, :]
            for ref in (mass_last, flow_last, momentum_last, cost_last)
        ],
        resistance,
    )
    for t in range(hours):
        at = 6 * hours + t
        seg_message[at : at + 1, : sz.classes] = duals_own[t, 0:1, :]
    write_layers(
        sz,
        hour_messages,
        hour == 0,
        pack_layer[...],
        mass_layer[...],
        momentum_layer[...],
        mass_start[...],
    )
    up = hour_messages[0]
    up[2 * segs + 1 : 2 * segs + 2, :] = map_own[hours - 1 : hours, :].astype(jnp.float32)
    halo = 2 * segs + SUBLANES
    up[halo:, :] = jnp.zeros((up.shape[0] - halo, sz.pipes), jnp.float32)
    up[halo : halo + sz.chunk, : sz.classes] = duals_own[hours - 1]


def start_scratch(sz):
    ends = (sz.hours, SUBLANES, sz.pipes)
    layer = (sz.segs, sz.pipes)
    return (
        [pltpu.VMEM(ends, jnp.float32)] * 7
        + [pltpu.VMEM((SUBLANES, sz.pipes), jnp.int32)]
        + [pltpu.VMEM(layer, jnp.float32)] * 4
        + [
            pltpu.VMEM((sz.hours, sz.pipes), jnp.int32),
            pltpu.SMEM((sz.levels,), jnp.float32),
            pltpu.SemaphoreType.DMA((15,)),
        ]
    )


def relay_kernel(sz, *refs):
    take = taker(refs)
    duals, seg_in, *hours_in = take(2 + (1 if sz.paired else 2))
    message, corner = take(2)
    earlier_in, later_in = hours_in[0], hours_in[-1]
    block, hour, first_seg = places()
    hours, segs = sz.hours, sz.segs
    message[...] = jnp.zeros(message.shape, jnp.float32)
    for t in range(hours):
        message[t * sz.chunk : (t + 1) * sz.chunk, :] = duals[t]
    halo = 2 * segs + SUBLANES
    message[sz.halo_hour : sz.halo_hour + sz.chunk, :] = earlier_in[
        halo : halo + sz.chunk, : sz.classes
    ]
    message[sz.halo_seg : sz.halo_seg + hours, :] = seg_in[
        6 * hours : 7 * hours, : sz.classes
    ]
    rows = []
    for slot, mass_slot in ((4, 0), (5, 0)):
        for t in range(hours):
            outlet, inlet = slot * hours + t, mass_slot * hours + t
            rows.append(
                jnp.where(first_seg, seg_in[outlet : outlet + 1, :], seg_in[inlet : inlet + 1, :])
            )
    write_ends(sz, message, sz.first_ends, rows)
    corner[...] = jnp.zeros(corner.shape, jnp.float32)
    corner[0:1, :] = jnp.where(
        first_seg, earlier_in[2 * segs : 2 * segs + 1, :], later_in[0:1, :]
    )


def spread_kernel(sz, later, *refs):
    take = taker(refs)
    flow, pack, mass, momentum, cost, friction, contract_map, matching = take(8)
    messages = take(sz.blocks)
    hours_in = take(1 if sz.paired else 2)
    old_duals = take(1)[0]
    old_weight = take(1)[0][0:1, 0:1] if later else 1.0
    seg_message, hour_message, duals, spread, scalars, found = take(6)
    earlier_in, later_in = hours_in[0], hours_in[-1]
    block, hour, first_seg = places()
    hours, segs, pipes = sz.hours, sz.segs, sz.pipes
    last = segs - 1

    ends = [read_ends(sz, ref, sz.sums) for ref in messages]
    matched_rows(sz, block, jnp.logical_not(first_seg), ends, matching, found)

    dual_step = STEP_SCALE * old_weight
    dual_sq = jnp.zeros((SUBLANES, LANES), jnp.float32)
    for t in range(hours):
        totals = sz.added(block, [ref[t * segs : (t + 1) * segs, :] for ref in messages])
        change = dual_step * totals
        duals[t] = old_duals[t] - change
        dual_sq = dual_sq + folded(change * change)
        onehot = contract_onehot(contract_map[t : t + 1, sz.own_pipes(block)], sz.classes)
        spread[t] = sz.share * exact_product(duals[t], onehot, NN)
    at = sz.sums + sz.end_packed
    write_squares(sz, block, [ref[at : at + SUBLANES, :] for ref in messages], dual_sq, scalars)

    seg_message[...] = jnp.zeros(seg_message.shape, jnp.float32)
    write_edges(
        sz,
        seg_message,
        [lambda t, ref=ref: ref[t, 0:1, :] for ref in (mass, pack, momentum)],
        [lambda t, ref=ref: ref[t, last:segs, :] for ref in (mass, flow, momentum, cost)],
        friction[last:segs, :],
    )
    for t in range(hours):
        at = 6 * hours + t
        seg_message[at : at + 1, :] = spread[t, 0:1, :]
    seg_message[sz.matched : sz.matched + sz.end_rows, :] = found[...]
    seg_message[sz.seg_tail : sz.seg_tail + 1, : 2 * LANES] = scalars[0:1, :]
    seg_message[sz.seg_tail + 1 : sz.seg_tail + 2, :] = jnp.where(
        first_seg, earlier_in[2 * segs : 2 * segs + 1, :], later_in[0:1, :]
    )
    hour_message[0:segs, :] = spread[hours - 1]
    if sz.paired:
        hour_message[segs:, :] = jnp.zeros((SUBLANES, pipes), jnp.float32)
        hour_message[segs : segs + 1, : 2 * LANES] = scalars[0:1, :]


def write_squares(sz, block, squares, dual_sq, scalars):
    total = sz.added(block, squares)
    scalars[...] = jnp.zeros(scalars.shape, jnp.float32)
    scalars[0:1, :LANES] = total[0:1]
    scalars[0:1, LANES:] = total[1:2] + jnp.sum(dual_sq, axis=0, keepdims=True)


def new_weight(weight, total):
    primal = jnp.sum(total[:, :LANES], axis=1, keepdims=True)
    dual = jnp.sum(total[:, LANES : 2 * LANES], axis=1, keepdims=True)
    return jnp.sqrt(weight * jnp.sqrt((dual + NORM_EPS) / (primal + NORM_EPS)))


def step(sz, block, hour, first_seg, weight, state, data, halo, spread_of, outs, message):
    flow, pack, mass, momentum = state
    cost, injection, resistance, contract_map, target = data
    flow_out, pack_out, mass_out, momentum_out = outs
    hours, segs, pipes = sz.hours, sz.segs, sz.pipes
    last, end = segs - 1, hours - 1
    has_earlier = hour > 0
    has_later = hour < sz.hour_parts - 1
    primal_step = STEP_SCALE / weight
    dual_step = STEP_SCALE * weight

    row_index = lax.broadcasted_iota(jnp.int32, (segs, pipes), 0)
    top, bottom = row_index == 0, row_index == last

    def from_above(values, row):
        return jnp.where(top, row, pltpu.roll(values, 1, 0))

    def from_below(values, row):
        return jnp.where(bottom, row, pltpu.roll(values, segs - 1, 0))

    def seg_row(slot, t):
        at = slot * hours + t
        return halo["seg"][at : at + 1, :]

    def matched_row(slot, t):
        at = halo["matched_at"] + slot * hours + t
        return halo["matched"][at : at + 1, :]

    def new_flow(start, gap):
        return jnp.clip(start - primal_step * gap, -FLOW_CAP, FLOW_CAP)

    def new_pack(start, gradient):
        return jnp.clip(start + primal_step * gradient, 0.0, PACK_CAP)

    corner = halo["corner"]
    earlier_pack = halo["earlier"][0:segs, :]
    earlier_gradient = (
        halo["earlier"][segs : 2 * segs, :]
        + halo["earlier_spread"]
        + jnp.where(top, jnp.where(first_seg, 0.0, corner), 0.0)
        - mass[0]
    )
    earlier_bar = jnp.where(
        has_earlier, 2.0 * new_pack(earlier_pack, earlier_gradient) - earlier_pack, 0.0
    )
    later_mass = jnp.where(has_later, halo["later"][0:segs, :], 0.0)
    later_corner = jnp.where(has_later, corner, 0.0)
    primal_sq = jnp.zeros((SUBLANES, LANES), jnp.float32)
    dual_sq = jnp.zeros((SUBLANES, LANES), jnp.float32)
    for t in range(hours):
        mass_now, momentum_now = mass[t], momentum[t]
        flow_now, pack_now = flow[t], pack[t]
        spread, edge_spread, onehot = spread_of(t)
        below_mass = jnp.where(first_seg, seg_row(0, t), matched_row(0, t))
        next_mass = mass[t + 1] if t < end else later_mass
        gap = cost[t] - (
            mass_now - from_below(mass_now, below_mass) + resistance * momentum_now
        )
        flow_next = new_flow(flow_now, gap)
        above_momentum = jnp.where(first_seg, 0.0, seg_row(3, t))
        gradient = (
            mass_now
            - next_mass
            - momentum_now
            + from_above(momentum_now, above_momentum)
            + spread
        )
        pack_next = new_pack(pack_now, gradient)
        flow_bar = 2.0 * flow_next - flow_now
        pack_bar = 2.0 * pack_next - pack_now

        edge_flow = jnp.where(first_seg, matched_row(0, t), seg_row(4, t))
        edge_gap = jnp.where(first_seg, matched_row(1, t), seg_row(5, t)) + mass_now[0:1, :]
        edge_flow_bar = 2.0 * new_flow(edge_flow, edge_gap) - edge_flow
        edge_pack = seg_row(1, t)
        edge_later = seg_row(0, t + 1) if t < end else later_corner
        edge_gradient = (
            seg_row(2, t) + edge_spread + momentum_now[last : last + 1, :] - edge_later
        )
        edge_pack_bar = jnp.where(
            first_seg, 2.0 * new_pack(edge_pack, edge_gradient) - edge_pack, 0.0
        )

        mass_rows = pack_bar - earlier_bar + flow_bar - from_above(flow_bar, edge_flow_bar)
        momentum_rows = resistance * flow_bar - (pack_bar - from_below(pack_bar, edge_pack_bar))
        mass_change = dual_step * (injection[t] - mass_rows)
        momentum_change = dual_step * momentum_rows
        flow_out[t] = flow_next
        pack_out[t] = pack_next
        mass_out[t] = mass_now + mass_change
        momentum_out[t] = momentum_now - momentum_change
        flow_change, pack_change = flow_next - flow_now, pack_next - pack_now
        primal_sq = primal_sq + folded(flow_change * flow_change + pack_change * pack_change)
        dual_sq = dual_sq + folded(
            mass_change * mass_change + momentum_change * momentum_change
        )
        message[t * segs : (t + 1) * segs, :] = sz.share * exact_product(pack_bar, onehot, NT)
        rows = pl.ds(pl.multiple_of(t * segs + block * sz.chunk, sz.chunk), sz.chunk)
        message[rows, :] = message[rows, :] - target[t]
        earlier_bar = pack_bar

    at = message.shape[0] - SUBLANES
    message[at:, :] = jnp.zeros((SUBLANES, LANES), jnp.float32)
    message[at : at + 1, :] = jnp.sum(primal_sq, axis=0, keepdims=True)
    message[at + 1 : at + 2, :] = jnp.sum(dual_sq, axis=0, keepdims=True)


def write_next(sz, hour, first_seg, outs, cost, resistance, message, hour_messages):
    flow, pack, mass, momentum = outs
    last = sz.segs - 1
    firsts = [mass[t, 0:1, :] for t in range(sz.hours)]
    lasts = [flow[t, last : last + 1, :] for t in range(sz.hours)]
    gaps = [
        cost[t, last : last + 1, :]
        - mass[t, last : last + 1, :]
        - resistance[last : last + 1, :] * momentum[t, last : last + 1, :]
        for t in range(sz.hours)
    ]
    rows = [jnp.where(first_seg, a, b) for a, b in zip(firsts + firsts, lasts + gaps)]
    write_ends(sz, message, sz.sums, rows)
    end = sz.hours - 1
    write_layers(sz, hour_messages, hour == 0, pack[end], mass[end], momentum[end], mass[0])


def first_kernel(sz, final, table, *refs):
    take = taker(refs)
    state, data = take(4), take(2)
    classes, contract_map, target, matching = take(4)
    messages, seg_in = take(sz.blocks), take(1)[0]
    hours_in, corner_in = take(1 if sz.paired else 2), take(1)[0]
    outs, message, duals, friction = take(4), *take(3)
    hour_messages = [] if final else take(1 if sz.paired else 2)
    halo_duals, found = take(2)
    block, hour, first_seg = places()
    hours, segs, chunk = sz.hours, sz.segs, sz.chunk
    friction[...] = friction_of(classes[...], table, sz.levels)
    edge_duals = jnp.zeros((hours, sz.classes), jnp.float32)
    for index, ref in enumerate(messages):
        owner = sz.owner(block, index)
        rows = pl.ds(pl.multiple_of(owner * chunk, chunk), chunk)
        for t in range(hours):
            duals[t, rows, :] = ref[t * chunk : (t + 1) * chunk, :]
        halo_duals[rows, :] = ref[sz.halo_hour : sz.halo_hour + chunk, :]
        edge_duals = jnp.where(
            owner == 0, ref[sz.halo_seg : sz.halo_seg + hours, :], edge_duals
        )
    ends = [read_ends(sz, ref, sz.first_ends) for ref in messages]
    matched_rows(sz, block, first_seg, ends, matching, found)
    map_row = hours_in[0][2 * segs + 1 : 2 * segs + 2, :].astype(jnp.int32)
    earlier_spread = sz.share * exact_product(
        halo_duals[...], contract_onehot(map_row, sz.classes), NN
    )

    def spread_of(t):
        onehot = contract_onehot(contract_map[t : t + 1, sz.own_pipes(block)], sz.classes)
        edge = jnp.broadcast_to(edge_duals[t : t + 1, :], (2 * SUBLANES, sz.classes))
        values = jnp.concatenate([duals[t], edge], axis=0)
        product = sz.share * exact_product(values, onehot, NN)
        return product[:segs], product[segs : segs + 1], onehot

    halo = {
        "seg": seg_in,
        "matched": found,
        "matched_at": 0,
        "corner": corner_in[0:1, :],
        "earlier": hours_in[0],
        "earlier_spread": earlier_spread,
        "later": hours_in[-1],
    }
    resistance = friction[...]
    data = [*data, resistance, contract_map, target]
    one = jnp.ones((1, 1), jnp.float32)
    step(sz, block, hour, first_seg, one, state, data, halo, spread_of, outs, message)
    if not final:
        write_next(sz, hour, first_seg, outs, data[0], resistance, message, hour_messages)


def later_kernel(sz, later, final, *refs):
    take = taker(refs)
    state, data = take(4), take(2)
    friction, contract_map, target, spread = take(4)
    seg_in, hours_in, spread_in = take(1)[0], take(1 if sz.paired else 2), take(1)[0]
    old_weight = take(1)[0][0:1, 0:1] if later else 1.0
    scalars = take(1)[0]
    corner_scalars = take(1) if sz.paired else []
    outs, message, weight_out = take(4), *take(2)
    hour_messages = [] if final else take(1 if sz.paired else 2)
    block, hour, first_seg = places()
    hours, segs = sz.hours, sz.segs
    total = scalars[0:1, :]
    if sz.paired:
        total = tree_sum(
            [
                total,
                seg_in[sz.seg_tail : sz.seg_tail + 1, : 2 * LANES],
                spread_in[segs : segs + 1, : 2 * LANES],
                corner_scalars[0][0:1, :],
            ]
        )
    weight = new_weight(old_weight, total)
    weight_out[...] = jnp.broadcast_to(weight, weight_out.shape)

    def spread_of(t):
        onehot = contract_onehot(contract_map[t : t + 1, sz.own_pipes(block)], sz.classes)
        at = 6 * hours + t
        return spread[t], seg_in[at : at + 1, :], onehot

    halo = {
        "seg": seg_in,
        "matched": seg_in,
        "matched_at": sz.matched,
        "corner": seg_in[sz.seg_tail + 1 : sz.seg_tail + 2, :],
        "earlier": hours_in[0],
        "earlier_spread": spread_in[0:segs, :],
        "later": hours_in[-1],
    }
    resistance = friction[...]
    data = [*data, resistance, contract_map, target]
    step(sz, block, hour, first_seg, weight, state, data, halo, spread_of, outs, message)
    if not final:
        write_next(sz, hour, first_seg, outs, data[0], resistance, message, hour_messages)


def close_kernel(sz, *refs):
    take = taker(refs)
    messages = take(sz.blocks)
    old_duals, weight, written, duals, scalars = take(5)
    block, hour, first_seg = places()
    segs = sz.segs
    dual_step = STEP_SCALE * weight[0:1, 0:1]
    dual_sq = jnp.zeros((SUBLANES, LANES), jnp.float32)
    start = block * sz.chunk
    for t in range(sz.hours):
        totals = sz.added(block, [ref[t * segs : (t + 1) * segs, :] for ref in messages])
        change = dual_step * totals
        dual_sq = dual_sq + folded(change * change)
        own = pl.ds(pl.multiple_of(start, sz.chunk), sz.chunk)
        rows = pl.ds(pl.multiple_of(t * segs + start, sz.chunk), sz.chunk)
        own_totals = sz.added(block, [ref[rows, :] for ref in messages])
        duals[t] = old_duals[t, own, :] - dual_step * own_totals
    squares = [ref[sz.sums : sz.sums + SUBLANES, :] for ref in messages]
    write_squares(sz, block, squares, dual_sq, scalars)


def written_out(state):
    count = len(state)

    def body(*refs):
        sources, targets, token, done = refs[:count], refs[count:-2], refs[-2], refs[-1]
        copies = [
            pltpu.make_async_copy(source, target, done.at[index])
            for index, (source, target) in enumerate(zip(sources, targets))
        ]
        for copy in copies:
            copy.start()
        token[...] = jnp.zeros(token.shape, jnp.float32)
        for copy in copies:
            copy.wait()

    return pl.pallas_call(
        body,
        out_shape=[pltpu.HBM(array.shape, array.dtype) for array in state]
        + [pltpu.VMEM((SUBLANES, LANES), jnp.float32)],
        in_specs=[pl.BlockSpec(memory_space=pltpu.VMEM) for _ in state],
        out_specs=[pl.BlockSpec(memory_space=pltpu.HBM) for _ in state]
        + [pl.BlockSpec(memory_space=pltpu.VMEM)],
        scratch_shapes=[pltpu.SemaphoreType.DMA((count,))],
        compiler_params=pltpu.CompilerParams(vmem_limit_bytes=VMEM_LIMIT),
    )(*state)


def weight_kernel(weight, *refs):
    *scalars, result = refs
    result[...] = new_weight(weight[0:1, 0:1], tree_sum([ref[0:1, :] for ref in scalars]))


def gathered(sz, message):
    if sz.shifted:
        ring = [
            [(i, (i + k) % sz.blocks) for i in range(sz.blocks)] for k in range(1, sz.blocks)
        ]
        return [message] + [lax.ppermute(message, "pipe", pairs) for pairs in ring]
    return [message] + [swapped(message, "pipe", k) for k in range(1, sz.blocks)]


def layers_exchanged(sz, hour_messages):
    if sz.paired:
        return [swapped(hour_messages[0], "hour", 1)]
    steps = range(sz.hour_parts - 1)
    return [
        lax.ppermute(hour_messages[0], "hour", [(i, i + 1) for i in steps]),
        lax.ppermute(hour_messages[1], "hour", [(i + 1, i) for i in steps]),
    ]


def on_device(
    segment_flow,
    linepack,
    mass_dual,
    momentum_dual,
    contract_dual,
    flow_cost,
    injection,
    contract_target,
    friction_table,
    friction_class,
    matching,
    contract_map,
):
    hours, segs, pipes = segment_flow.shape
    chunk, classes = contract_dual.shape[2:]
    sz = Sizes(hours, segs, pipes, chunk, classes, friction_table.shape[0])
    duals_now = contract_dual.reshape(hours, chunk, classes)
    target_now = contract_target.reshape(hours, chunk, classes)
    matching = matching.reshape(1, matching.shape[0])
    cells, contracts = (hours, segs, pipes), (hours, segs, classes)
    layer_shapes = [(2 * segs + SUBLANES, pipes)]
    raw_shapes = [(2 * segs + SUBLANES + rounded_up(chunk), pipes)]
    if not sz.paired:
        layer_shapes.append((segs, pipes))
        raw_shapes.append((segs, pipes))
    scalars_shape = (SUBLANES, 2 * LANES)
    found_scratch = [pltpu.VMEM((sz.end_rows, pipes), jnp.float32)]

    state = [segment_flow, linepack, mass_dual, momentum_dual]
    raw = [*state, flow_cost, friction_class, duals_now, contract_map, friction_table]
    seg_message, own_duals, *hour_messages = local_call(
        functools.partial(start_kernel, sz),
        [(rounded_up(7 * hours), pipes), (hours, chunk, classes), *raw_shapes],
        [("hbm", array) for array in raw],
        kept=True,
        scratch=start_scratch(sz),
    )
    seg_in = swapped(seg_message, "seg", 1)
    hours_in = layers_exchanged(sz, hour_messages)
    message, corner = local_call(
        functools.partial(relay_kernel, sz),
        [(sz.first_ends + sz.end_packed, classes), (SUBLANES, pipes)],
        vmem(own_duals, seg_in, *hours_in),
        kept=True,
    )
    messages = gathered(sz, message)
    corner_in = swapped(corner, "seg", 1)

    def message_shape(final):
        return (sz.sums + SUBLANES + (0 if final else sz.end_packed), classes)

    final = ITERS == 1
    args = vmem(*state, flow_cost, injection, friction_class, contract_map, target_now)
    args += vmem(matching, *messages, seg_in, *hours_in, corner_in)
    results = local_call(
        functools.partial(first_kernel, sz, final),
        [cells] * 4
        + [message_shape(final), contracts, (segs, pipes)]
        + ([] if final else layer_shapes),
        [("smem", friction_table)] + args,
        kept=True,
        scratch=[pltpu.VMEM((segs, classes), jnp.float32)] + found_scratch,
    )
    state, message, duals, friction = results[:4], *results[4:7]
    hour_messages = results[7:]
    weight = []
    for iteration in range(1, ITERS):
        later, final = iteration > 1, iteration == ITERS - 1
        messages = gathered(sz, message)
        hours_in = layers_exchanged(sz, hour_messages)
        args = vmem(*state, flow_cost, friction, contract_map, matching)
        args += vmem(*messages, *hours_in, duals, *weight)
        spread_rows = segs + (SUBLANES if sz.paired else 0)
        seg_message, spread_message, duals, spread, scalars = local_call(
            functools.partial(spread_kernel, sz, later),
            [(sz.seg_tail + SUBLANES, pipes), (spread_rows, pipes), contracts, cells]
            + [scalars_shape],
            args,
            kept=True,
            scratch=found_scratch,
        )
        seg_in = swapped(seg_message, "seg", 1)
        if sz.paired:
            spread_in = swapped(spread_message, "hour", 1)
            sums = [scalars, swapped(scalars, ("hour", "seg"), 3)]
        else:
            steps = range(sz.hour_parts - 1)
            spread_in = lax.ppermute(spread_message, "hour", [(i, i + 1) for i in steps])
            sums = [lax.psum(scalars, ("hour", "seg"))]
        args = vmem(*state, flow_cost, injection, friction, contract_map, target_now, spread)
        args += vmem(seg_in, *hours_in, spread_in, *weight, *sums)
        results = local_call(
            functools.partial(later_kernel, sz, later, final),
            [cells] * 4
            + [message_shape(final), (SUBLANES, LANES)]
            + ([] if final else layer_shapes),
            args,
            kept=True,
        )
        state, message, weight = results[:4], results[4], results[5:6]
        hour_messages = results[6:]
    *state, written = written_out(state)
    contract_out, scalars = local_call(
        functools.partial(close_kernel, sz),
        [(hours, chunk, classes), scalars_shape],
        vmem(*gathered(sz, message), duals, *weight, written),
        kept=True,
    )
    if sz.paired:
        sums = [scalars] + [swapped(scalars, ("hour", "seg"), k) for k in (1, 2, 3)]
    else:
        sums = [lax.psum(scalars, ("hour", "seg"))]
    (weight,) = local_call(weight_kernel, [(1, 1)], vmem(*weight, *sums))
    return (
        *state,
        contract_out.reshape(contract_dual.shape),
        weight.reshape(1),
    )


def solution(mesh):
    cells = P(("groups", "hour"), "seg", "pipe")
    contracts = P(("groups", "hour"), "seg", "pipe", None)
    return jax.shard_map(
        on_device,
        mesh=mesh,
        in_specs=(
            cells,
            cells,
            cells,
            cells,
            contracts,
            cells,
            cells,
            contracts,
            P(),
            P("seg", ("groups", "pipe")),
            P("groups"),
            P(("groups", "hour"), None),
        ),
        out_specs=(cells, cells, cells, cells, contracts, P("groups")),
        check_vma=False,
    )
```

```python
import functools

import jax
import jax.numpy as jnp
from jax import lax
from jax.experimental import pallas as pl
from jax.experimental.pallas import tpu as pltpu
from jax.sharding import PartitionSpec as P

ITERS = 2

FLOW_CAP = 1.5
PACK_CAP = 2.5
STEP_SCALE = 0.25
NORM_EPS = 1e-06

LANES = 128
SUBLANES = 8
VMEM_LIMIT = 8 * 1024 * 1024
PIPE_ORDER = (1, 3, 2)
NT = (((1,), (1,)), ((), ()))
NN = (((1,), (0,)), ((), ()))


def rounded_up(count):
    return -(-count // SUBLANES) * SUBLANES


def local_call(body, outs, args, kept=False, scratch=(), kinds={}):
    spaces = {"smem": pltpu.SMEM, "vmem": pltpu.VMEM, "hbm": pltpu.HBM}
    shape_of = pltpu.VMEM if kept else jax.ShapeDtypeStruct
    arrays = [
        pltpu.with_memory_space_constraint(array, pltpu.HBM) if space == "hbm" else array
        for space, array in args
    ]
    results = pl.pallas_call(
        body,
        out_shape=[shape_of(shape, kinds.get(index, jnp.float32)) for index, shape in enumerate(outs)],
        in_specs=[pl.BlockSpec(memory_space=spaces[space]) for space, _ in args],
        out_specs=[pl.BlockSpec(memory_space=pltpu.VMEM) for _ in outs],
        scratch_shapes=scratch,
        compiler_params=pltpu.CompilerParams(vmem_limit_bytes=VMEM_LIMIT),
    )(*arrays)
    return list(results)


def vmem(*arrays):
    return [("vmem", array) for array in arrays]


def taker(refs):
    refs = list(refs)

    def take(count):
        return [refs.pop(0) for _ in range(count)]

    return take


def parts_of(values):
    high = values.astype(jnp.bfloat16).astype(jnp.float32)
    rest = values - high
    middle = rest.astype(jnp.bfloat16).astype(jnp.float32)
    return jnp.concatenate([high, middle, rest - middle], axis=0).astype(jnp.bfloat16)


def exact_product(values, onehot, dims):
    rows = values.shape[0]
    product = lax.dot_general(
        parts_of(values), onehot, dims, preferred_element_type=jnp.float32
    )
    return product[:rows] + product[rows : 2 * rows] + product[2 * rows :]


def as_onehot(mask):
    return jnp.where(mask, 1.0, 0.0).astype(jnp.bfloat16)


def contract_onehot(map_row, class_count):
    shape = (class_count, map_row.shape[1])
    return as_onehot(lax.broadcasted_iota(jnp.int32, shape, 0) == map_row)


def friction_of(classes, table_ref, levels):
    friction = jnp.zeros(classes.shape, jnp.float32)
    for level in range(levels):
        friction = jnp.where(classes == level, table_ref[level], friction)
    return friction


def folded(values):
    rows, width = values.shape
    total = values[:SUBLANES]
    for start in range(SUBLANES, rows, SUBLANES):
        total = total + values[start : start + SUBLANES]
    result = total[:, :LANES]
    for start in range(LANES, width, LANES):
        result = result + total[:, start : start + LANES]
    return result


def tree_sum(terms):
    while len(terms) > 1:
        terms = [a + b for a, b in zip(terms[0::2], terms[1::2])]
    return terms[0]


def swapped(message, axes, distance):
    count = lax.axis_size(axes)
    return lax.ppermute(message, axes, [(i, i ^ distance) for i in range(count)])


class Sizes:
    def __init__(self, hours, segs, pipes, chunk, classes, levels):
        self.hours, self.segs, self.pipes = hours, segs, pipes
        self.chunk, self.classes, self.levels = chunk, classes, levels
        self.blocks = lax.axis_size("pipe")
        self.hour_parts = lax.axis_size("hour")
        self.share = classes / (pipes * self.blocks)
        self.halves = pipes // LANES
        self.paired = self.hour_parts == 2
        self.pipe_order = PIPE_ORDER if self.blocks == 4 else range(1, self.blocks)
        self.end_rows = 2 * hours
        self.end_packed = self.end_rows * self.halves
        self.sums = hours * segs
        self.first_ends = rounded_up(hours * chunk)
        self.matched = 7 * hours
        self.seg_tail = rounded_up(9 * hours)

    def owner(self, block, index):
        return lax.bitwise_xor(block, index)

    def own_pipes(self, block):
        return pl.ds(pl.multiple_of(block * self.pipes, LANES), self.pipes)


def take_messages(sz, take):
    own, *received = take(sz.blocks)
    by_distance = dict(zip(sz.pipe_order, received))
    return [own] + [by_distance[distance] for distance in range(1, sz.blocks)]


def places():
    return lax.axis_index("pipe"), lax.axis_index("hour"), lax.axis_index("seg") == 0


def write_ends(sz, message, start, rows):
    for index, row in enumerate(rows):
        for half in range(sz.halves):
            at = start + half * sz.end_rows + index
            message[at : at + 1, :] = row[:, half * LANES : (half + 1) * LANES]


def read_ends(sz, message, start):
    pieces = [
        message[start + half * sz.end_rows : start + (half + 1) * sz.end_rows, :]
        for half in range(sz.halves)
    ]
    return jnp.concatenate(pieces, axis=1)


def write_edges(sz, message, first_rows, last_rows, resistance):
    for t in range(sz.hours):
        mass, pack, momentum = [ref(t) for ref in first_rows]
        last_mass, flow, last_momentum, cost = [ref(t) for ref in last_rows]
        gap = cost - last_mass - resistance * last_momentum
        rows = [mass, pack, mass - momentum, last_momentum, flow, gap]
        for slot, row in enumerate(rows):
            at = slot * sz.hours + t
            message[at : at + 1, :] = row


def write_layers(sz, outs, first_hour, pack, mass, momentum, first_mass):
    segs = sz.segs
    top = lax.broadcasted_iota(jnp.int32, (segs, sz.pipes), 0) == 0
    gradient = mass - momentum + jnp.where(top, 0.0, pltpu.roll(momentum, 1, 0))
    if sz.paired:
        outs[0][0:segs, :] = jnp.where(first_hour, pack, first_mass)
    else:
        outs[0][0:segs, :] = pack
        outs[1][...] = first_mass
    outs[0][segs : 2 * segs, :] = gradient
    outs[0][2 * segs : 2 * segs + SUBLANES, :] = jnp.zeros((SUBLANES, sz.pipes), jnp.float32)
    outs[0][2 * segs : 2 * segs + 1, :] = momentum[segs - 1 : segs, :]


def matched_rows(sz, block, inlet_side, ends, matching, found):
    shape = (sz.pipes, sz.pipes)
    row = lax.broadcasted_iota(jnp.int32, shape, 0)
    total = jnp.zeros((sz.end_rows, sz.pipes), jnp.float32)

    @pl.when(inlet_side)
    def _():
        own = matching[0:1, sz.own_pipes(block)]
        result = total
        for index, values in enumerate(ends):
            there = row + sz.owner(block, index) * sz.pipes
            result = result + exact_product(values, as_onehot(there == own), NN)
        found[...] = result

    @pl.when(jnp.logical_not(inlet_side))
    def _():
        here = row + block * sz.pipes
        result = total
        for index, values in enumerate(ends):
            feeds = matching[0:1, sz.own_pipes(sz.owner(block, index))]
            result = result + exact_product(values, as_onehot(here == feeds), NT)
        found[...] = result


def start_kernel(sz, *refs):
    take = taker(refs)
    flow, pack, mass, momentum, cost, classes_in, duals_in, contract_map, table_in = take(9)
    matching_in = take(1)[0]
    message, friction, matching, *hour_messages = take(3 + (1 if sz.paired else 2))
    flow_last, cost_last, mass_last, momentum_last, mass_first = take(5)
    pack_layer, mass_layer, momentum_layer, mass_start = take(4)
    duals, map_own, classes, table, arrived = take(5)
    block, hour, first_seg = places()
    hours, segs = sz.hours, sz.segs
    low, high = pl.ds(0, SUBLANES), pl.ds(segs - SUBLANES, SUBLANES)
    copies = [
        (flow.at[:, high], flow_last),
        (cost.at[:, high], cost_last),
        (mass.at[:, high], mass_last),
        (momentum.at[:, high], momentum_last),
        (mass.at[:, low], mass_first),
        (pack.at[hours - 1], pack_layer),
        (mass.at[hours - 1], mass_layer),
        (momentum.at[hours - 1], momentum_layer),
        (mass.at[0], mass_start),
        (duals_in, duals),
        (contract_map.at[:, sz.own_pipes(block)], map_own),
        (classes_in, classes),
        (table_in, table),
        (matching_in, matching),
    ]
    copies = [
        pltpu.make_async_copy(source, target, arrived.at[index])
        for index, (source, target) in enumerate(copies)
    ]
    for copy in copies:
        copy.start()
    for copy in copies:
        copy.wait()
    friction[...] = friction_of(classes[...], table, sz.levels)
    end = SUBLANES - 1
    firsts = [mass_first[t, 0:1, :] for t in range(hours)]
    lasts = [flow_last[t, end : end + 1, :] for t in range(hours)]
    gaps = [
        cost_last[t, end : end + 1, :]
        - mass_last[t, end : end + 1, :]
        - friction[segs - 1 : segs, :] * momentum_last[t, end : end + 1, :]
        for t in range(hours)
    ]
    for t in range(hours):
        message[t * sz.chunk : (t + 1) * sz.chunk, :] = duals[t]
    rows = [jnp.where(first_seg, a, b) for a, b in zip(firsts + firsts, lasts + gaps)]
    write_ends(sz, message, sz.first_ends, rows)
    write_layers(
        sz,
        hour_messages,
        hour == 0,
        pack_layer[...],
        mass_layer[...],
        momentum_layer[...],
        mass_start[...],
    )
    map_row = map_own[hours - 1 : hours, :].astype(jnp.float32)
    hour_messages[0][2 * segs + 1 : 2 * segs + 2, :] = map_row


def start_scratch(sz):
    ends = pltpu.VMEM((sz.hours, SUBLANES, sz.pipes), jnp.float32)
    layer = pltpu.VMEM((sz.segs, sz.pipes), jnp.float32)
    return (
        [ends] * 5
        + [layer] * 4
        + [
            pltpu.VMEM((sz.hours, sz.chunk, sz.classes), jnp.float32),
            pltpu.VMEM((sz.hours, sz.pipes), jnp.int32),
            pltpu.VMEM((sz.segs, sz.pipes), jnp.int32),
            pltpu.SMEM((sz.levels,), jnp.float32),
            pltpu.SemaphoreType.DMA((14,)),
        ]
    )


def spread_kernel(sz, iteration, *refs):
    take = taker(refs)
    first = iteration == 0
    flow, pack, mass, momentum, cost, friction, contract_map, matching = take(8)
    messages = take_messages(sz, take)
    hours_in = take(1 if sz.paired else 2)
    old_duals = None if first else take(1)[0]
    old_weight = take(1)[0][0:1, 0:1] if iteration > 1 else 1.0
    seg_message, hour_message, duals, spread = take(4)
    scalars = None if first else take(1)[0]
    found = take(1)[0]
    earlier_in, later_in = hours_in[0], hours_in[-1]
    block, hour, first_seg = places()
    hours, segs, pipes, chunk = sz.hours, sz.segs, sz.pipes, sz.chunk
    last = segs - 1

    ends = [read_ends(sz, ref, sz.first_ends if first else sz.sums) for ref in messages]
    matched_rows(sz, block, jnp.logical_not(first_seg), ends, matching, found)

    if first:
        for index, ref in enumerate(messages):
            owner = sz.owner(block, index)
            rows = pl.ds(pl.multiple_of(owner * chunk, chunk), chunk)
            for t in range(hours):
                duals[t, rows, :] = ref[t * chunk : (t + 1) * chunk, :]
    else:
        dual_step = STEP_SCALE * old_weight
        dual_sq = jnp.zeros((SUBLANES, LANES), jnp.float32)
        for t in range(hours):
            totals = tree_sum([ref[t * segs : (t + 1) * segs, :] for ref in messages])
            change = dual_step * totals
            duals[t] = old_duals[t] - change
            dual_sq = dual_sq + folded(change * change)
        at = sz.sums + sz.end_packed
        write_squares([ref[at : at + SUBLANES, :] for ref in messages], dual_sq, scalars)
    for t in range(hours):
        onehot = contract_onehot(contract_map[t : t + 1, sz.own_pipes(block)], sz.classes)
        spread[t] = sz.share * exact_product(duals[t], onehot, NN)

    seg_message[...] = jnp.zeros(seg_message.shape, jnp.float32)
    write_edges(
        sz,
        seg_message,
        [lambda t, ref=ref: ref[t, 0:1, :] for ref in (mass, pack, momentum)],
        [lambda t, ref=ref: ref[t, last:segs, :] for ref in (mass, flow, momentum, cost)],
        friction[last:segs, :],
    )
    for t in range(hours):
        at = 6 * hours + t
        seg_message[at : at + 1, :] = spread[t, 0:1, :]
    seg_message[sz.matched : sz.matched + sz.end_rows, :] = found[...]
    if not first:
        seg_message[sz.seg_tail : sz.seg_tail + 1, : 2 * LANES] = scalars[0:1, :]
    seg_message[sz.seg_tail + 1 : sz.seg_tail + 2, :] = jnp.where(
        first_seg, earlier_in[2 * segs : 2 * segs + 1, :], later_in[0:1, :]
    )
    hour_message[0:segs, :] = duals[hours - 1]
    if sz.paired and not first:
        hour_message[segs:, :] = jnp.zeros((SUBLANES, sz.classes), jnp.float32)
        for part in (0, 1):
            at = segs + part
            hour_message[at : at + 1, :LANES] = scalars[0:1, part * LANES : (part + 1) * LANES]


def write_squares(squares, dual_sq, scalars):
    total = tree_sum(squares)
    scalars[...] = jnp.zeros(scalars.shape, jnp.float32)
    scalars[0:1, :LANES] = total[0:1]
    scalars[0:1, LANES:] = total[1:2] + jnp.sum(dual_sq, axis=0, keepdims=True)


def new_weight(weight, total):
    primal = jnp.sum(total[:, :LANES], axis=1, keepdims=True)
    dual = jnp.sum(total[:, LANES : 2 * LANES], axis=1, keepdims=True)
    return jnp.sqrt(weight * jnp.sqrt((dual + NORM_EPS) / (primal + NORM_EPS)))


def step(sz, block, hour, first_seg, weight, state, data, halo, spread_of, outs, message):
    flow, pack, mass, momentum = state
    cost, injection, resistance, contract_map, target = data
    flow_out, pack_out, mass_out, momentum_out = outs
    hours, segs, pipes = sz.hours, sz.segs, sz.pipes
    last, end = segs - 1, hours - 1
    has_earlier = hour > 0
    has_later = hour < sz.hour_parts - 1
    primal_step = STEP_SCALE / weight
    dual_step = STEP_SCALE * weight

    row_index = lax.broadcasted_iota(jnp.int32, (segs, pipes), 0)
    top, bottom = row_index == 0, row_index == last

    def from_above(values, row):
        return jnp.where(top, row, pltpu.roll(values, 1, 0))

    def from_below(values, row):
        return jnp.where(bottom, row, pltpu.roll(values, segs - 1, 0))

    def seg_row(slot, t):
        at = slot * hours + t
        return halo["seg"][at : at + 1, :]

    def matched_row(slot, t):
        at = sz.matched + slot * hours + t
        return halo["seg"][at : at + 1, :]

    def new_flow(start, gap):
        return jnp.clip(start - primal_step * gap, -FLOW_CAP, FLOW_CAP)

    def new_pack(start, gradient):
        return jnp.clip(start + primal_step * gradient, 0.0, PACK_CAP)

    corner = halo["corner"]
    earlier_pack = halo["earlier"][0:segs, :]
    earlier_gradient = (
        halo["earlier"][segs : 2 * segs, :]
        + halo["earlier_spread"]
        + jnp.where(top, jnp.where(first_seg, 0.0, corner), 0.0)
        - mass[0]
    )
    earlier_bar = jnp.where(
        has_earlier, 2.0 * new_pack(earlier_pack, earlier_gradient) - earlier_pack, 0.0
    )
    later_mass = jnp.where(has_later, halo["later"][0:segs, :], 0.0)
    later_corner = jnp.where(has_later, corner, 0.0)
    primal_sq = jnp.zeros((SUBLANES, LANES), jnp.float32)
    dual_sq = jnp.zeros((SUBLANES, LANES), jnp.float32)
    for t in range(hours):
        mass_now, momentum_now = mass[t], momentum[t]
        flow_now, pack_now = flow[t], pack[t]
        spread, edge_spread, onehot = spread_of(t)
        below_mass = jnp.where(first_seg, seg_row(0, t), matched_row(0, t))
        next_mass = mass[t + 1] if t < end else later_mass
        gap = cost[t] - (
            mass_now - from_below(mass_now, below_mass) + resistance * momentum_now
        )
        flow_next = new_flow(flow_now, gap)
        above_momentum = jnp.where(first_seg, 0.0, seg_row(3, t))
        gradient = (
            mass_now
            - next_mass
            - momentum_now
            + from_above(momentum_now, above_momentum)
            + spread
        )
        pack_next = new_pack(pack_now, gradient)
        flow_bar = 2.0 * flow_next - flow_now
        pack_bar = 2.0 * pack_next - pack_now

        edge_flow = jnp.where(first_seg, matched_row(0, t), seg_row(4, t))
        edge_gap = jnp.where(first_seg, matched_row(1, t), seg_row(5, t)) + mass_now[0:1, :]
        edge_flow_bar = 2.0 * new_flow(edge_flow, edge_gap) - edge_flow
        edge_pack = seg_row(1, t)
        edge_later = seg_row(0, t + 1) if t < end else later_corner
        edge_gradient = (
            seg_row(2, t) + edge_spread + momentum_now[last : last + 1, :] - edge_later
        )
        edge_pack_bar = jnp.where(
            first_seg, 2.0 * new_pack(edge_pack, edge_gradient) - edge_pack, 0.0
        )

        mass_rows = pack_bar - earlier_bar + flow_bar - from_above(flow_bar, edge_flow_bar)
        momentum_rows = resistance * flow_bar - (pack_bar - from_below(pack_bar, edge_pack_bar))
        mass_change = dual_step * (injection[t] - mass_rows)
        momentum_change = dual_step * momentum_rows
        flow_out[t] = flow_next
        pack_out[t] = pack_next
        mass_out[t] = mass_now + mass_change
        momentum_out[t] = momentum_now - momentum_change
        flow_change, pack_change = flow_next - flow_now, pack_next - pack_now
        primal_sq = primal_sq + folded(flow_change * flow_change + pack_change * pack_change)
        dual_sq = dual_sq + folded(
            mass_change * mass_change + momentum_change * momentum_change
        )
        message[t * segs : (t + 1) * segs, :] = sz.share * exact_product(pack_bar, onehot, NT)
        rows = pl.ds(pl.multiple_of(t * segs + block * sz.chunk, sz.chunk), sz.chunk)
        message[rows, :] = message[rows, :] - target[t]
        earlier_bar = pack_bar

    at = message.shape[0] - SUBLANES
    message[at:, :] = jnp.zeros((SUBLANES, LANES), jnp.float32)
    message[at : at + 1, :] = jnp.sum(primal_sq, axis=0, keepdims=True)
    message[at + 1 : at + 2, :] = jnp.sum(dual_sq, axis=0, keepdims=True)


def write_next(sz, hour, first_seg, outs, cost, resistance, message, hour_messages):
    flow, pack, mass, momentum = outs
    last = sz.segs - 1
    firsts = [mass[t, 0:1, :] for t in range(sz.hours)]
    lasts = [flow[t, last : last + 1, :] for t in range(sz.hours)]
    gaps = [
        cost[t, last : last + 1, :]
        - mass[t, last : last + 1, :]
        - resistance[last : last + 1, :] * momentum[t, last : last + 1, :]
        for t in range(sz.hours)
    ]
    rows = [jnp.where(first_seg, a, b) for a, b in zip(firsts + firsts, lasts + gaps)]
    write_ends(sz, message, sz.sums, rows)
    end = sz.hours - 1
    write_layers(sz, hour_messages, hour == 0, pack[end], mass[end], momentum[end], mass[0])


def step_kernel(sz, iteration, final, *refs):
    take = taker(refs)
    first = iteration == 0
    state, data = take(4), take(2)
    friction, contract_map, target, spread = take(4)
    seg_in, hours_in, duals_in, map_in = take(1)[0], take(1 if sz.paired else 2), *take(2)
    old_weight = take(1)[0][0:1, 0:1] if iteration > 1 else 1.0
    scalars = [] if first else take(2 if sz.paired else 1)
    outs, message = take(4), take(1)[0]
    weight_out = [] if first else take(1)
    hour_messages = [] if final else take(1 if sz.paired else 2)
    block, hour, first_seg = places()
    hours, segs = sz.hours, sz.segs
    weight = jnp.ones((1, 1), jnp.float32)
    if not first:
        total = scalars[0][0:1, :]
        if sz.paired:
            parts = [duals_in[segs + part : segs + part + 1, :LANES] for part in (0, 1)]
            total = tree_sum(
                [
                    total,
                    seg_in[sz.seg_tail : sz.seg_tail + 1, : 2 * LANES],
                    jnp.concatenate(parts, axis=1),
                    scalars[1][0:1, :],
                ]
            )
        weight = new_weight(old_weight, total)
        weight_out[0][...] = jnp.broadcast_to(weight, weight_out[0].shape)
    map_row = map_in[2 * segs + 1 : 2 * segs + 2, :].astype(jnp.int32)
    earlier_spread = sz.share * exact_product(
        duals_in[0:segs, :], contract_onehot(map_row, sz.classes), NN
    )

    def spread_of(t):
        onehot = contract_onehot(contract_map[t : t + 1, sz.own_pipes(block)], sz.classes)
        at = 6 * hours + t
        return spread[t], seg_in[at : at + 1, :], onehot

    halo = {
        "seg": seg_in,
        "corner": seg_in[sz.seg_tail + 1 : sz.seg_tail + 2, :],
        "earlier": hours_in[0],
        "earlier_spread": earlier_spread,
        "later": hours_in[-1],
    }
    resistance = friction[...]
    data = [*data, resistance, contract_map, target]
    step(sz, block, hour, first_seg, weight, state, data, halo, spread_of, outs, message)
    if not final:
        write_next(sz, hour, first_seg, outs, data[0], resistance, message, hour_messages)


def close_kernel(sz, *refs):
    take = taker(refs)
    messages = take_messages(sz, take)
    old_duals, weight, written, duals, scalars = take(5)
    block, hour, first_seg = places()
    segs = sz.segs
    dual_step = STEP_SCALE * weight[0:1, 0:1]
    dual_sq = jnp.zeros((SUBLANES, LANES), jnp.float32)
    start = block * sz.chunk
    for t in range(sz.hours):
        totals = tree_sum([ref[t * segs : (t + 1) * segs, :] for ref in messages])
        change = dual_step * totals
        dual_sq = dual_sq + folded(change * change)
        own = pl.ds(pl.multiple_of(start, sz.chunk), sz.chunk)
        rows = pl.ds(pl.multiple_of(t * segs + start, sz.chunk), sz.chunk)
        own_totals = tree_sum([ref[rows, :] for ref in messages])
        duals[t] = old_duals[t, own, :] - dual_step * own_totals
    squares = [ref[sz.sums : sz.sums + SUBLANES, :] for ref in messages]
    write_squares(squares, dual_sq, scalars)


def written_out(state):
    count = len(state)

    def body(*refs):
        sources, targets, token, done = refs[:count], refs[count:-2], refs[-2], refs[-1]
        copies = [
            pltpu.make_async_copy(source, target, done.at[index])
            for index, (source, target) in enumerate(zip(sources, targets))
        ]
        for copy in copies:
            copy.start()
        token[...] = jnp.zeros(token.shape, jnp.float32)
        for copy in copies:
            copy.wait()

    return pl.pallas_call(
        body,
        out_shape=[pltpu.HBM(array.shape, array.dtype) for array in state]
        + [pltpu.VMEM((SUBLANES, LANES), jnp.float32)],
        in_specs=[pl.BlockSpec(memory_space=pltpu.VMEM) for _ in state],
        out_specs=[pl.BlockSpec(memory_space=pltpu.HBM) for _ in state]
        + [pl.BlockSpec(memory_space=pltpu.VMEM)],
        scratch_shapes=[pltpu.SemaphoreType.DMA((count,))],
        compiler_params=pltpu.CompilerParams(vmem_limit_bytes=VMEM_LIMIT),
    )(*state)


def weight_kernel(weight, *refs):
    *scalars, result = refs
    result[...] = new_weight(weight[0:1, 0:1], tree_sum([ref[0:1, :] for ref in scalars]))


def gathered(sz, message):
    return [message] + [swapped(message, "pipe", k) for k in sz.pipe_order]


def layers_exchanged(sz, hour_messages):
    if sz.paired:
        return [swapped(hour_messages[0], "hour", 1)]
    steps = range(sz.hour_parts - 1)
    return [
        lax.ppermute(hour_messages[0], "hour", [(i, i + 1) for i in steps]),
        lax.ppermute(hour_messages[1], "hour", [(i + 1, i) for i in steps]),
    ]


def on_device(
    segment_flow,
    linepack,
    mass_dual,
    momentum_dual,
    contract_dual,
    flow_cost,
    injection,
    contract_target,
    friction_table,
    friction_class,
    matching,
    contract_map,
):
    hours, segs, pipes = segment_flow.shape
    chunk, classes = contract_dual.shape[2:]
    sz = Sizes(hours, segs, pipes, chunk, classes, friction_table.shape[0])
    duals_now = contract_dual.reshape(hours, chunk, classes)
    target_now = contract_target.reshape(hours, chunk, classes)
    matching = matching.reshape(1, matching.shape[0])
    cells, contracts = (hours, segs, pipes), (hours, segs, classes)
    layer_shapes = [(2 * segs + SUBLANES, pipes)]
    if not sz.paired:
        layer_shapes.append((segs, pipes))
    scalars_shape = (SUBLANES, 2 * LANES)

    state = [segment_flow, linepack, mass_dual, momentum_dual]
    raw = [*state, flow_cost, friction_class, duals_now, contract_map, friction_table, matching]
    message, friction, matching, *hour_messages = local_call(
        functools.partial(start_kernel, sz),
        [(sz.first_ends + sz.end_packed, classes), (segs, pipes), matching.shape, *layer_shapes],
        [("hbm", array) for array in raw],
        kept=True,
        scratch=start_scratch(sz),
        kinds={2: jnp.int32},
    )
    duals, weight, map_in = [], [], None
    for iteration in range(ITERS):
        first, final = iteration == 0, iteration == ITERS - 1
        messages = gathered(sz, message)
        hours_in = layers_exchanged(sz, hour_messages)
        map_in = hours_in[0] if first else map_in
        args = vmem(*state, flow_cost, friction, contract_map, matching)
        args += vmem(*messages, *hours_in, *duals, *weight)
        duals_rows = segs + (SUBLANES if sz.paired and not first else 0)
        outs = [(sz.seg_tail + SUBLANES, pipes), (duals_rows, classes), contracts, cells]
        seg_message, duals_message, full_duals, spread, *scalars = local_call(
            functools.partial(spread_kernel, sz, iteration),
            outs + ([] if first else [scalars_shape]),
            args,
            kept=True,
            scratch=[pltpu.VMEM((sz.end_rows, pipes), jnp.float32)],
        )
        duals = [full_duals]
        seg_in = swapped(seg_message, "seg", 1)
        if sz.paired:
            duals_in = swapped(duals_message, "hour", 1)
            scalars += [swapped(part, ("hour", "seg"), 3) for part in scalars]
        else:
            steps = range(sz.hour_parts - 1)
            duals_in = lax.ppermute(duals_message, "hour", [(i, i + 1) for i in steps])
            scalars = [lax.psum(part, ("hour", "seg")) for part in scalars]
        args = vmem(*state, flow_cost, injection, friction, contract_map, target_now, spread)
        args += vmem(seg_in, *hours_in, duals_in, map_in, *weight, *scalars)
        message_rows = sz.sums + SUBLANES + (0 if final else sz.end_packed)
        outs = [cells] * 4 + [(message_rows, classes)]
        outs += [] if first else [(SUBLANES, LANES)]
        results = local_call(
            functools.partial(step_kernel, sz, iteration, final),
            outs + ([] if final else layer_shapes),
            args,
            kept=True,
        )
        state, message, rest = results[:4], results[4], results[5:]
        weight, hour_messages = ([], rest) if first else (rest[:1], rest[1:])
    *state, written = written_out(state)
    contract_out, scalars = local_call(
        functools.partial(close_kernel, sz),
        [(hours, chunk, classes), scalars_shape],
        vmem(*gathered(sz, message), *duals, *weight, written),
        kept=True,
    )
    if sz.paired:
        sums = [scalars] + [swapped(scalars, ("hour", "seg"), k) for k in (1, 2, 3)]
    else:
        sums = [lax.psum(scalars, ("hour", "seg"))]
    (weight,) = local_call(weight_kernel, [(1, 1)], vmem(*weight, *sums))
    return (
        *state,
        contract_out.reshape(contract_dual.shape),
        weight.reshape(1),
    )


def solution(mesh):
    cells = P(("groups", "hour"), "seg", "pipe")
    contracts = P(("groups", "hour"), "seg", "pipe", None)
    return jax.shard_map(
        on_device,
        mesh=mesh,
        in_specs=(
            cells,
            cells,
            cells,
            cells,
            contracts,
            cells,
            cells,
            contracts,
            P(),
            P("seg", ("groups", "pipe")),
            P("groups"),
            P(("groups", "hour"), None),
        ),
        out_specs=(cells, cells, cells, cells, contracts, P("groups")),
        check_vma=False,
    )
```

```python
import functools

import jax
import jax.numpy as jnp
from jax import lax
from jax.experimental import pallas as pl
from jax.experimental.pallas import tpu as pltpu
from jax.sharding import PartitionSpec as P

ITERS = 2

FLOW_CAP = 1.5
PACK_CAP = 2.5
STEP_SCALE = 0.25
NORM_EPS = 1e-06

LANES = 128
SUBLANES = 8
VMEM_LIMIT = 8 * 1024 * 1024
PIPE_ORDERS = ((1, 3, 2), (1, 3, 2), (3, 1, 2))
NT = (((1,), (1,)), ((), ()))
NN = (((1,), (0,)), ((), ()))


def rounded_up(count):
    return -(-count // SUBLANES) * SUBLANES


def local_call(body, outs, args, kept=False, scratch=(), kinds={}):
    spaces = {"smem": pltpu.SMEM, "vmem": pltpu.VMEM, "hbm": pltpu.HBM}
    shape_of = pltpu.VMEM if kept else jax.ShapeDtypeStruct
    arrays = [
        pltpu.with_memory_space_constraint(array, pltpu.HBM) if space == "hbm" else array
        for space, array in args
    ]
    results = pl.pallas_call(
        body,
        out_shape=[shape_of(shape, kinds.get(index, jnp.float32)) for index, shape in enumerate(outs)],
        in_specs=[pl.BlockSpec(memory_space=spaces[space]) for space, _ in args],
        out_specs=[pl.BlockSpec(memory_space=pltpu.VMEM) for _ in outs],
        scratch_shapes=scratch,
        compiler_params=pltpu.CompilerParams(vmem_limit_bytes=VMEM_LIMIT),
    )(*arrays)
    return list(results)


def vmem(*arrays):
    return [("vmem", array) for array in arrays]


def taker(refs):
    refs = list(refs)

    def take(count):
        return [refs.pop(0) for _ in range(count)]

    return take


def parts_of(values):
    high = values.astype(jnp.bfloat16).astype(jnp.float32)
    rest = values - high
    middle = rest.astype(jnp.bfloat16).astype(jnp.float32)
    return jnp.concatenate([high, middle, rest - middle], axis=0).astype(jnp.bfloat16)


def exact_product(values, onehot, dims):
    rows = values.shape[0]
    product = lax.dot_general(
        parts_of(values), onehot, dims, preferred_element_type=jnp.float32
    )
    return product[:rows] + product[rows : 2 * rows] + product[2 * rows :]


def as_onehot(mask):
    return jnp.where(mask, 1.0, 0.0).astype(jnp.bfloat16)


def contract_onehot(map_row, class_count):
    shape = (class_count, map_row.shape[1])
    return as_onehot(lax.broadcasted_iota(jnp.int32, shape, 0) == map_row)


def friction_of(classes, table_ref, levels):
    friction = jnp.zeros(classes.shape, jnp.float32)
    for level in range(levels):
        friction = jnp.where(classes == level, table_ref[level], friction)
    return friction


def folded(values):
    rows, width = values.shape
    total = values[:SUBLANES]
    for start in range(SUBLANES, rows, SUBLANES):
        total = total + values[start : start + SUBLANES]
    result = total[:, :LANES]
    for start in range(LANES, width, LANES):
        result = result + total[:, start : start + LANES]
    return result


def tree_sum(terms):
    while len(terms) > 1:
        terms = [a + b for a, b in zip(terms[0::2], terms[1::2])]
    return terms[0]


def swapped(message, axes, distance):
    count = lax.axis_size(axes)
    return lax.ppermute(message, axes, [(i, i ^ distance) for i in range(count)])


class Sizes:
    def __init__(self, hours, segs, pipes, chunk, classes, levels):
        self.hours, self.segs, self.pipes = hours, segs, pipes
        self.chunk, self.classes, self.levels = chunk, classes, levels
        self.blocks = lax.axis_size("pipe")
        self.hour_parts = lax.axis_size("hour")
        self.share = classes / (pipes * self.blocks)
        self.halves = pipes // LANES
        self.paired = self.hour_parts == 2
        self.end_rows = {True: 2 * hours, False: hours}
        self.sums = hours * segs
        self.first_ends = rounded_up(hours * chunk)
        self.matched = 7 * hours
        self.seg_tail = rounded_up(9 * hours)

    def owner(self, block, index):
        return lax.bitwise_xor(block, index)

    def pipe_order(self, phase):
        return PIPE_ORDERS[phase] if self.blocks == 4 else range(1, self.blocks)

    def ends_packed(self, first):
        return rounded_up(self.end_rows[first] * self.halves)

    def own_pipes(self, block):
        return pl.ds(pl.multiple_of(block * self.pipes, LANES), self.pipes)


def take_messages(sz, phase, take):
    own, *received = take(sz.blocks)
    by_distance = dict(zip(sz.pipe_order(phase), received))
    return [own] + [by_distance[distance] for distance in range(1, sz.blocks)]


def places():
    return lax.axis_index("pipe"), lax.axis_index("hour"), lax.axis_index("seg") == 0


def write_ends(sz, message, start, rows):
    for index, row in enumerate(rows):
        for half in range(sz.halves):
            at = start + half * len(rows) + index
            message[at : at + 1, :] = row[:, half * LANES : (half + 1) * LANES]


def read_ends(sz, message, start, count):
    pieces = [
        message[start + half * count : start + (half + 1) * count, :]
        for half in range(sz.halves)
    ]
    return jnp.concatenate(pieces, axis=1)


def write_edges(sz, message, first_rows, last_rows, resistance):
    for t in range(sz.hours):
        mass, pack, momentum = [ref(t) for ref in first_rows]
        last_mass, flow, last_momentum, cost = [ref(t) for ref in last_rows]
        gap = cost - last_mass - resistance * last_momentum
        rows = [mass, pack, mass - momentum, last_momentum, flow, gap]
        for slot, row in enumerate(rows):
            at = slot * sz.hours + t
            message[at : at + 1, :] = row


def write_layers(sz, outs, first_hour, pack, mass, momentum, first_mass):
    segs = sz.segs
    top = lax.broadcasted_iota(jnp.int32, (segs, sz.pipes), 0) == 0
    gradient = mass - momentum + jnp.where(top, 0.0, pltpu.roll(momentum, 1, 0))
    if sz.paired:
        outs[0][0:segs, :] = jnp.where(first_hour, gradient, first_mass)
    else:
        outs[0][0:segs, :] = gradient
        outs[1][...] = first_mass
    if pack is not None:
        outs[0][segs : 2 * segs, :] = pack
    tail = outs[0].shape[0] - SUBLANES
    outs[0][tail:, :] = jnp.zeros((SUBLANES, sz.pipes), jnp.float32)
    outs[0][tail : tail + 1, :] = momentum[segs - 1 : segs, :]


def matched_rows(sz, block, inlet_side, ends, matching, found):
    shape = (sz.pipes, sz.pipes)
    row = lax.broadcasted_iota(jnp.int32, shape, 0)
    total = jnp.zeros(found.shape, jnp.float32)

    @pl.when(inlet_side)
    def _():
        own = matching[0:1, sz.own_pipes(block)]
        result = total
        for index, values in enumerate(ends):
            there = row + sz.owner(block, index) * sz.pipes
            result = result + exact_product(values, as_onehot(there == own), NN)
        found[...] = result

    @pl.when(jnp.logical_not(inlet_side))
    def _():
        here = row + block * sz.pipes
        result = total
        for index, values in enumerate(ends):
            feeds = matching[0:1, sz.own_pipes(sz.owner(block, index))]
            result = result + exact_product(values, as_onehot(here == feeds), NT)
        found[...] = result


def start_kernel(sz, *refs):
    take = taker(refs)
    flow, pack, mass, momentum, cost, classes_in, duals_in, contract_map, table_in = take(9)
    matching_in = take(1)[0]
    message, friction, matching, *hour_messages = take(3 + (1 if sz.paired else 2))
    flow_last, cost_last, mass_last, momentum_last, mass_first = take(5)
    pack_layer, mass_layer, momentum_layer, mass_start = take(4)
    duals, map_own, classes, table, arrived = take(5)
    block, hour, first_seg = places()
    hours, segs = sz.hours, sz.segs
    low, high = pl.ds(0, SUBLANES), pl.ds(segs - SUBLANES, SUBLANES)
    copies = [
        (flow.at[:, high], flow_last),
        (cost.at[:, high], cost_last),
        (mass.at[:, high], mass_last),
        (momentum.at[:, high], momentum_last),
        (mass.at[:, low], mass_first),
        (pack.at[hours - 1], pack_layer),
        (mass.at[hours - 1], mass_layer),
        (momentum.at[hours - 1], momentum_layer),
        (mass.at[0], mass_start),
        (duals_in, duals),
        (contract_map.at[:, sz.own_pipes(block)], map_own),
        (classes_in, classes),
        (table_in, table),
        (matching_in, matching),
    ]
    copies = [
        pltpu.make_async_copy(source, target, arrived.at[index])
        for index, (source, target) in enumerate(copies)
    ]
    for copy in copies:
        copy.start()
    for copy in copies:
        copy.wait()
    friction[...] = friction_of(classes[...], table, sz.levels)
    end = SUBLANES - 1
    firsts = [mass_first[t, 0:1, :] for t in range(hours)]
    lasts = [flow_last[t, end : end + 1, :] for t in range(hours)]
    gaps = [
        cost_last[t, end : end + 1, :]
        - mass_last[t, end : end + 1, :]
        - friction[segs - 1 : segs, :] * momentum_last[t, end : end + 1, :]
        for t in range(hours)
    ]
    for t in range(hours):
        message[t * sz.chunk : (t + 1) * sz.chunk, :] = duals[t]
    rows = [jnp.where(first_seg, a, b) for a, b in zip(firsts + firsts, gaps + lasts)]
    write_ends(sz, message, sz.first_ends, rows)
    write_layers(
        sz,
        hour_messages,
        hour == 0,
        pack_layer[...],
        mass_layer[...],
        momentum_layer[...],
        mass_start[...],
    )
    map_row = map_own[hours - 1 : hours, :].astype(jnp.float32)
    tail = hour_messages[0].shape[0] - SUBLANES
    hour_messages[0][tail + 1 : tail + 2, :] = map_row


def start_scratch(sz):
    ends = pltpu.VMEM((sz.hours, SUBLANES, sz.pipes), jnp.float32)
    layer = pltpu.VMEM((sz.segs, sz.pipes), jnp.float32)
    return (
        [ends] * 5
        + [layer] * 4
        + [
            pltpu.VMEM((sz.hours, sz.chunk, sz.classes), jnp.float32),
            pltpu.VMEM((sz.hours, sz.pipes), jnp.int32),
            pltpu.VMEM((sz.segs, sz.pipes), jnp.int32),
            pltpu.SMEM((sz.levels,), jnp.float32),
            pltpu.SemaphoreType.DMA((14,)),
        ]
    )


def spread_kernel(sz, iteration, *refs):
    take = taker(refs)
    first = iteration == 0
    flow, pack, mass, momentum, cost, friction, contract_map, matching = take(8)
    messages = take_messages(sz, iteration, take)
    hours_in = take(1 if sz.paired else 2)
    old_duals = None if first else take(1)[0]
    old_weight = take(1)[0][0:1, 0:1] if iteration > 1 else 1.0
    seg_message, hour_message, duals, spread = take(4)
    scalars = None if first else take(1)[0]
    found = take(1)[0]
    earlier_in, later_in = hours_in[0], hours_in[-1]
    block, hour, first_seg = places()
    hours, segs, pipes, chunk = sz.hours, sz.segs, sz.pipes, sz.chunk
    last = segs - 1

    ends_at, count = sz.first_ends if first else sz.sums, sz.end_rows[first]
    ends = [read_ends(sz, ref, ends_at, count) for ref in messages]
    matched_rows(sz, block, jnp.logical_not(first_seg), ends, matching, found)

    if first:
        for index, ref in enumerate(messages):
            owner = sz.owner(block, index)
            rows = pl.ds(pl.multiple_of(owner * chunk, chunk), chunk)
            for t in range(hours):
                duals[t, rows, :] = ref[t * chunk : (t + 1) * chunk, :]
    else:
        dual_step = STEP_SCALE * old_weight
        dual_sq = jnp.zeros((SUBLANES, LANES), jnp.float32)
        for t in range(hours):
            totals = tree_sum([ref[t * segs : (t + 1) * segs, :] for ref in messages])
            change = dual_step * totals
            duals[t] = old_duals[t] - change
            dual_sq = dual_sq + folded(change * change)
        at = sz.sums + sz.ends_packed(False)
        write_squares([ref[at : at + SUBLANES, :] for ref in messages], dual_sq, scalars)
    for t in range(hours):
        onehot = contract_onehot(contract_map[t : t + 1, sz.own_pipes(block)], sz.classes)
        spread[t] = sz.share * exact_product(duals[t], onehot, NN)

    seg_message[...] = jnp.zeros(seg_message.shape, jnp.float32)
    write_edges(
        sz,
        seg_message,
        [lambda t, ref=ref: ref[t, 0:1, :] for ref in (mass, pack, momentum)],
        [lambda t, ref=ref: ref[t, last:segs, :] for ref in (mass, flow, momentum, cost)],
        friction[last:segs, :],
    )
    for t in range(hours):
        at = 6 * hours + t
        seg_message[at : at + 1, :] = spread[t, 0:1, :]
    seg_message[sz.matched : sz.matched + count, :] = found[...]
    tail = earlier_in.shape[0] - SUBLANES
    if not first:
        seg_message[sz.seg_tail : sz.seg_tail + 1, : 2 * LANES] = scalars[0:1, :]
    seg_message[sz.seg_tail + 1 : sz.seg_tail + 2, :] = jnp.where(
        first_seg, earlier_in[tail : tail + 1, :], later_in[0:1, :]
    )
    hour_message[0:segs, :] = duals[hours - 1]
    if sz.paired and not first:
        hour_message[segs:, :] = jnp.zeros((SUBLANES, sz.classes), jnp.float32)
        for part in (0, 1):
            at = segs + part
            hour_message[at : at + 1, :LANES] = scalars[0:1, part * LANES : (part + 1) * LANES]


def write_squares(squares, dual_sq, scalars):
    total = tree_sum(squares)
    scalars[...] = jnp.zeros(scalars.shape, jnp.float32)
    scalars[0:1, :LANES] = total[0:1]
    scalars[0:1, LANES:] = total[1:2] + jnp.sum(dual_sq, axis=0, keepdims=True)


def new_weight(weight, total):
    primal = jnp.sum(total[:, :LANES], axis=1, keepdims=True)
    dual = jnp.sum(total[:, LANES : 2 * LANES], axis=1, keepdims=True)
    return jnp.sqrt(weight * jnp.sqrt((dual + NORM_EPS) / (primal + NORM_EPS)))


def step(sz, block, hour, first_seg, weight, state, data, halo, spread_of, outs, message, kept):
    flow, pack, mass, momentum = state
    cost, injection, resistance, contract_map, target = data
    flow_out, pack_out, mass_out, momentum_out = outs
    edge_flow_out, earlier_pack_out = kept
    hours, segs, pipes = sz.hours, sz.segs, sz.pipes
    last, end = segs - 1, hours - 1
    has_earlier = hour > 0
    has_later = hour < sz.hour_parts - 1
    primal_step = STEP_SCALE / weight
    dual_step = STEP_SCALE * weight

    row_index = lax.broadcasted_iota(jnp.int32, (segs, pipes), 0)
    top, bottom = row_index == 0, row_index == last

    def from_above(values, row):
        return jnp.where(top, row, pltpu.roll(values, 1, 0))

    def from_below(values, row):
        return jnp.where(bottom, row, pltpu.roll(values, segs - 1, 0))

    def seg_row(slot, t):
        at = slot * hours + t
        return halo["seg"][at : at + 1, :]

    def matched_row(slot, t):
        at = sz.matched + slot * hours + t
        return halo["seg"][at : at + 1, :]

    def new_flow(start, gap):
        return jnp.clip(start - primal_step * gap, -FLOW_CAP, FLOW_CAP)

    def new_pack(start, gradient):
        return jnp.clip(start + primal_step * gradient, 0.0, PACK_CAP)

    corner = halo["corner"]
    earlier_pack = halo["earlier_pack"]
    earlier_gradient = (
        halo["earlier"][0:segs, :]
        + halo["earlier_spread"]
        + jnp.where(top, jnp.where(first_seg, 0.0, corner), 0.0)
        - mass[0]
    )
    earlier_next = new_pack(earlier_pack, earlier_gradient)
    earlier_bar = jnp.where(has_earlier, 2.0 * earlier_next - earlier_pack, 0.0)
    if earlier_pack_out is not None:
        earlier_pack_out[...] = earlier_next
    later_mass = jnp.where(has_later, halo["later"][0:segs, :], 0.0)
    later_corner = jnp.where(has_later, corner, 0.0)
    primal_sq = jnp.zeros((SUBLANES, LANES), jnp.float32)
    dual_sq = jnp.zeros((SUBLANES, LANES), jnp.float32)
    for t in range(hours):
        mass_now, momentum_now = mass[t], momentum[t]
        flow_now, pack_now = flow[t], pack[t]
        spread, edge_spread, onehot = spread_of(t)
        below_mass = jnp.where(first_seg, seg_row(0, t), matched_row(0, t))
        next_mass = mass[t + 1] if t < end else later_mass
        gap = cost[t] - (
            mass_now - from_below(mass_now, below_mass) + resistance * momentum_now
        )
        flow_next = new_flow(flow_now, gap)
        above_momentum = jnp.where(first_seg, 0.0, seg_row(3, t))
        gradient = (
            mass_now
            - next_mass
            - momentum_now
            + from_above(momentum_now, above_momentum)
            + spread
        )
        pack_next = new_pack(pack_now, gradient)
        flow_bar = 2.0 * flow_next - flow_now
        pack_bar = 2.0 * pack_next - pack_now

        edge_flow = jnp.where(first_seg, halo["matched_flow"](t), seg_row(4, t))
        edge_gap = jnp.where(first_seg, matched_row(0, t), seg_row(5, t)) + mass_now[0:1, :]
        edge_flow_next = new_flow(edge_flow, edge_gap)
        edge_flow_bar = 2.0 * edge_flow_next - edge_flow
        if edge_flow_out is not None:
            edge_flow_out[t : t + 1, :] = edge_flow_next
        edge_pack = seg_row(1, t)
        edge_later = seg_row(0, t + 1) if t < end else later_corner
        edge_gradient = (
            seg_row(2, t) + edge_spread + momentum_now[last : last + 1, :] - edge_later
        )
        edge_pack_bar = jnp.where(
            first_seg, 2.0 * new_pack(edge_pack, edge_gradient) - edge_pack, 0.0
        )

        mass_rows = pack_bar - earlier_bar + flow_bar - from_above(flow_bar, edge_flow_bar)
        momentum_rows = resistance * flow_bar - (pack_bar - from_below(pack_bar, edge_pack_bar))
        mass_change = dual_step * (injection[t] - mass_rows)
        momentum_change = dual_step * momentum_rows
        flow_out[t] = flow_next
        pack_out[t] = pack_next
        mass_out[t] = mass_now + mass_change
        momentum_out[t] = momentum_now - momentum_change
        flow_change, pack_change = flow_next - flow_now, pack_next - pack_now
        primal_sq = primal_sq + folded(flow_change * flow_change + pack_change * pack_change)
        dual_sq = dual_sq + folded(
            mass_change * mass_change + momentum_change * momentum_change
        )
        message[t * segs : (t + 1) * segs, :] = sz.share * exact_product(pack_bar, onehot, NT)
        rows = pl.ds(pl.multiple_of(t * segs + block * sz.chunk, sz.chunk), sz.chunk)
        message[rows, :] = message[rows, :] - target[t]
        earlier_bar = pack_bar

    at = message.shape[0] - SUBLANES
    message[at:, :] = jnp.zeros((SUBLANES, LANES), jnp.float32)
    message[at : at + 1, :] = jnp.sum(primal_sq, axis=0, keepdims=True)
    message[at + 1 : at + 2, :] = jnp.sum(dual_sq, axis=0, keepdims=True)


def write_next(sz, hour, first_seg, outs, cost, resistance, message, hour_messages):
    flow, pack, mass, momentum = outs
    last = sz.segs - 1
    firsts = [mass[t, 0:1, :] for t in range(sz.hours)]
    gaps = [
        cost[t, last : last + 1, :]
        - mass[t, last : last + 1, :]
        - resistance[last : last + 1, :] * momentum[t, last : last + 1, :]
        for t in range(sz.hours)
    ]
    rows = [jnp.where(first_seg, a, b) for a, b in zip(firsts, gaps)]
    write_ends(sz, message, sz.sums, rows)
    end = sz.hours - 1
    write_layers(sz, hour_messages, hour == 0, None, mass[end], momentum[end], mass[0])


def step_kernel(sz, iteration, final, *refs):
    take = taker(refs)
    first = iteration == 0
    state, data = take(4), take(2)
    friction, contract_map, target, spread = take(4)
    seg_in, hours_in, duals_in, map_in = take(1)[0], take(1 if sz.paired else 2), *take(2)
    known = [] if first else take(2)
    old_weight = take(1)[0][0:1, 0:1] if iteration > 1 else 1.0
    scalars = [] if first else take(2 if sz.paired else 1)
    outs, message = take(4), take(1)[0]
    weight_out = [] if first else take(1)
    kept = [None, None] if final else take(2)
    hour_messages = [] if final else take(1 if sz.paired else 2)
    block, hour, first_seg = places()
    hours, segs = sz.hours, sz.segs
    weight = jnp.ones((1, 1), jnp.float32)
    if not first:
        total = scalars[0][0:1, :]
        if sz.paired:
            parts = [duals_in[segs + part : segs + part + 1, :LANES] for part in (0, 1)]
            total = tree_sum(
                [
                    total,
                    seg_in[sz.seg_tail : sz.seg_tail + 1, : 2 * LANES],
                    jnp.concatenate(parts, axis=1),
                    scalars[1][0:1, :],
                ]
            )
        weight = new_weight(old_weight, total)
        weight_out[0][...] = jnp.broadcast_to(weight, weight_out[0].shape)
    tail = map_in.shape[0] - SUBLANES
    map_row = map_in[tail + 1 : tail + 2, :].astype(jnp.int32)
    earlier_spread = sz.share * exact_product(
        duals_in[0:segs, :], contract_onehot(map_row, sz.classes), NN
    )

    def spread_of(t):
        onehot = contract_onehot(contract_map[t : t + 1, sz.own_pipes(block)], sz.classes)
        at = 6 * hours + t
        return spread[t], seg_in[at : at + 1, :], onehot

    def matched_flow(t):
        at = sz.matched + hours + t
        return seg_in[at : at + 1, :] if first else known[0][t : t + 1, :]

    halo = {
        "seg": seg_in,
        "corner": seg_in[sz.seg_tail + 1 : sz.seg_tail + 2, :],
        "earlier": hours_in[0],
        "earlier_pack": hours_in[0][segs : 2 * segs, :] if first else known[1][...],
        "matched_flow": matched_flow,
        "earlier_spread": earlier_spread,
        "later": hours_in[-1],
    }
    resistance = friction[...]
    data = [*data, resistance, contract_map, target]
    step(sz, block, hour, first_seg, weight, state, data, halo, spread_of, outs, message, kept)
    if not final:
        write_next(sz, hour, first_seg, outs, data[0], resistance, message, hour_messages)


def close_kernel(sz, *refs):
    take = taker(refs)
    messages = take_messages(sz, ITERS, take)
    old_duals, weight, written, duals, scalars = take(5)
    block, hour, first_seg = places()
    segs = sz.segs
    dual_step = STEP_SCALE * weight[0:1, 0:1]
    dual_sq = jnp.zeros((SUBLANES, LANES), jnp.float32)
    start = block * sz.chunk
    for t in range(sz.hours):
        totals = tree_sum([ref[t * segs : (t + 1) * segs, :] for ref in messages])
        change = dual_step * totals
        dual_sq = dual_sq + folded(change * change)
        own = pl.ds(pl.multiple_of(start, sz.chunk), sz.chunk)
        rows = pl.ds(pl.multiple_of(t * segs + start, sz.chunk), sz.chunk)
        own_totals = tree_sum([ref[rows, :] for ref in messages])
        duals[t] = old_duals[t, own, :] - dual_step * own_totals
    squares = [ref[sz.sums : sz.sums + SUBLANES, :] for ref in messages]
    write_squares(squares, dual_sq, scalars)


def written_out(state):
    count = len(state)

    def body(*refs):
        sources, targets, token, done = refs[:count], refs[count:-2], refs[-2], refs[-1]
        copies = [
            pltpu.make_async_copy(source, target, done.at[index])
            for index, (source, target) in enumerate(zip(sources, targets))
        ]
        for copy in copies:
            copy.start()
        token[...] = jnp.zeros(token.shape, jnp.float32)
        for copy in copies:
            copy.wait()

    return pl.pallas_call(
        body,
        out_shape=[pltpu.HBM(array.shape, array.dtype) for array in state]
        + [pltpu.VMEM((SUBLANES, LANES), jnp.float32)],
        in_specs=[pl.BlockSpec(memory_space=pltpu.VMEM) for _ in state],
        out_specs=[pl.BlockSpec(memory_space=pltpu.HBM) for _ in state]
        + [pl.BlockSpec(memory_space=pltpu.VMEM)],
        scratch_shapes=[pltpu.SemaphoreType.DMA((count,))],
        compiler_params=pltpu.CompilerParams(vmem_limit_bytes=VMEM_LIMIT),
    )(*state)


def weight_kernel(weight, *refs):
    *scalars, result = refs
    result[...] = new_weight(weight[0:1, 0:1], tree_sum([ref[0:1, :] for ref in scalars]))


def gathered(sz, phase, message):
    return [message] + [swapped(message, "pipe", k) for k in sz.pipe_order(phase)]


def layers_exchanged(sz, hour_messages):
    if sz.paired:
        return [swapped(hour_messages[0], "hour", 1)]
    steps = range(sz.hour_parts - 1)
    return [
        lax.ppermute(hour_messages[0], "hour", [(i, i + 1) for i in steps]),
        lax.ppermute(hour_messages[1], "hour", [(i + 1, i) for i in steps]),
    ]


def on_device(
    segment_flow,
    linepack,
    mass_dual,
    momentum_dual,
    contract_dual,
    flow_cost,
    injection,
    contract_target,
    friction_table,
    friction_class,
    matching,
    contract_map,
):
    hours, segs, pipes = segment_flow.shape
    chunk, classes = contract_dual.shape[2:]
    sz = Sizes(hours, segs, pipes, chunk, classes, friction_table.shape[0])
    duals_now = contract_dual.reshape(hours, chunk, classes)
    target_now = contract_target.reshape(hours, chunk, classes)
    matching = matching.reshape(1, matching.shape[0])
    cells, contracts = (hours, segs, pipes), (hours, segs, classes)
    layer_shapes = [(segs + SUBLANES, pipes)]
    if not sz.paired:
        layer_shapes.append((segs, pipes))
    known_shapes = [(rounded_up(hours), pipes), (segs, pipes)]
    scalars_shape = (SUBLANES, 2 * LANES)

    state = [segment_flow, linepack, mass_dual, momentum_dual]
    raw = [*state, flow_cost, friction_class, duals_now, contract_map, friction_table, matching]
    message, friction, matching, *hour_messages = local_call(
        functools.partial(start_kernel, sz),
        [
            (sz.first_ends + sz.ends_packed(True), classes),
            (segs, pipes),
            matching.shape,
            (2 * segs + SUBLANES, pipes),
            *layer_shapes[1:],
        ],
        [("hbm", array) for array in raw],
        kept=True,
        scratch=start_scratch(sz),
        kinds={2: jnp.int32},
    )
    duals, weight, known, map_in = [], [], [], None
    for iteration in range(ITERS):
        first, final = iteration == 0, iteration == ITERS - 1
        messages = gathered(sz, iteration, message)
        hours_in = layers_exchanged(sz, hour_messages)
        map_in = hours_in[0] if first else map_in
        args = vmem(*state, flow_cost, friction, contract_map, matching)
        args += vmem(*messages, *hours_in, *duals, *weight)
        duals_rows = segs + (SUBLANES if sz.paired and not first else 0)
        outs = [(sz.seg_tail + SUBLANES, pipes), (duals_rows, classes), contracts, cells]
        seg_message, duals_message, full_duals, spread, *scalars = local_call(
            functools.partial(spread_kernel, sz, iteration),
            outs + ([] if first else [scalars_shape]),
            args,
            kept=True,
            scratch=[pltpu.VMEM((sz.end_rows[first], pipes), jnp.float32)],
        )
        duals = [full_duals]
        seg_in = swapped(seg_message, "seg", 1)
        if sz.paired:
            duals_in = swapped(duals_message, "hour", 1)
            scalars += [swapped(part, ("hour", "seg"), 3) for part in scalars]
        else:
            steps = range(sz.hour_parts - 1)
            duals_in = lax.ppermute(duals_message, "hour", [(i, i + 1) for i in steps])
            scalars = [lax.psum(part, ("hour", "seg")) for part in scalars]
        args = vmem(*state, flow_cost, injection, friction, contract_map, target_now, spread)
        args += vmem(seg_in, *hours_in, duals_in, map_in, *known, *weight, *scalars)
        message_rows = sz.sums + SUBLANES + (0 if final else sz.ends_packed(False))
        outs = [cells] * 4 + [(message_rows, classes)]
        outs += [] if first else [(SUBLANES, LANES)]
        results = local_call(
            functools.partial(step_kernel, sz, iteration, final),
            outs + ([] if final else known_shapes + layer_shapes),
            args,
            kept=True,
        )
        state, message, rest = results[:4], results[4], results[5:]
        weight, rest = ([], rest) if first else (rest[:1], rest[1:])
        known, hour_messages = rest[:2], rest[2:]
    *state, written = written_out(state)
    contract_out, scalars = local_call(
        functools.partial(close_kernel, sz),
        [(hours, chunk, classes), scalars_shape],
        vmem(*gathered(sz, ITERS, message), *duals, *weight, written),
        kept=True,
    )
    if sz.paired:
        sums = [scalars] + [swapped(scalars, ("hour", "seg"), k) for k in (1, 2, 3)]
    else:
        sums = [lax.psum(scalars, ("hour", "seg"))]
    (weight,) = local_call(weight_kernel, [(1, 1)], vmem(*weight, *sums))
    return (
        *state,
        contract_out.reshape(contract_dual.shape),
        weight.reshape(1),
    )


def solution(mesh):
    cells = P(("groups", "hour"), "seg", "pipe")
    contracts = P(("groups", "hour"), "seg", "pipe", None)
    return jax.shard_map(
        on_device,
        mesh=mesh,
        in_specs=(
            cells,
            cells,
            cells,
            cells,
            contracts,
            cells,
            cells,
            contracts,
            P(),
            P("seg", ("groups", "pipe")),
            P("groups"),
            P(("groups", "hour"), None),
        ),
        out_specs=(cells, cells, cells, cells, contracts, P("groups")),
        check_vma=False,
    )
```

```python
import functools

import jax
import jax.numpy as jnp
from jax import lax
from jax.experimental import pallas as pl
from jax.experimental.pallas import tpu as pltpu
from jax.sharding import PartitionSpec as P

ITERS = 2

FLOW_CAP = 1.5
PACK_CAP = 2.5
STEP_SCALE = 0.25
NORM_EPS = 1e-06

LANES = 128
SUBLANES = 8
VMEM_LIMIT = 8 * 1024 * 1024
CORNER_ORDER = (1, 2, 3)
PIPE_ORDERS = ((1, 3, 2), (1, 3, 2), (1, 3, 2))
NT = (((1,), (1,)), ((), ()))
NN = (((1,), (0,)), ((), ()))


def rounded_up(count):
    return -(-count // SUBLANES) * SUBLANES


def local_call(body, outs, args, kept=False, scratch=(), kinds={}):
    spaces = {"smem": pltpu.SMEM, "vmem": pltpu.VMEM, "hbm": pltpu.HBM}
    shape_of = pltpu.VMEM if kept else jax.ShapeDtypeStruct
    arrays = [
        pltpu.with_memory_space_constraint(array, pltpu.HBM) if space == "hbm" else array
        for space, array in args
    ]
    results = pl.pallas_call(
        body,
        out_shape=[shape_of(shape, kinds.get(index, jnp.float32)) for index, shape in enumerate(outs)],
        in_specs=[pl.BlockSpec(memory_space=spaces[space]) for space, _ in args],
        out_specs=[pl.BlockSpec(memory_space=pltpu.VMEM) for _ in outs],
        scratch_shapes=scratch,
        compiler_params=pltpu.CompilerParams(vmem_limit_bytes=VMEM_LIMIT),
    )(*arrays)
    return list(results)


def vmem(*arrays):
    return [("vmem", array) for array in arrays]


def taker(refs):
    refs = list(refs)

    def take(count):
        return [refs.pop(0) for _ in range(count)]

    return take


def parts_of(values):
    high = values.astype(jnp.bfloat16).astype(jnp.float32)
    rest = values - high
    middle = rest.astype(jnp.bfloat16).astype(jnp.float32)
    return jnp.concatenate([high, middle, rest - middle], axis=0).astype(jnp.bfloat16)


def exact_product(values, onehot, dims):
    rows = values.shape[0]
    product = lax.dot_general(
        parts_of(values), onehot, dims, preferred_element_type=jnp.float32
    )
    return product[:rows] + product[rows : 2 * rows] + product[2 * rows :]


def as_onehot(mask):
    return jnp.where(mask, 1.0, 0.0).astype(jnp.bfloat16)


def contract_onehot(map_row, class_count):
    shape = (class_count, map_row.shape[1])
    return as_onehot(lax.broadcasted_iota(jnp.int32, shape, 0) == map_row)


def friction_of(classes, table_ref, levels):
    friction = jnp.zeros(classes.shape, jnp.float32)
    for level in range(levels):
        friction = jnp.where(classes == level, table_ref[level], friction)
    return friction


def folded(values):
    rows, width = values.shape
    total = values[:SUBLANES]
    for start in range(SUBLANES, rows, SUBLANES):
        total = total + values[start : start + SUBLANES]
    result = total[:, :LANES]
    for start in range(LANES, width, LANES):
        result = result + total[:, start : start + LANES]
    return result


def tree_sum(terms):
    while len(terms) > 1:
        terms = [a + b for a, b in zip(terms[0::2], terms[1::2])]
    return terms[0]


def swapped(message, axes, distance):
    count = lax.axis_size(axes)
    return lax.ppermute(message, axes, [(i, i ^ distance) for i in range(count)])


class Sizes:
    def __init__(self, hours, segs, pipes, chunk, classes, levels):
        self.hours, self.segs, self.pipes = hours, segs, pipes
        self.chunk, self.classes, self.levels = chunk, classes, levels
        self.blocks = lax.axis_size("pipe")
        self.hour_parts = lax.axis_size("hour")
        self.share = classes / (pipes * self.blocks)
        self.halves = pipes // LANES
        self.paired = self.hour_parts == 2
        self.end_rows = {True: 2 * hours, False: hours}
        self.sums = hours * segs
        self.first_ends = rounded_up(hours * chunk)
        self.seg_tail = {True: 5 * hours, False: 3 * hours}

    def owner(self, block, index):
        return lax.bitwise_xor(block, index)

    def pipe_order(self, phase):
        return PIPE_ORDERS[phase] if self.blocks == 4 else range(1, self.blocks)

    def ends_packed(self, first):
        return rounded_up(self.end_rows[first] * self.halves)

    def own_pipes(self, block):
        return pl.ds(pl.multiple_of(block * self.pipes, LANES), self.pipes)


def take_messages(sz, phase, take):
    own, *received = take(sz.blocks)
    by_distance = dict(zip(sz.pipe_order(phase), received))
    return [own] + [by_distance[distance] for distance in range(1, sz.blocks)]


def places():
    return lax.axis_index("pipe"), lax.axis_index("hour"), lax.axis_index("seg") == 0


def write_ends(sz, message, start, rows):
    for index, row in enumerate(rows):
        for half in range(sz.halves):
            at = start + half * len(rows) + index
            message[at : at + 1, :] = row[:, half * LANES : (half + 1) * LANES]


def read_ends(sz, message, start, count):
    pieces = [
        message[start + half * count : start + (half + 1) * count, :]
        for half in range(sz.halves)
    ]
    return jnp.concatenate(pieces, axis=1)


def write_edges(sz, message, first, first_seg, state, cost, resistance, spread, found):
    flow, pack, mass, momentum = state
    hours, last = sz.hours, sz.segs - 1
    top, bottom = slice(0, 1), slice(last, last + 1)
    for t in range(hours):
        gap = cost[t, bottom, :] - mass[t, bottom, :] - resistance * momentum[t, bottom, :]
        gradient = mass[t, top, :] - momentum[t, top, :] + spread[t, top, :]
        matched = found[t : t + 1, :]
        rows = [
            jnp.where(first_seg, matched, mass[t, top, :]),
            jnp.where(first_seg, momentum[t, bottom, :], gradient),
            jnp.where(first_seg, gap, matched),
        ]
        if first:
            rows.append(jnp.where(first_seg, flow[t, bottom, :], pack[t, top, :]))
            rows.append(found[hours + t : hours + t + 1, :])
        for slot, row in enumerate(rows):
            at = slot * hours + t
            message[at : at + 1, :] = row


def write_layers(sz, outs, first_hour, pack, mass, momentum, first_mass):
    segs = sz.segs
    top = lax.broadcasted_iota(jnp.int32, (segs, sz.pipes), 0) == 0
    gradient = mass - momentum + jnp.where(top, 0.0, pltpu.roll(momentum, 1, 0))
    if sz.paired:
        outs[0][0:segs, :] = jnp.where(first_hour, gradient, first_mass)
    else:
        outs[0][0:segs, :] = gradient
        outs[1][...] = first_mass
    if pack is not None:
        outs[0][segs : 2 * segs, :] = pack
    tail = outs[0].shape[0] - SUBLANES
    outs[0][tail:, :] = jnp.zeros((SUBLANES, sz.pipes), jnp.float32)
    outs[0][tail : tail + 1, :] = momentum[segs - 1 : segs, :]


def match_onehots(sz, block, inlet_side, matching, result):
    row = lax.broadcasted_iota(jnp.int32, (sz.pipes, sz.pipes), 0)

    @pl.when(inlet_side)
    def _():
        own = matching[0:1, sz.own_pipes(block)]
        for index in range(sz.blocks):
            result[index] = as_onehot(row + sz.owner(block, index) * sz.pipes == own)

    @pl.when(jnp.logical_not(inlet_side))
    def _():
        here = row + block * sz.pipes
        for index in range(sz.blocks):
            feeds = matching[0:1, sz.own_pipes(sz.owner(block, index))]
            result[index] = as_onehot(here == feeds)


def matched_rows(sz, inlet_side, ends, onehots, found):
    for side, dims in ((inlet_side, NN), (jnp.logical_not(inlet_side), NT)):

        @pl.when(side)
        def _(dims=dims):
            result = jnp.zeros(found.shape, jnp.float32)
            for index, values in enumerate(ends):
                result = result + exact_product(values, onehots[index], dims)
            found[...] = result


def prepare_kernel(sz, *refs):
    contract_map_in, classes_in, table_in, matching = refs[:4]
    onehots, matches, friction = refs[4:7]
    contract_map, classes, table, arrived = refs[7:]
    block, hour, first_seg = places()
    pairs = [
        (contract_map_in.at[:, sz.own_pipes(block)], contract_map),
        (classes_in, classes),
        (table_in, table),
    ]
    copies = [
        pltpu.make_async_copy(source, target, arrived.at[index])
        for index, (source, target) in enumerate(pairs)
    ]
    for copy in copies:
        copy.start()
    match_onehots(sz, block, jnp.logical_not(first_seg), matching, matches)
    for copy in copies:
        copy.wait()
    for t in range(sz.hours):
        onehots[t] = contract_onehot(contract_map[t : t + 1, :], sz.classes)
    friction[...] = friction_of(classes[...], table, sz.levels)


def prepare_scratch(sz):
    return [
        pltpu.VMEM((sz.hours, sz.pipes), jnp.int32),
        pltpu.VMEM((sz.segs, sz.pipes), jnp.int32),
        pltpu.SMEM((sz.levels,), jnp.float32),
        pltpu.SemaphoreType.DMA((3,)),
    ]


def start_kernel(sz, *refs):
    take = taker(refs)
    flow, pack, mass, momentum, cost, classes_in, duals_in, contract_map, table_in = take(9)
    matching_in = take(1)[0]
    message, matching, *hour_messages = take(2 + (1 if sz.paired else 2))
    flow_last, cost_last, mass_last, momentum_last, mass_first = take(5)
    pack_layer, mass_layer, momentum_layer, mass_start = take(4)
    duals, map_own, classes, table, arrived = take(5)
    block, hour, first_seg = places()
    hours, segs = sz.hours, sz.segs
    low, high = pl.ds(0, SUBLANES), pl.ds(segs - SUBLANES, SUBLANES)
    copies = [
        (flow.at[:, high], flow_last),
        (cost.at[:, high], cost_last),
        (mass.at[:, high], mass_last),
        (momentum.at[:, high], momentum_last),
        (mass.at[:, low], mass_first),
        (pack.at[hours - 1], pack_layer),
        (mass.at[hours - 1], mass_layer),
        (momentum.at[hours - 1], momentum_layer),
        (mass.at[0], mass_start),
        (duals_in, duals),
        (contract_map.at[:, sz.own_pipes(block)], map_own),
        (classes_in.at[high], classes),
        (table_in, table),
        (matching_in, matching),
    ]
    copies = [
        pltpu.make_async_copy(source, target, arrived.at[index])
        for index, (source, target) in enumerate(copies)
    ]
    for copy in copies:
        copy.start()
    for copy in copies:
        copy.wait()
    end = SUBLANES - 1
    resistance = friction_of(classes[...], table, sz.levels)[end:]
    firsts = [mass_first[t, 0:1, :] for t in range(hours)]
    lasts = [flow_last[t, end : end + 1, :] for t in range(hours)]
    gaps = [
        cost_last[t, end : end + 1, :]
        - mass_last[t, end : end + 1, :]
        - resistance * momentum_last[t, end : end + 1, :]
        for t in range(hours)
    ]
    for t in range(hours):
        message[t * sz.chunk : (t + 1) * sz.chunk, :] = duals[t]
    rows = [jnp.where(first_seg, a, b) for a, b in zip(firsts + firsts, gaps + lasts)]
    write_ends(sz, message, sz.first_ends, rows)
    write_layers(
        sz,
        hour_messages,
        hour == 0,
        pack_layer[...],
        mass_layer[...],
        momentum_layer[...],
        mass_start[...],
    )
    map_row = map_own[hours - 1 : hours, :].astype(jnp.float32)
    tail = hour_messages[0].shape[0] - SUBLANES
    hour_messages[0][tail + 1 : tail + 2, :] = map_row


def start_scratch(sz):
    ends = pltpu.VMEM((sz.hours, SUBLANES, sz.pipes), jnp.float32)
    layer = pltpu.VMEM((sz.segs, sz.pipes), jnp.float32)
    return (
        [ends] * 5
        + [layer] * 4
        + [
            pltpu.VMEM((sz.hours, sz.chunk, sz.classes), jnp.float32),
            pltpu.VMEM((sz.hours, sz.pipes), jnp.int32),
            pltpu.VMEM((SUBLANES, sz.pipes), jnp.int32),
            pltpu.SMEM((sz.levels,), jnp.float32),
            pltpu.SemaphoreType.DMA((14,)),
        ]
    )


def duals_kernel(sz, iteration, *refs):
    take = taker(refs)
    first = iteration == 0
    messages = take_messages(sz, iteration, take)
    prepared = take(1)
    old_duals = None if first else take(1)[0]
    old_weight = take(1)[0][0:1, 0:1] if iteration > 1 else 1.0
    duals, hour_message = take(2)
    scalars = None if first else take(1)[0]
    block = places()[0]
    hours, segs, chunk = sz.hours, sz.segs, sz.chunk
    if first:
        for index, ref in enumerate(messages):
            owner = sz.owner(block, index)
            rows = pl.ds(pl.multiple_of(owner * chunk, chunk), chunk)
            for t in range(hours):
                duals[t, rows, :] = ref[t * chunk : (t + 1) * chunk, :]
    else:
        dual_step = STEP_SCALE * old_weight
        dual_sq = jnp.zeros((SUBLANES, LANES), jnp.float32)
        for t in range(hours):
            totals = tree_sum([ref[t * segs : (t + 1) * segs, :] for ref in messages])
            change = dual_step * totals
            duals[t] = old_duals[t] - change
            dual_sq = dual_sq + folded(change * change)
        at = sz.sums + sz.ends_packed(False)
        write_squares([ref[at : at + SUBLANES, :] for ref in messages], dual_sq, scalars)
    hour_message[0:segs, :] = duals[hours - 1]
    if sz.paired:
        rest = (hour_message.shape[0] - segs, sz.classes)
        hour_message[segs:, :] = jnp.zeros(rest, jnp.float32)
    if sz.paired and not first:
        for part in (0, 1):
            at = segs + part
            hour_message[at : at + 1, :LANES] = scalars[0:1, part * LANES : (part + 1) * LANES]


def spread_kernel(sz, iteration, *refs):
    take = taker(refs)
    first = iteration == 0
    flow, pack, mass, momentum, cost, friction, onehots, matches = take(8)
    messages = take_messages(sz, iteration, take)
    hours_in = take(1 if sz.paired else 2)
    duals = take(1)[0]
    scalars = None if first else take(1)[0]
    map_in = take(1)[0] if first else None
    seg_message, spread = take(2)
    earlier_onehot = take(1)[0] if first else None
    found = take(1)[0]
    earlier_in, later_in = hours_in[0], hours_in[-1]
    block, hour, first_seg = places()
    hours, segs = sz.hours, sz.segs
    last = segs - 1

    ends_at, count = sz.first_ends if first else sz.sums, sz.end_rows[first]
    ends = [read_ends(sz, ref, ends_at, count) for ref in messages]
    matched_rows(sz, jnp.logical_not(first_seg), ends, matches, found)
    for t in range(hours):
        spread[t] = sz.share * exact_product(duals[t], onehots[t], NN)
    if first:
        tail = map_in.shape[0] - SUBLANES
        map_row = map_in[tail + 1 : tail + 2, :].astype(jnp.int32)
        earlier_onehot[...] = contract_onehot(map_row, sz.classes)

    state = (flow, pack, mass, momentum)
    resistance = friction[last:segs, :]
    write_edges(sz, seg_message, first, first_seg, state, cost, resistance, spread, found)
    at = sz.seg_tail[first]
    seg_message[at:, :] = jnp.zeros((seg_message.shape[0] - at, sz.pipes), jnp.float32)
    if not first:
        seg_message[at : at + 1, : 2 * LANES] = scalars[0:1, :]
    tail = earlier_in.shape[0] - SUBLANES
    seg_message[at + 1 : at + 2, :] = jnp.where(
        first_seg, earlier_in[tail : tail + 1, :], later_in[0:1, :]
    )


def write_squares(squares, dual_sq, scalars):
    total = tree_sum(squares)
    scalars[...] = jnp.zeros(scalars.shape, jnp.float32)
    scalars[0:1, :LANES] = total[0:1]
    scalars[0:1, LANES:] = total[1:2] + jnp.sum(dual_sq, axis=0, keepdims=True)


def new_weight(weight, total):
    primal = jnp.sum(total[:, :LANES], axis=1, keepdims=True)
    dual = jnp.sum(total[:, LANES : 2 * LANES], axis=1, keepdims=True)
    return jnp.sqrt(weight * jnp.sqrt((dual + NORM_EPS) / (primal + NORM_EPS)))


def step(sz, block, hour, first_seg, weight, state, data, halo, spread_of, outs, message, kept):
    flow, pack, mass, momentum = state
    cost, injection, resistance, target = data
    flow_out, pack_out, mass_out, momentum_out = outs
    edge_flow_out, edge_pack_out, earlier_pack_out = kept
    hours, segs, pipes = sz.hours, sz.segs, sz.pipes
    last, end = segs - 1, hours - 1
    has_earlier = hour > 0
    has_later = hour < sz.hour_parts - 1
    primal_step = STEP_SCALE / weight
    dual_step = STEP_SCALE * weight

    row_index = lax.broadcasted_iota(jnp.int32, (segs, pipes), 0)
    top, bottom = row_index == 0, row_index == last

    def from_above(values, row):
        return jnp.where(top, row, pltpu.roll(values, 1, 0))

    def from_below(values, row):
        return jnp.where(bottom, row, pltpu.roll(values, segs - 1, 0))

    def seg_row(slot, t):
        at = slot * hours + t
        return halo["seg"][at : at + 1, :]

    def new_flow(start, gap):
        return jnp.clip(start - primal_step * gap, -FLOW_CAP, FLOW_CAP)

    def new_pack(start, gradient):
        return jnp.clip(start + primal_step * gradient, 0.0, PACK_CAP)

    corner = halo["corner"]
    earlier_pack = halo["earlier_pack"]
    earlier_gradient = (
        halo["earlier"][0:segs, :]
        + halo["earlier_spread"]
        + jnp.where(top, jnp.where(first_seg, 0.0, corner), 0.0)
        - mass[0]
    )
    earlier_next = new_pack(earlier_pack, earlier_gradient)
    earlier_bar = jnp.where(has_earlier, 2.0 * earlier_next - earlier_pack, 0.0)
    if earlier_pack_out is not None:
        earlier_pack_out[...] = earlier_next
    later_mass = jnp.where(has_later, halo["later"][0:segs, :], 0.0)
    later_corner = jnp.where(has_later, corner, 0.0)
    primal_sq = jnp.zeros((SUBLANES, LANES), jnp.float32)
    dual_sq = jnp.zeros((SUBLANES, LANES), jnp.float32)
    for t in range(hours):
        mass_now, momentum_now = mass[t], momentum[t]
        flow_now, pack_now = flow[t], pack[t]
        spread, onehot = spread_of(t)
        below_mass = seg_row(0, t)
        next_mass = mass[t + 1] if t < end else later_mass
        gap = cost[t] - (
            mass_now - from_below(mass_now, below_mass) + resistance * momentum_now
        )
        flow_next = new_flow(flow_now, gap)
        above_momentum = jnp.where(first_seg, 0.0, seg_row(1, t))
        gradient = (
            mass_now
            - next_mass
            - momentum_now
            + from_above(momentum_now, above_momentum)
            + spread
        )
        pack_next = new_pack(pack_now, gradient)
        flow_bar = 2.0 * flow_next - flow_now
        pack_bar = 2.0 * pack_next - pack_now

        edge_flow, edge_pack = halo["edges"](t)
        edge_gap = seg_row(2, t) + mass_now[0:1, :]
        edge_flow_next = new_flow(edge_flow, edge_gap)
        edge_flow_bar = 2.0 * edge_flow_next - edge_flow
        edge_later = seg_row(0, t + 1) if t < end else later_corner
        edge_gradient = seg_row(1, t) + momentum_now[last : last + 1, :] - edge_later
        edge_pack_next = new_pack(edge_pack, edge_gradient)
        edge_pack_bar = jnp.where(first_seg, 2.0 * edge_pack_next - edge_pack, 0.0)
        if edge_flow_out is not None:
            edge_flow_out[t : t + 1, :] = edge_flow_next
            edge_pack_out[t : t + 1, :] = edge_pack_next

        mass_rows = pack_bar - earlier_bar + flow_bar - from_above(flow_bar, edge_flow_bar)
        momentum_rows = resistance * flow_bar - (pack_bar - from_below(pack_bar, edge_pack_bar))
        mass_change = dual_step * (injection[t] - mass_rows)
        momentum_change = dual_step * momentum_rows
        flow_out[t] = flow_next
        pack_out[t] = pack_next
        mass_out[t] = mass_now + mass_change
        momentum_out[t] = momentum_now - momentum_change
        flow_change, pack_change = flow_next - flow_now, pack_next - pack_now
        primal_sq = primal_sq + folded(flow_change * flow_change + pack_change * pack_change)
        dual_sq = dual_sq + folded(
            mass_change * mass_change + momentum_change * momentum_change
        )
        message[t * segs : (t + 1) * segs, :] = sz.share * exact_product(pack_bar, onehot, NT)
        rows = pl.ds(pl.multiple_of(t * segs + block * sz.chunk, sz.chunk), sz.chunk)
        message[rows, :] = message[rows, :] - target[t]
        earlier_bar = pack_bar

    at = message.shape[0] - SUBLANES
    message[at:, :] = jnp.zeros((SUBLANES, LANES), jnp.float32)
    message[at : at + 1, :] = jnp.sum(primal_sq, axis=0, keepdims=True)
    message[at + 1 : at + 2, :] = jnp.sum(dual_sq, axis=0, keepdims=True)


def write_next(sz, hour, first_seg, outs, cost, resistance, message, hour_messages):
    flow, pack, mass, momentum = outs
    last = sz.segs - 1
    firsts = [mass[t, 0:1, :] for t in range(sz.hours)]
    gaps = [
        cost[t, last : last + 1, :]
        - mass[t, last : last + 1, :]
        - resistance[last : last + 1, :] * momentum[t, last : last + 1, :]
        for t in range(sz.hours)
    ]
    rows = [jnp.where(first_seg, a, b) for a, b in zip(firsts, gaps)]
    write_ends(sz, message, sz.sums, rows)
    end = sz.hours - 1
    write_layers(sz, hour_messages, hour == 0, None, mass[end], momentum[end], mass[0])


def step_kernel(sz, iteration, final, *refs):
    take = taker(refs)
    first = iteration == 0
    state, data = take(4), take(2)
    friction, onehots, earlier_onehot, target, spread = take(5)
    corner_scalars = take(1) if sz.paired and not first else []
    seg_in, hours_in, duals_in = take(1)[0], take(1 if sz.paired else 2), take(1)[0]
    known = [] if first else take(3)
    old_weight = take(1)[0][0:1, 0:1] if iteration > 1 else 1.0
    scalars = [] if first else take(1)
    outs, message = take(4), take(1)[0]
    weight_out = [] if first else take(1)
    kept = [None] * 3 if final else take(3)
    hour_messages = [] if final else take(1 if sz.paired else 2)
    block, hour, first_seg = places()
    hours, segs = sz.hours, sz.segs
    weight = jnp.ones((1, 1), jnp.float32)
    if not first:
        total = scalars[0][0:1, :]
        if sz.paired:


            def sums_of(ref):
                parts = [ref[segs + part : segs + part + 1, :LANES] for part in (0, 1)]
                return jnp.concatenate(parts, axis=1)

            total = tree_sum(
                [
                    total,
                    seg_in[sz.seg_tail[False] : sz.seg_tail[False] + 1, : 2 * LANES],
                    sums_of(duals_in),
                sums_of(corner_scalars[0]),
                ]
            )
        weight = new_weight(old_weight, total)
        weight_out[0][...] = jnp.broadcast_to(weight, weight_out[0].shape)
    earlier_spread = sz.share * exact_product(duals_in[0:segs, :], earlier_onehot[...], NN)

    def spread_of(t):
        return spread[t], onehots[t]

    def edges(t):
        if not first:
            return known[0][t : t + 1, :], known[1][t : t + 1, :]
        shared, matched = [slot * hours + t for slot in (3, 4)]
        sent = seg_in[shared : shared + 1, :]
        return jnp.where(first_seg, seg_in[matched : matched + 1, :], sent), sent

    at = sz.seg_tail[first] + 1
    halo = {
        "seg": seg_in,
        "corner": seg_in[at : at + 1, :],
        "earlier": hours_in[0],
        "earlier_pack": hours_in[0][segs : 2 * segs, :] if first else known[2][...],
        "edges": edges,
        "later": hours_in[-1],
        "earlier_spread": earlier_spread,
    }
    resistance = friction[...]
    data = [*data, resistance, target]
    step(sz, block, hour, first_seg, weight, state, data, halo, spread_of, outs, message, kept)
    if not final:
        write_next(sz, hour, first_seg, outs, data[0], resistance, message, hour_messages)


def close_kernel(sz, *refs):
    take = taker(refs)
    messages = take_messages(sz, ITERS, take)
    old_duals, weight, written, duals, scalars = take(5)
    block, hour, first_seg = places()
    segs = sz.segs
    dual_step = STEP_SCALE * weight[0:1, 0:1]
    dual_sq = jnp.zeros((SUBLANES, LANES), jnp.float32)
    start = block * sz.chunk
    for t in range(sz.hours):
        totals = tree_sum([ref[t * segs : (t + 1) * segs, :] for ref in messages])
        change = dual_step * totals
        dual_sq = dual_sq + folded(change * change)
        own = pl.ds(pl.multiple_of(start, sz.chunk), sz.chunk)
        rows = pl.ds(pl.multiple_of(t * segs + start, sz.chunk), sz.chunk)
        own_totals = tree_sum([ref[rows, :] for ref in messages])
        duals[t] = old_duals[t, own, :] - dual_step * own_totals
    squares = [ref[sz.sums : sz.sums + SUBLANES, :] for ref in messages]
    write_squares(squares, dual_sq, scalars)


def written_out(state):
    count = len(state)

    def body(*refs):
        sources, targets, token, done = refs[:count], refs[count:-2], refs[-2], refs[-1]
        copies = [
            pltpu.make_async_copy(source, target, done.at[index])
            for index, (source, target) in enumerate(zip(sources, targets))
        ]
        for copy in copies:
            copy.start()
        token[...] = jnp.zeros(token.shape, jnp.float32)
        for copy in copies:
            copy.wait()

    return pl.pallas_call(
        body,
        out_shape=[pltpu.HBM(array.shape, array.dtype) for array in state]
        + [pltpu.VMEM((SUBLANES, LANES), jnp.float32)],
        in_specs=[pl.BlockSpec(memory_space=pltpu.VMEM) for _ in state],
        out_specs=[pl.BlockSpec(memory_space=pltpu.HBM) for _ in state]
        + [pl.BlockSpec(memory_space=pltpu.VMEM)],
        scratch_shapes=[pltpu.SemaphoreType.DMA((count,))],
        compiler_params=pltpu.CompilerParams(vmem_limit_bytes=VMEM_LIMIT),
    )(*state)


def weight_kernel(weight, *refs):
    *scalars, result = refs
    if len(scalars) == 4:
        own, *received = scalars
        by_distance = dict(zip(CORNER_ORDER, received))
        scalars = [own, by_distance[1], by_distance[2], by_distance[3]]
    result[...] = new_weight(weight[0:1, 0:1], tree_sum([ref[0:1, :] for ref in scalars]))


def gathered(sz, phase, message):
    return [message] + [swapped(message, "pipe", k) for k in sz.pipe_order(phase)]


def layers_exchanged(sz, hour_messages):
    if sz.paired:
        return [swapped(hour_messages[0], "hour", 1)]
    steps = range(sz.hour_parts - 1)
    return [
        lax.ppermute(hour_messages[0], "hour", [(i, i + 1) for i in steps]),
        lax.ppermute(hour_messages[1], "hour", [(i + 1, i) for i in steps]),
    ]


def on_device(
    segment_flow,
    linepack,
    mass_dual,
    momentum_dual,
    contract_dual,
    flow_cost,
    injection,
    contract_target,
    friction_table,
    friction_class,
    matching,
    contract_map,
):
    hours, segs, pipes = segment_flow.shape
    chunk, classes = contract_dual.shape[2:]
    sz = Sizes(hours, segs, pipes, chunk, classes, friction_table.shape[0])
    duals_now = contract_dual.reshape(hours, chunk, classes)
    target_now = contract_target.reshape(hours, chunk, classes)
    matching = matching.reshape(1, matching.shape[0])
    cells, contracts = (hours, segs, pipes), (hours, segs, classes)
    layer_shapes = [(segs + SUBLANES, pipes)]
    if not sz.paired:
        layer_shapes.append((segs, pipes))
    known_shapes = [(rounded_up(hours), pipes)] * 2 + [(segs, pipes)]
    scalars_shape = (SUBLANES, 2 * LANES)

    state = [segment_flow, linepack, mass_dual, momentum_dual]
    raw = [*state, flow_cost, friction_class, duals_now, contract_map, friction_table, matching]
    message, matching, *hour_messages = local_call(
        functools.partial(start_kernel, sz),
        [
            (sz.first_ends + sz.ends_packed(True), classes),
            matching.shape,
            (2 * segs + SUBLANES, pipes),
            *layer_shapes[1:],
        ],
        [("hbm", array) for array in raw],
        kept=True,
        scratch=start_scratch(sz),
        kinds={1: jnp.int32},
    )
    onehots, matches, friction = local_call(
        functools.partial(prepare_kernel, sz),
        [(hours, classes, pipes), (sz.blocks, pipes, pipes), (segs, pipes)],
        [("hbm", array) for array in (contract_map, friction_class, friction_table)]
        + vmem(matching),
        kept=True,
        scratch=prepare_scratch(sz),
        kinds={0: jnp.bfloat16, 1: jnp.bfloat16},
    )
    duals, weight, known, earlier_onehot = [], [], [], None
    for iteration in range(ITERS):
        first, final = iteration == 0, iteration == ITERS - 1
        messages = gathered(sz, iteration, message)
        hours_in = layers_exchanged(sz, hour_messages)
        seg_rows = rounded_up(sz.seg_tail[first] + 2)
        duals_rows = segs
        if sz.paired:
            duals_rows = max(segs + SUBLANES, seg_rows * sz.halves + SUBLANES)
        full_duals, duals_message, *scalars = local_call(
            functools.partial(duals_kernel, sz, iteration),
            [contracts, (duals_rows, classes)] + ([] if first else [scalars_shape]),
            vmem(*messages, friction, *duals, *weight),
            kept=True,
        )
        duals = [full_duals]
        args = vmem(*state, flow_cost, friction, onehots, matches)
        args += vmem(*messages, *hours_in, *duals, *scalars, *(hours_in[:1] if first else []))
        seg_message, spread, *built = local_call(
            functools.partial(spread_kernel, sz, iteration),
            [(seg_rows, pipes), cells] + ([(classes, pipes)] if first else []),
            args,
            kept=True,
            scratch=[pltpu.VMEM((sz.end_rows[first], pipes), jnp.float32)],
            kinds={2: jnp.bfloat16},
        )
        earlier_onehot = built[0] if first else earlier_onehot
        seg_in = swapped(seg_message, "seg", 1)
        if sz.paired:
            duals_in = swapped(duals_message, "hour", 1)
            corner_in = [swapped(duals_message, ("hour", "seg"), 3) for part in scalars]
        else:
            steps = range(sz.hour_parts - 1)
            duals_in = lax.ppermute(duals_message, "hour", [(i, i + 1) for i in steps])
            scalars = [lax.psum(part, ("hour", "seg")) for part in scalars]
            corner_in = []
        args = vmem(
            *state, flow_cost, injection, friction, onehots, earlier_onehot, target_now, spread
        )
        args += vmem(*corner_in, seg_in, *hours_in, duals_in, *known, *weight, *scalars)
        message_rows = sz.sums + SUBLANES + (0 if final else sz.ends_packed(False))
        outs = [cells] * 4 + [(message_rows, classes)]
        outs += [] if first else [(SUBLANES, LANES)]
        results = local_call(
            functools.partial(step_kernel, sz, iteration, final),
            outs + ([] if final else known_shapes + layer_shapes),
            args,
            kept=True,
        )
        state, message, rest = results[:4], results[4], results[5:]
        weight, rest = ([], rest) if first else (rest[:1], rest[1:])
        known, hour_messages = rest[:3], rest[3:]
    *state, written = written_out(state)
    contract_out, scalars = local_call(
        functools.partial(close_kernel, sz),
        [(hours, chunk, classes), scalars_shape],
        vmem(*gathered(sz, ITERS, message), *duals, *weight, written),
        kept=True,
    )
    if sz.paired:
        sums = [scalars] + [swapped(scalars, ("hour", "seg"), k) for k in CORNER_ORDER]
    else:
        sums = [lax.psum(scalars, ("hour", "seg"))]
    (weight,) = local_call(weight_kernel, [(1, 1)], vmem(*weight, *sums))
    return (
        *state,
        contract_out.reshape(contract_dual.shape),
        weight.reshape(1),
    )


def solution(mesh):
    cells = P(("groups", "hour"), "seg", "pipe")
    contracts = P(("groups", "hour"), "seg", "pipe", None)
    return jax.shard_map(
        on_device,
        mesh=mesh,
        in_specs=(
            cells,
            cells,
            cells,
            cells,
            contracts,
            cells,
            cells,
            contracts,
            P(),
            P("seg", ("groups", "pipe")),
            P("groups"),
            P(("groups", "hour"), None),
        ),
        out_specs=(cells, cells, cells, cells, contracts, P("groups")),
        check_vma=False,
    )
```

```python
import functools

import jax
import jax.numpy as jnp
from jax import lax
from jax.experimental import pallas as pl
from jax.experimental.pallas import tpu as pltpu
from jax.sharding import PartitionSpec as P

ITERS = 2

FLOW_CAP = 1.5
PACK_CAP = 2.5
STEP_SCALE = 0.25
NORM_EPS = 1e-06

LANES = 128
PREP_FLOPS = 1 << 30
SUBLANES = 8
VMEM_LIMIT = 8 * 1024 * 1024
CORNER_ORDER = (1, 2, 3)
PIPE_ORDERS = ((1, 3, 2), (2, 1, 3), (1, 3, 2))
NT = (((1,), (1,)), ((), ()))
NN = (((1,), (0,)), ((), ()))


def rounded_up(count):
    return -(-count // SUBLANES) * SUBLANES


def local_call(body, outs, args, kept=False, scratch=(), kinds={}, cost=None):
    spaces = {"smem": pltpu.SMEM, "vmem": pltpu.VMEM, "hbm": pltpu.HBM}
    shape_of = pltpu.VMEM if kept else jax.ShapeDtypeStruct
    arrays = [
        pltpu.with_memory_space_constraint(array, pltpu.HBM) if space == "hbm" else array
        for space, array in args
    ]
    results = pl.pallas_call(
        body,
        out_shape=[shape_of(shape, kinds.get(index, jnp.float32)) for index, shape in enumerate(outs)],
        in_specs=[pl.BlockSpec(memory_space=spaces[space]) for space, _ in args],
        out_specs=[pl.BlockSpec(memory_space=pltpu.VMEM) for _ in outs],
        scratch_shapes=scratch,
        compiler_params=pltpu.CompilerParams(vmem_limit_bytes=VMEM_LIMIT),
        cost_estimate=cost,
    )(*arrays)
    return list(results)


def vmem(*arrays):
    return [("vmem", array) for array in arrays]


def taker(refs):
    refs = list(refs)

    def take(count):
        return [refs.pop(0) for _ in range(count)]

    return take


def parts_of(values):
    high = values.astype(jnp.bfloat16).astype(jnp.float32)
    rest = values - high
    middle = rest.astype(jnp.bfloat16).astype(jnp.float32)
    return jnp.concatenate([high, middle, rest - middle], axis=0).astype(jnp.bfloat16)


def exact_product(values, onehot, dims):
    rows = values.shape[0]
    product = lax.dot_general(
        parts_of(values), onehot, dims, preferred_element_type=jnp.float32
    )
    return product[:rows] + product[rows : 2 * rows] + product[2 * rows :]


def as_onehot(mask):
    return jnp.where(mask, 1.0, 0.0).astype(jnp.bfloat16)


def contract_onehot(map_row, class_count):
    shape = (class_count, map_row.shape[1])
    return as_onehot(lax.broadcasted_iota(jnp.int32, shape, 0) == map_row)


def friction_of(classes, table_ref, levels):
    friction = jnp.zeros(classes.shape, jnp.float32)
    for level in range(levels):
        friction = jnp.where(classes == level, table_ref[level], friction)
    return friction


def folded(values):
    rows, width = values.shape
    total = values[:SUBLANES]
    for start in range(SUBLANES, rows, SUBLANES):
        total = total + values[start : start + SUBLANES]
    result = total[:, :LANES]
    for start in range(LANES, width, LANES):
        result = result + total[:, start : start + LANES]
    return result


def tree_sum(terms):
    while len(terms) > 1:
        terms = [a + b for a, b in zip(terms[0::2], terms[1::2])]
    return terms[0]


def swapped(message, axes, distance):
    count = lax.axis_size(axes)
    return lax.ppermute(message, axes, [(i, i ^ distance) for i in range(count)])


class Sizes:
    def __init__(self, hours, segs, pipes, chunk, classes, levels):
        self.hours, self.segs, self.pipes = hours, segs, pipes
        self.chunk, self.classes, self.levels = chunk, classes, levels
        self.blocks = lax.axis_size("pipe")
        self.hour_parts = lax.axis_size("hour")
        self.share = classes / (pipes * self.blocks)
        self.halves = pipes // LANES
        self.paired = self.hour_parts == 2
        self.end_rows = {True: 2 * hours, False: hours}
        self.sums = hours * segs
        self.first_ends = rounded_up(hours * chunk)
        self.seg_tail = {True: 5 * hours, False: 3 * hours}

    def owner(self, block, index):
        return lax.bitwise_xor(block, index)

    def pipe_order(self, phase):
        return PIPE_ORDERS[phase] if self.blocks == 4 else range(1, self.blocks)

    def ends_packed(self, first):
        return rounded_up(self.end_rows[first] * self.halves)

    def own_pipes(self, block):
        return pl.ds(pl.multiple_of(block * self.pipes, LANES), self.pipes)


def take_messages(sz, phase, take):
    own, *received = take(sz.blocks)
    by_distance = dict(zip(sz.pipe_order(phase), received))
    return [own] + [by_distance[distance] for distance in range(1, sz.blocks)]


def places():
    return lax.axis_index("pipe"), lax.axis_index("hour"), lax.axis_index("seg") == 0


def write_ends(sz, message, start, rows):
    for index, row in enumerate(rows):
        for half in range(sz.halves):
            at = start + half * len(rows) + index
            message[at : at + 1, :] = row[:, half * LANES : (half + 1) * LANES]


def read_ends(sz, message, start, count):
    pieces = [
        message[start + half * count : start + (half + 1) * count, :]
        for half in range(sz.halves)
    ]
    return jnp.concatenate(pieces, axis=1)


def write_edges(sz, message, first, first_seg, state, cost, resistance, spread, found):
    flow, pack, mass, momentum = state
    hours, last = sz.hours, sz.segs - 1
    top, bottom = slice(0, 1), slice(last, last + 1)
    for t in range(hours):
        gap = cost[t, bottom, :] - mass[t, bottom, :] - resistance * momentum[t, bottom, :]
        gradient = mass[t, top, :] - momentum[t, top, :] + spread[t, top, :]
        matched = found[t : t + 1, :]
        rows = [
            jnp.where(first_seg, matched, mass[t, top, :]),
            jnp.where(first_seg, momentum[t, bottom, :], gradient),
            jnp.where(first_seg, gap, matched),
        ]
        if first:
            rows.append(jnp.where(first_seg, flow[t, bottom, :], pack[t, top, :]))
            rows.append(found[hours + t : hours + t + 1, :])
        for slot, row in enumerate(rows):
            at = slot * hours + t
            message[at : at + 1, :] = row


def write_layers(sz, outs, first_hour, pack, mass, momentum, first_mass):
    segs = sz.segs
    top = lax.broadcasted_iota(jnp.int32, (segs, sz.pipes), 0) == 0
    gradient = mass - momentum + jnp.where(top, 0.0, pltpu.roll(momentum, 1, 0))
    if sz.paired:
        outs[0][0:segs, :] = jnp.where(first_hour, gradient, first_mass)
    else:
        outs[0][0:segs, :] = gradient
        outs[1][...] = first_mass
    if pack is not None:
        outs[0][segs : 2 * segs, :] = pack
    tail = outs[0].shape[0] - SUBLANES
    outs[0][tail:, :] = jnp.zeros((SUBLANES, sz.pipes), jnp.float32)
    outs[0][tail : tail + 1, :] = momentum[segs - 1 : segs, :]


def match_onehots(sz, block, inlet_side, matching, result):
    row = lax.broadcasted_iota(jnp.int32, (sz.pipes, sz.pipes), 0)

    @pl.when(inlet_side)
    def _():
        own = matching[0:1, sz.own_pipes(block)]
        for index in range(sz.blocks):
            result[index] = as_onehot(row + sz.owner(block, index) * sz.pipes == own)

    @pl.when(jnp.logical_not(inlet_side))
    def _():
        here = row + block * sz.pipes
        for index in range(sz.blocks):
            feeds = matching[0:1, sz.own_pipes(sz.owner(block, index))]
            result[index] = as_onehot(here == feeds)


def matched_rows(sz, inlet_side, ends, onehots, found):
    for side, dims in ((inlet_side, NN), (jnp.logical_not(inlet_side), NT)):

        @pl.when(side)
        def _(dims=dims):
            result = jnp.zeros(found.shape, jnp.float32)
            for index, values in enumerate(ends):
                result = result + exact_product(values, onehots[index], dims)
            found[...] = result


def prepare_kernel(sz, *refs):
    contract_map_in, classes_in, table_in, matching = refs[:4]
    onehots, matches, friction = refs[4:7]
    contract_map, classes, table, arrived = refs[7:]
    block, hour, first_seg = places()
    pairs = [
        (contract_map_in.at[:, sz.own_pipes(block)], contract_map),
        (classes_in, classes),
        (table_in, table),
    ]
    copies = [
        pltpu.make_async_copy(source, target, arrived.at[index])
        for index, (source, target) in enumerate(pairs)
    ]
    for copy in copies:
        copy.start()
    match_onehots(sz, block, jnp.logical_not(first_seg), matching, matches)
    for copy in copies:
        copy.wait()
    for t in range(sz.hours):
        onehots[t] = contract_onehot(contract_map[t : t + 1, :], sz.classes)
    friction[...] = friction_of(classes[...], table, sz.levels)


def prepare_scratch(sz):
    return [
        pltpu.VMEM((sz.hours, sz.pipes), jnp.int32),
        pltpu.VMEM((sz.segs, sz.pipes), jnp.int32),
        pltpu.SMEM((sz.levels,), jnp.float32),
        pltpu.SemaphoreType.DMA((3,)),
    ]


def start_kernel(sz, *refs):
    take = taker(refs)
    flow, pack, mass, momentum, cost, classes_in, duals_in, contract_map, table_in = take(9)
    matching_in = take(1)[0]
    message, matching, *hour_messages = take(2 + (1 if sz.paired else 2))
    flow_last, cost_last, mass_last, momentum_last, mass_first = take(5)
    pack_layer, mass_layer, momentum_layer, mass_start = take(4)
    duals, map_own, classes, table, arrived = take(5)
    block, hour, first_seg = places()
    hours, segs = sz.hours, sz.segs
    low, high = pl.ds(0, SUBLANES), pl.ds(segs - SUBLANES, SUBLANES)
    copies = [
        (flow.at[:, high], flow_last),
        (cost.at[:, high], cost_last),
        (mass.at[:, high], mass_last),
        (momentum.at[:, high], momentum_last),
        (mass.at[:, low], mass_first),
        (pack.at[hours - 1], pack_layer),
        (mass.at[hours - 1], mass_layer),
        (momentum.at[hours - 1], momentum_layer),
        (mass.at[0], mass_start),
        (duals_in, duals),
        (contract_map.at[:, sz.own_pipes(block)], map_own),
        (classes_in.at[high], classes),
        (table_in, table),
        (matching_in, matching),
    ]
    copies = [
        pltpu.make_async_copy(source, target, arrived.at[index])
        for index, (source, target) in enumerate(copies)
    ]
    for copy in copies:
        copy.start()
    for copy in copies:
        copy.wait()
    end = SUBLANES - 1
    resistance = friction_of(classes[...], table, sz.levels)[end:]
    firsts = [mass_first[t, 0:1, :] for t in range(hours)]
    lasts = [flow_last[t, end : end + 1, :] for t in range(hours)]
    gaps = [
        cost_last[t, end : end + 1, :]
        - mass_last[t, end : end + 1, :]
        - resistance * momentum_last[t, end : end + 1, :]
        for t in range(hours)
    ]
    for t in range(hours):
        message[t * sz.chunk : (t + 1) * sz.chunk, :] = duals[t]
    rows = [jnp.where(first_seg, a, b) for a, b in zip(firsts + firsts, gaps + lasts)]
    write_ends(sz, message, sz.first_ends, rows)
    write_layers(
        sz,
        hour_messages,
        hour == 0,
        pack_layer[...],
        mass_layer[...],
        momentum_layer[...],
        mass_start[...],
    )
    map_row = map_own[hours - 1 : hours, :].astype(jnp.float32)
    tail = hour_messages[0].shape[0] - SUBLANES
    hour_messages[0][tail + 1 : tail + 2, :] = map_row


def start_scratch(sz):
    ends = pltpu.VMEM((sz.hours, SUBLANES, sz.pipes), jnp.float32)
    layer = pltpu.VMEM((sz.segs, sz.pipes), jnp.float32)
    return (
        [ends] * 5
        + [layer] * 4
        + [
            pltpu.VMEM((sz.hours, sz.chunk, sz.classes), jnp.float32),
            pltpu.VMEM((sz.hours, sz.pipes), jnp.int32),
            pltpu.VMEM((SUBLANES, sz.pipes), jnp.int32),
            pltpu.SMEM((sz.levels,), jnp.float32),
            pltpu.SemaphoreType.DMA((14,)),
        ]
    )


def duals_kernel(sz, iteration, *refs):
    take = taker(refs)
    first = iteration == 0
    messages = take_messages(sz, iteration, take)
    prepared = take(1)
    old_duals = None if first else take(1)[0]
    old_weight = take(1)[0][0:1, 0:1] if iteration > 1 else 1.0
    duals, hour_message = take(2)
    scalars = None if first else take(1)[0]
    block = places()[0]
    hours, segs, chunk = sz.hours, sz.segs, sz.chunk
    if first:
        for index, ref in enumerate(messages):
            owner = sz.owner(block, index)
            rows = pl.ds(pl.multiple_of(owner * chunk, chunk), chunk)
            for t in range(hours):
                duals[t, rows, :] = ref[t * chunk : (t + 1) * chunk, :]
    else:
        dual_step = STEP_SCALE * old_weight
        dual_sq = jnp.zeros((SUBLANES, LANES), jnp.float32)
        for t in range(hours):
            totals = tree_sum([ref[t * segs : (t + 1) * segs, :] for ref in messages])
            change = dual_step * totals
            duals[t] = old_duals[t] - change
            dual_sq = dual_sq + folded(change * change)
        at = sz.sums + sz.ends_packed(False)
        write_squares([ref[at : at + SUBLANES, :] for ref in messages], dual_sq, scalars)
    hour_message[0:segs, :] = duals[hours - 1]
    if sz.paired:
        rest = (hour_message.shape[0] - segs, sz.classes)
        hour_message[segs:, :] = jnp.zeros(rest, jnp.float32)
    if sz.paired and not first:
        for part in (0, 1):
            at = segs + part
            hour_message[at : at + 1, :LANES] = scalars[0:1, part * LANES : (part + 1) * LANES]


def spread_kernel(sz, iteration, *refs):
    take = taker(refs)
    first = iteration == 0
    flow, pack, mass, momentum, cost, friction, onehots, matches = take(8)
    messages = take_messages(sz, iteration, take)
    hours_in = take(1 if sz.paired else 2)
    duals = take(1)[0]
    scalars = None if first else take(1)[0]
    map_in = take(1)[0] if first else None
    seg_message, spread = take(2)
    earlier_onehot = take(1)[0] if first else None
    found = take(1)[0]
    earlier_in, later_in = hours_in[0], hours_in[-1]
    block, hour, first_seg = places()
    hours, segs = sz.hours, sz.segs
    last = segs - 1

    ends_at, count = sz.first_ends if first else sz.sums, sz.end_rows[first]
    ends = [read_ends(sz, ref, ends_at, count) for ref in messages]
    matched_rows(sz, jnp.logical_not(first_seg), ends, matches, found)
    for t in range(hours):
        spread[t] = sz.share * exact_product(duals[t], onehots[t], NN)
    if first:
        tail = map_in.shape[0] - SUBLANES
        map_row = map_in[tail + 1 : tail + 2, :].astype(jnp.int32)
        earlier_onehot[...] = contract_onehot(map_row, sz.classes)

    state = (flow, pack, mass, momentum)
    resistance = friction[last:segs, :]
    write_edges(sz, seg_message, first, first_seg, state, cost, resistance, spread, found)
    at = sz.seg_tail[first]
    seg_message[at:, :] = jnp.zeros((seg_message.shape[0] - at, sz.pipes), jnp.float32)
    if not first:
        seg_message[at : at + 1, : 2 * LANES] = scalars[0:1, :]
    tail = earlier_in.shape[0] - SUBLANES
    seg_message[at + 1 : at + 2, :] = jnp.where(
        first_seg, earlier_in[tail : tail + 1, :], later_in[0:1, :]
    )


def write_squares(squares, dual_sq, scalars):
    total = tree_sum(squares)
    scalars[...] = jnp.zeros(scalars.shape, jnp.float32)
    scalars[0:1, :LANES] = total[0:1]
    scalars[0:1, LANES:] = total[1:2] + jnp.sum(dual_sq, axis=0, keepdims=True)


def new_weight(weight, total):
    primal = jnp.sum(total[:, :LANES], axis=1, keepdims=True)
    dual = jnp.sum(total[:, LANES : 2 * LANES], axis=1, keepdims=True)
    return jnp.sqrt(weight * jnp.sqrt((dual + NORM_EPS) / (primal + NORM_EPS)))


def step(sz, block, hour, first_seg, weight, state, data, halo, spread_of, outs, message, kept):
    flow, pack, mass, momentum = state
    cost, injection, resistance, target = data
    flow_out, pack_out, mass_out, momentum_out = outs
    edge_flow_out, edge_pack_out, earlier_pack_out = kept
    hours, segs, pipes = sz.hours, sz.segs, sz.pipes
    last, end = segs - 1, hours - 1
    has_earlier = hour > 0
    has_later = hour < sz.hour_parts - 1
    primal_step = STEP_SCALE / weight
    dual_step = STEP_SCALE * weight

    row_index = lax.broadcasted_iota(jnp.int32, (segs, pipes), 0)
    top, bottom = row_index == 0, row_index == last

    def from_above(values, row):
        return jnp.where(top, row, pltpu.roll(values, 1, 0))

    def from_below(values, row):
        return jnp.where(bottom, row, pltpu.roll(values, segs - 1, 0))

    def seg_row(slot, t):
        at = slot * hours + t
        return halo["seg"][at : at + 1, :]

    def new_flow(start, gap):
        return jnp.clip(start - primal_step * gap, -FLOW_CAP, FLOW_CAP)

    def new_pack(start, gradient):
        return jnp.clip(start + primal_step * gradient, 0.0, PACK_CAP)

    corner = halo["corner"]
    earlier_pack = halo["earlier_pack"]
    earlier_gradient = (
        halo["earlier"][0:segs, :]
        + halo["earlier_spread"]
        + jnp.where(top, jnp.where(first_seg, 0.0, corner), 0.0)
        - mass[0]
    )
    earlier_next = new_pack(earlier_pack, earlier_gradient)
    earlier_bar = jnp.where(has_earlier, 2.0 * earlier_next - earlier_pack, 0.0)
    if earlier_pack_out is not None:
        earlier_pack_out[...] = earlier_next
    later_mass = jnp.where(has_later, halo["later"][0:segs, :], 0.0)
    later_corner = jnp.where(has_later, corner, 0.0)
    primal_sq = jnp.zeros((SUBLANES, LANES), jnp.float32)
    dual_sq = jnp.zeros((SUBLANES, LANES), jnp.float32)
    for t in range(hours):
        mass_now, momentum_now = mass[t], momentum[t]
        flow_now, pack_now = flow[t], pack[t]
        spread, onehot = spread_of(t)
        below_mass = seg_row(0, t)
        next_mass = mass[t + 1] if t < end else later_mass
        gap = cost[t] - (
            mass_now - from_below(mass_now, below_mass) + resistance * momentum_now
        )
        flow_next = new_flow(flow_now, gap)
        above_momentum = jnp.where(first_seg, 0.0, seg_row(1, t))
        gradient = (
            mass_now
            - next_mass
            - momentum_now
            + from_above(momentum_now, above_momentum)
            + spread
        )
        pack_next = new_pack(pack_now, gradient)
        flow_bar = 2.0 * flow_next - flow_now
        pack_bar = 2.0 * pack_next - pack_now

        edge_flow, edge_pack = halo["edges"](t)
        edge_gap = seg_row(2, t) + mass_now[0:1, :]
        edge_flow_next = new_flow(edge_flow, edge_gap)
        edge_flow_bar = 2.0 * edge_flow_next - edge_flow
        edge_later = seg_row(0, t + 1) if t < end else later_corner
        edge_gradient = seg_row(1, t) + momentum_now[last : last + 1, :] - edge_later
        edge_pack_next = new_pack(edge_pack, edge_gradient)
        edge_pack_bar = jnp.where(first_seg, 2.0 * edge_pack_next - edge_pack, 0.0)
        if edge_flow_out is not None:
            edge_flow_out[t : t + 1, :] = edge_flow_next
            edge_pack_out[t : t + 1, :] = edge_pack_next

        mass_rows = pack_bar - earlier_bar + flow_bar - from_above(flow_bar, edge_flow_bar)
        momentum_rows = resistance * flow_bar - (pack_bar - from_below(pack_bar, edge_pack_bar))
        mass_change = dual_step * (injection[t] - mass_rows)
        momentum_change = dual_step * momentum_rows
        flow_out[t] = flow_next
        pack_out[t] = pack_next
        mass_out[t] = mass_now + mass_change
        momentum_out[t] = momentum_now - momentum_change
        flow_change, pack_change = flow_next - flow_now, pack_next - pack_now
        primal_sq = primal_sq + folded(flow_change * flow_change + pack_change * pack_change)
        dual_sq = dual_sq + folded(
            mass_change * mass_change + momentum_change * momentum_change
        )
        message[t * segs : (t + 1) * segs, :] = sz.share * exact_product(pack_bar, onehot, NT)
        rows = pl.ds(pl.multiple_of(t * segs + block * sz.chunk, sz.chunk), sz.chunk)
        message[rows, :] = message[rows, :] - target[t]
        earlier_bar = pack_bar

    at = message.shape[0] - SUBLANES
    message[at:, :] = jnp.zeros((SUBLANES, LANES), jnp.float32)
    message[at : at + 1, :] = jnp.sum(primal_sq, axis=0, keepdims=True)
    message[at + 1 : at + 2, :] = jnp.sum(dual_sq, axis=0, keepdims=True)


def write_next(sz, hour, first_seg, outs, cost, resistance, message, hour_messages):
    flow, pack, mass, momentum = outs
    last = sz.segs - 1
    firsts = [mass[t, 0:1, :] for t in range(sz.hours)]
    gaps = [
        cost[t, last : last + 1, :]
        - mass[t, last : last + 1, :]
        - resistance[last : last + 1, :] * momentum[t, last : last + 1, :]
        for t in range(sz.hours)
    ]
    rows = [jnp.where(first_seg, a, b) for a, b in zip(firsts, gaps)]
    write_ends(sz, message, sz.sums, rows)
    end = sz.hours - 1
    write_layers(sz, hour_messages, hour == 0, None, mass[end], momentum[end], mass[0])


def step_kernel(sz, iteration, final, *refs):
    take = taker(refs)
    first = iteration == 0
    state, data = take(4), take(2)
    friction, onehots, earlier_onehot, target, spread = take(5)
    corner_scalars = take(1) if sz.paired and not first else []
    seg_in, hours_in, duals_in = take(1)[0], take(1 if sz.paired else 2), take(1)[0]
    known = [] if first else take(3)
    old_weight = take(1)[0][0:1, 0:1] if iteration > 1 else 1.0
    scalars = [] if first else take(1)
    outs, message = take(4), take(1)[0]
    weight_out = [] if first else take(1)
    kept = [None] * 3 if final else take(3)
    hour_messages = [] if final else take(1 if sz.paired else 2)
    block, hour, first_seg = places()
    hours, segs = sz.hours, sz.segs
    weight = jnp.ones((1, 1), jnp.float32)
    if not first:
        total = scalars[0][0:1, :]
        if sz.paired:


            def sums_of(ref):
                parts = [ref[segs + part : segs + part + 1, :LANES] for part in (0, 1)]
                return jnp.concatenate(parts, axis=1)

            total = tree_sum(
                [
                    total,
                    seg_in[sz.seg_tail[False] : sz.seg_tail[False] + 1, : 2 * LANES],
                    sums_of(duals_in),
                sums_of(corner_scalars[0]),
                ]
            )
        weight = new_weight(old_weight, total)
        weight_out[0][...] = jnp.broadcast_to(weight, weight_out[0].shape)
    earlier_spread = sz.share * exact_product(duals_in[0:segs, :], earlier_onehot[...], NN)

    def spread_of(t):
        return spread[t], onehots[t]

    def edges(t):
        if not first:
            return known[0][t : t + 1, :], known[1][t : t + 1, :]
        shared, matched = [slot * hours + t for slot in (3, 4)]
        sent = seg_in[shared : shared + 1, :]
        return jnp.where(first_seg, seg_in[matched : matched + 1, :], sent), sent

    at = sz.seg_tail[first] + 1
    halo = {
        "seg": seg_in,
        "corner": seg_in[at : at + 1, :],
        "earlier": hours_in[0],
        "earlier_pack": hours_in[0][segs : 2 * segs, :] if first else known[2][...],
        "edges": edges,
        "later": hours_in[-1],
        "earlier_spread": earlier_spread,
    }
    resistance = friction[...]
    data = [*data, resistance, target]
    step(sz, block, hour, first_seg, weight, state, data, halo, spread_of, outs, message, kept)
    if not final:
        write_next(sz, hour, first_seg, outs, data[0], resistance, message, hour_messages)


def close_kernel(sz, *refs):
    take = taker(refs)
    messages = take_messages(sz, ITERS, take)
    old_duals, weight, written, duals, scalars = take(5)
    block, hour, first_seg = places()
    segs = sz.segs
    dual_step = STEP_SCALE * weight[0:1, 0:1]
    dual_sq = jnp.zeros((SUBLANES, LANES), jnp.float32)
    start = block * sz.chunk
    for t in range(sz.hours):
        totals = tree_sum([ref[t * segs : (t + 1) * segs, :] for ref in messages])
        change = dual_step * totals
        dual_sq = dual_sq + folded(change * change)
        own = pl.ds(pl.multiple_of(start, sz.chunk), sz.chunk)
        rows = pl.ds(pl.multiple_of(t * segs + start, sz.chunk), sz.chunk)
        own_totals = tree_sum([ref[rows, :] for ref in messages])
        duals[t] = old_duals[t, own, :] - dual_step * own_totals
    squares = [ref[sz.sums : sz.sums + SUBLANES, :] for ref in messages]
    write_squares(squares, dual_sq, scalars)


def written_out(state):
    count = len(state)

    def body(*refs):
        sources, targets, token, done = refs[:count], refs[count:-2], refs[-2], refs[-1]
        copies = [
            pltpu.make_async_copy(source, target, done.at[index])
            for index, (source, target) in enumerate(zip(sources, targets))
        ]
        for copy in copies:
            copy.start()
        token[...] = jnp.zeros(token.shape, jnp.float32)
        for copy in copies:
            copy.wait()

    return pl.pallas_call(
        body,
        out_shape=[pltpu.HBM(array.shape, array.dtype) for array in state]
        + [pltpu.VMEM((SUBLANES, LANES), jnp.float32)],
        in_specs=[pl.BlockSpec(memory_space=pltpu.VMEM) for _ in state],
        out_specs=[pl.BlockSpec(memory_space=pltpu.HBM) for _ in state]
        + [pl.BlockSpec(memory_space=pltpu.VMEM)],
        scratch_shapes=[pltpu.SemaphoreType.DMA((count,))],
        compiler_params=pltpu.CompilerParams(vmem_limit_bytes=VMEM_LIMIT),
    )(*state)


def weight_kernel(weight, *refs):
    *scalars, result = refs
    if len(scalars) == 4:
        own, *received = scalars
        by_distance = dict(zip(CORNER_ORDER, received))
        scalars = [own, by_distance[1], by_distance[2], by_distance[3]]
    result[...] = new_weight(weight[0:1, 0:1], tree_sum([ref[0:1, :] for ref in scalars]))


def gathered(sz, phase, message):
    return [message] + [swapped(message, "pipe", k) for k in sz.pipe_order(phase)]


def layers_exchanged(sz, hour_messages):
    if sz.paired:
        return [swapped(hour_messages[0], "hour", 1)]
    steps = range(sz.hour_parts - 1)
    return [
        lax.ppermute(hour_messages[0], "hour", [(i, i + 1) for i in steps]),
        lax.ppermute(hour_messages[1], "hour", [(i + 1, i) for i in steps]),
    ]


def on_device(
    segment_flow,
    linepack,
    mass_dual,
    momentum_dual,
    contract_dual,
    flow_cost,
    injection,
    contract_target,
    friction_table,
    friction_class,
    matching,
    contract_map,
):
    hours, segs, pipes = segment_flow.shape
    chunk, classes = contract_dual.shape[2:]
    sz = Sizes(hours, segs, pipes, chunk, classes, friction_table.shape[0])
    duals_now = contract_dual.reshape(hours, chunk, classes)
    target_now = contract_target.reshape(hours, chunk, classes)
    matching = matching.reshape(1, matching.shape[0])
    cells, contracts = (hours, segs, pipes), (hours, segs, classes)
    layer_shapes = [(segs + SUBLANES, pipes)]
    if not sz.paired:
        layer_shapes.append((segs, pipes))
    known_shapes = [(rounded_up(hours), pipes)] * 2 + [(segs, pipes)]
    scalars_shape = (SUBLANES, 2 * LANES)

    state = [segment_flow, linepack, mass_dual, momentum_dual]
    raw = [*state, flow_cost, friction_class, duals_now, contract_map, friction_table, matching]
    message, matching, *hour_messages = local_call(
        functools.partial(start_kernel, sz),
        [
            (sz.first_ends + sz.ends_packed(True), classes),
            matching.shape,
            (2 * segs + SUBLANES, pipes),
            *layer_shapes[1:],
        ],
        [("hbm", array) for array in raw],
        kept=True,
        scratch=start_scratch(sz),
        kinds={1: jnp.int32},
    )
    onehots, matches, friction = local_call(
        functools.partial(prepare_kernel, sz),
        [(hours, classes, pipes), (sz.blocks, pipes, pipes), (segs, pipes)],
        [("hbm", array) for array in (contract_map, friction_class, friction_table)]
        + vmem(matching),
        kept=True,
        scratch=prepare_scratch(sz),
        cost=pl.CostEstimate(flops=PREP_FLOPS, bytes_accessed=1 << 20, transcendentals=0),
        kinds={0: jnp.bfloat16, 1: jnp.bfloat16},
    )
    duals, weight, known, earlier_onehot = [], [], [], None
    for iteration in range(ITERS):
        first, final = iteration == 0, iteration == ITERS - 1
        messages = gathered(sz, iteration, message)
        hours_in = layers_exchanged(sz, hour_messages)
        seg_rows = rounded_up(sz.seg_tail[first] + 2)
        duals_rows = segs
        if sz.paired:
            duals_rows = max(segs + SUBLANES, seg_rows * sz.halves + SUBLANES)
        full_duals, duals_message, *scalars = local_call(
            functools.partial(duals_kernel, sz, iteration),
            [contracts, (duals_rows, classes)] + ([] if first else [scalars_shape]),
            vmem(*messages, friction, *duals, *weight),
            kept=True,
        )
        duals = [full_duals]
        args = vmem(*state, flow_cost, friction, onehots, matches)
        args += vmem(*messages, *hours_in, *duals, *scalars, *(hours_in[:1] if first else []))
        seg_message, spread, *built = local_call(
            functools.partial(spread_kernel, sz, iteration),
            [(seg_rows, pipes), cells] + ([(classes, pipes)] if first else []),
            args,
            kept=True,
            scratch=[pltpu.VMEM((sz.end_rows[first], pipes), jnp.float32)],
            kinds={2: jnp.bfloat16},
        )
        earlier_onehot = built[0] if first else earlier_onehot
        seg_in = swapped(seg_message, "seg", 1)
        if sz.paired:
            duals_in = swapped(duals_message, "hour", 1)
            corner_in = [swapped(duals_message, ("hour", "seg"), 3) for part in scalars]
        else:
            steps = range(sz.hour_parts - 1)
            duals_in = lax.ppermute(duals_message, "hour", [(i, i + 1) for i in steps])
            scalars = [lax.psum(part, ("hour", "seg")) for part in scalars]
            corner_in = []
        args = vmem(
            *state, flow_cost, injection, friction, onehots, earlier_onehot, target_now, spread
        )
        args += vmem(*corner_in, seg_in, *hours_in, duals_in, *known, *weight, *scalars)
        message_rows = sz.sums + SUBLANES + (0 if final else sz.ends_packed(False))
        outs = [cells] * 4 + [(message_rows, classes)]
        outs += [] if first else [(SUBLANES, LANES)]
        results = local_call(
            functools.partial(step_kernel, sz, iteration, final),
            outs + ([] if final else known_shapes + layer_shapes),
            args,
            kept=True,
        )
        state, message, rest = results[:4], results[4], results[5:]
        weight, rest = ([], rest) if first else (rest[:1], rest[1:])
        known, hour_messages = rest[:3], rest[3:]
    *state, written = written_out(state)
    contract_out, scalars = local_call(
        functools.partial(close_kernel, sz),
        [(hours, chunk, classes), scalars_shape],
        vmem(*gathered(sz, ITERS, message), *duals, *weight, written),
        kept=True,
    )
    if sz.paired:
        sums = [scalars] + [swapped(scalars, ("hour", "seg"), k) for k in CORNER_ORDER]
    else:
        sums = [lax.psum(scalars, ("hour", "seg"))]
    (weight,) = local_call(weight_kernel, [(1, 1)], vmem(*weight, *sums))
    return (
        *state,
        contract_out.reshape(contract_dual.shape),
        weight.reshape(1),
    )


def solution(mesh):
    cells = P(("groups", "hour"), "seg", "pipe")
    contracts = P(("groups", "hour"), "seg", "pipe", None)
    return jax.shard_map(
        on_device,
        mesh=mesh,
        in_specs=(
            cells,
            cells,
            cells,
            cells,
            contracts,
            cells,
            cells,
            contracts,
            P(),
            P("seg", ("groups", "pipe")),
            P("groups"),
            P(("groups", "hour"), None),
        ),
        out_specs=(cells, cells, cells, cells, contracts, P("groups")),
        check_vma=False,
    )
```

```python
import functools

import jax
import jax.numpy as jnp
from jax import lax
from jax.experimental import pallas as pl
from jax.experimental.pallas import tpu as pltpu
from jax.sharding import PartitionSpec as P

ITERS = 2

FLOW_CAP = 1.5
PACK_CAP = 2.5
STEP_SCALE = 0.25
NORM_EPS = 1e-06

LANES = 128
PREP_FLOPS = 1 << 30
SUBLANES = 8
VMEM_LIMIT = 8 * 1024 * 1024
CORNER_ORDER = (1, 2, 3)
PIPE_ORDERS = ((1, 3, 2), (2, 1, 3), (2, 1, 3))
NT = (((1,), (1,)), ((), ()))
NN = (((1,), (0,)), ((), ()))


def rounded_up(count):
    return -(-count // SUBLANES) * SUBLANES


def local_call(body, outs, args, kept=False, scratch=(), kinds={}, cost=None):
    spaces = {"smem": pltpu.SMEM, "vmem": pltpu.VMEM, "hbm": pltpu.HBM}
    shape_of = pltpu.VMEM if kept else jax.ShapeDtypeStruct
    arrays = [
        pltpu.with_memory_space_constraint(array, pltpu.HBM) if space == "hbm" else array
        for space, array in args
    ]
    results = pl.pallas_call(
        body,
        out_shape=[shape_of(shape, kinds.get(index, jnp.float32)) for index, shape in enumerate(outs)],
        in_specs=[pl.BlockSpec(memory_space=spaces[space]) for space, _ in args],
        out_specs=[pl.BlockSpec(memory_space=pltpu.VMEM) for _ in outs],
        scratch_shapes=scratch,
        compiler_params=pltpu.CompilerParams(vmem_limit_bytes=VMEM_LIMIT),
        cost_estimate=cost,
    )(*arrays)
    return list(results)


def vmem(*arrays):
    return [("vmem", array) for array in arrays]


def taker(refs):
    refs = list(refs)

    def take(count):
        return [refs.pop(0) for _ in range(count)]

    return take


def parts_of(values):
    high = values.astype(jnp.bfloat16).astype(jnp.float32)
    rest = values - high
    middle = rest.astype(jnp.bfloat16).astype(jnp.float32)
    return jnp.concatenate([high, middle, rest - middle], axis=0).astype(jnp.bfloat16)


def exact_product(values, onehot, dims):
    rows = values.shape[0]
    product = lax.dot_general(
        parts_of(values), onehot, dims, preferred_element_type=jnp.float32
    )
    return product[:rows] + product[rows : 2 * rows] + product[2 * rows :]


def as_onehot(mask):
    return jnp.where(mask, 1.0, 0.0).astype(jnp.bfloat16)


def contract_onehot(map_row, class_count):
    shape = (class_count, map_row.shape[1])
    return as_onehot(lax.broadcasted_iota(jnp.int32, shape, 0) == map_row)


def friction_of(classes, table_ref, levels):
    friction = jnp.zeros(classes.shape, jnp.float32)
    for level in range(levels):
        friction = jnp.where(classes == level, table_ref[level], friction)
    return friction


def folded(values):
    rows, width = values.shape
    total = values[:SUBLANES]
    for start in range(SUBLANES, rows, SUBLANES):
        total = total + values[start : start + SUBLANES]
    result = total[:, :LANES]
    for start in range(LANES, width, LANES):
        result = result + total[:, start : start + LANES]
    return result


def tree_sum(terms):
    while len(terms) > 1:
        terms = [a + b for a, b in zip(terms[0::2], terms[1::2])]
    return terms[0]


def swapped(message, axes, distance):
    count = lax.axis_size(axes)
    return lax.ppermute(message, axes, [(i, i ^ distance) for i in range(count)])


class Sizes:
    def __init__(self, hours, segs, pipes, chunk, classes, levels):
        self.hours, self.segs, self.pipes = hours, segs, pipes
        self.chunk, self.classes, self.levels = chunk, classes, levels
        self.blocks = lax.axis_size("pipe")
        self.hour_parts = lax.axis_size("hour")
        self.share = classes / (pipes * self.blocks)
        self.halves = pipes // LANES
        self.paired = self.hour_parts == 2
        self.end_rows = {True: 2 * hours, False: hours}
        self.sums = hours * segs
        self.first_ends = rounded_up(hours * chunk)
        self.seg_tail = {True: 5 * hours, False: 3 * hours}

    def owner(self, block, index):
        return lax.bitwise_xor(block, index)

    def pipe_order(self, phase):
        return PIPE_ORDERS[phase] if self.blocks == 4 else range(1, self.blocks)

    def ends_packed(self, first):
        return rounded_up(self.end_rows[first] * self.halves)

    def own_pipes(self, block):
        return pl.ds(pl.multiple_of(block * self.pipes, LANES), self.pipes)


def take_messages(sz, phase, take):
    own, *received = take(sz.blocks)
    by_distance = dict(zip(sz.pipe_order(phase), received))
    return [own] + [by_distance[distance] for distance in range(1, sz.blocks)]


def places():
    return lax.axis_index("pipe"), lax.axis_index("hour"), lax.axis_index("seg") == 0


def write_ends(sz, message, start, rows):
    for index, row in enumerate(rows):
        for half in range(sz.halves):
            at = start + half * len(rows) + index
            message[at : at + 1, :] = row[:, half * LANES : (half + 1) * LANES]


def read_ends(sz, message, start, count):
    pieces = [
        message[start + half * count : start + (half + 1) * count, :]
        for half in range(sz.halves)
    ]
    return jnp.concatenate(pieces, axis=1)


def write_edges(sz, message, first, first_seg, state, cost, resistance, spread, found):
    flow, pack, mass, momentum = state
    hours, last = sz.hours, sz.segs - 1
    top, bottom = slice(0, 1), slice(last, last + 1)
    for t in range(hours):
        gap = cost[t, bottom, :] - mass[t, bottom, :] - resistance * momentum[t, bottom, :]
        gradient = mass[t, top, :] - momentum[t, top, :] + spread[t, top, :]
        matched = found[t : t + 1, :]
        rows = [
            jnp.where(first_seg, matched, mass[t, top, :]),
            jnp.where(first_seg, momentum[t, bottom, :], gradient),
            jnp.where(first_seg, gap, matched),
        ]
        if first:
            rows.append(jnp.where(first_seg, flow[t, bottom, :], pack[t, top, :]))
            rows.append(found[hours + t : hours + t + 1, :])
        for slot, row in enumerate(rows):
            at = slot * hours + t
            message[at : at + 1, :] = row


def write_layers(sz, outs, first_hour, pack, mass, momentum, first_mass):
    segs = sz.segs
    top = lax.broadcasted_iota(jnp.int32, (segs, sz.pipes), 0) == 0
    gradient = mass - momentum + jnp.where(top, 0.0, pltpu.roll(momentum, 1, 0))
    if sz.paired:
        outs[0][0:segs, :] = jnp.where(first_hour, gradient, first_mass)
    else:
        outs[0][0:segs, :] = gradient
        outs[1][...] = first_mass
    if pack is not None:
        outs[0][segs : 2 * segs, :] = pack
    tail = outs[0].shape[0] - SUBLANES
    outs[0][tail:, :] = jnp.zeros((SUBLANES, sz.pipes), jnp.float32)
    outs[0][tail : tail + 1, :] = momentum[segs - 1 : segs, :]


def match_onehots(sz, block, inlet_side, matching, result):
    row = lax.broadcasted_iota(jnp.int32, (sz.pipes, sz.pipes), 0)

    @pl.when(inlet_side)
    def _():
        own = matching[0:1, sz.own_pipes(block)]
        for index in range(sz.blocks):
            result[index] = as_onehot(row + sz.owner(block, index) * sz.pipes == own)

    @pl.when(jnp.logical_not(inlet_side))
    def _():
        here = row + block * sz.pipes
        for index in range(sz.blocks):
            feeds = matching[0:1, sz.own_pipes(sz.owner(block, index))]
            result[index] = as_onehot(here == feeds)


def matched_rows(sz, inlet_side, ends, onehots, found):
    for side, dims in ((inlet_side, NN), (jnp.logical_not(inlet_side), NT)):

        @pl.when(side)
        def _(dims=dims):
            result = jnp.zeros(found.shape, jnp.float32)
            for index, values in enumerate(ends):
                result = result + exact_product(values, onehots[index], dims)
            found[...] = result


def prepare_kernel(sz, *refs):
    contract_map_in, classes_in, table_in, matching = refs[:4]
    onehots, matches, friction = refs[4:7]
    contract_map, classes, table, arrived = refs[7:]
    block, hour, first_seg = places()
    pairs = [
        (contract_map_in.at[:, sz.own_pipes(block)], contract_map),
        (classes_in, classes),
        (table_in, table),
    ]
    copies = [
        pltpu.make_async_copy(source, target, arrived.at[index])
        for index, (source, target) in enumerate(pairs)
    ]
    for copy in copies:
        copy.start()
    match_onehots(sz, block, jnp.logical_not(first_seg), matching, matches)
    for copy in copies:
        copy.wait()
    for t in range(sz.hours):
        onehots[t] = contract_onehot(contract_map[t : t + 1, :], sz.classes)
    friction[...] = friction_of(classes[...], table, sz.levels)


def prepare_scratch(sz):
    return [
        pltpu.VMEM((sz.hours, sz.pipes), jnp.int32),
        pltpu.VMEM((sz.segs, sz.pipes), jnp.int32),
        pltpu.SMEM((sz.levels,), jnp.float32),
        pltpu.SemaphoreType.DMA((3,)),
    ]


def start_kernel(sz, *refs):
    take = taker(refs)
    flow, mass, momentum, cost, classes_in, duals_in, table_in, matching_in = take(8)
    message, matching = take(2)
    flow_last, cost_last, mass_last, momentum_last, mass_first = take(5)
    duals, classes, table, arrived = take(4)
    block, hour, first_seg = places()
    hours, segs = sz.hours, sz.segs
    low, high = pl.ds(0, SUBLANES), pl.ds(segs - SUBLANES, SUBLANES)
    copies = [
        (flow.at[:, high], flow_last),
        (cost.at[:, high], cost_last),
        (mass.at[:, high], mass_last),
        (momentum.at[:, high], momentum_last),
        (mass.at[:, low], mass_first),
        (duals_in, duals),
        (classes_in.at[high], classes),
        (table_in, table),
        (matching_in, matching),
    ]
    copies = [
        pltpu.make_async_copy(source, target, arrived.at[index])
        for index, (source, target) in enumerate(copies)
    ]
    for copy in copies:
        copy.start()
    for copy in copies:
        copy.wait()
    end = SUBLANES - 1
    resistance = friction_of(classes[...], table, sz.levels)[end:]
    firsts = [mass_first[t, 0:1, :] for t in range(hours)]
    lasts = [flow_last[t, end : end + 1, :] for t in range(hours)]
    gaps = [
        cost_last[t, end : end + 1, :]
        - mass_last[t, end : end + 1, :]
        - resistance * momentum_last[t, end : end + 1, :]
        for t in range(hours)
    ]
    for t in range(hours):
        message[t * sz.chunk : (t + 1) * sz.chunk, :] = duals[t]
    rows = [jnp.where(first_seg, a, b) for a, b in zip(firsts + firsts, gaps + lasts)]
    write_ends(sz, message, sz.first_ends, rows)


def layers_kernel(sz, *refs):
    take = taker(refs)
    pack, mass, momentum, contract_map, started = take(5)
    block, hour, first_seg = places()
    end = sz.hours - 1
    write_layers(sz, refs[5:], hour == 0, pack[end], mass[end], momentum[end], mass[0])
    map_row = contract_map[end : end + 1, sz.own_pipes(block)].astype(jnp.float32)
    tail = refs[5].shape[0] - SUBLANES
    refs[5][tail + 1 : tail + 2, :] = map_row


def start_scratch(sz):
    ends = pltpu.VMEM((sz.hours, SUBLANES, sz.pipes), jnp.float32)
    return [ends] * 5 + [
        pltpu.VMEM((sz.hours, sz.chunk, sz.classes), jnp.float32),
        pltpu.VMEM((SUBLANES, sz.pipes), jnp.int32),
        pltpu.SMEM((sz.levels,), jnp.float32),
        pltpu.SemaphoreType.DMA((9,)),
    ]


def duals_kernel(sz, iteration, *refs):
    take = taker(refs)
    first = iteration == 0
    messages = take_messages(sz, iteration, take)
    prepared = take(1)
    old_duals = None if first else take(1)[0]
    old_weight = take(1)[0][0:1, 0:1] if iteration > 1 else 1.0
    duals, hour_message = take(2)
    scalars = None if first else take(1)[0]
    block = places()[0]
    hours, segs, chunk = sz.hours, sz.segs, sz.chunk
    if first:
        for index, ref in enumerate(messages):
            owner = sz.owner(block, index)
            rows = pl.ds(pl.multiple_of(owner * chunk, chunk), chunk)
            for t in range(hours):
                duals[t, rows, :] = ref[t * chunk : (t + 1) * chunk, :]
    else:
        dual_step = STEP_SCALE * old_weight
        dual_sq = jnp.zeros((SUBLANES, LANES), jnp.float32)
        for t in range(hours):
            totals = tree_sum([ref[t * segs : (t + 1) * segs, :] for ref in messages])
            change = dual_step * totals
            duals[t] = old_duals[t] - change
            dual_sq = dual_sq + folded(change * change)
        at = sz.sums + sz.ends_packed(False)
        write_squares([ref[at : at + SUBLANES, :] for ref in messages], dual_sq, scalars)
    hour_message[0:segs, :] = duals[hours - 1]
    if sz.paired:
        rest = (hour_message.shape[0] - segs, sz.classes)
        hour_message[segs:, :] = jnp.zeros(rest, jnp.float32)
    if sz.paired and not first:
        for part in (0, 1):
            at = segs + part
            hour_message[at : at + 1, :LANES] = scalars[0:1, part * LANES : (part + 1) * LANES]


def spread_kernel(sz, iteration, *refs):
    take = taker(refs)
    first = iteration == 0
    flow, pack, mass, momentum, cost, friction, onehots, matches = take(8)
    messages = take_messages(sz, iteration, take)
    hours_in = take(1 if sz.paired else 2)
    duals = take(1)[0]
    scalars = None if first else take(1)[0]
    map_in = take(1)[0] if first else None
    seg_message, spread = take(2)
    earlier_onehot = take(1)[0] if first else None
    found = take(1)[0]
    earlier_in, later_in = hours_in[0], hours_in[-1]
    block, hour, first_seg = places()
    hours, segs = sz.hours, sz.segs
    last = segs - 1

    ends_at, count = sz.first_ends if first else sz.sums, sz.end_rows[first]
    ends = [read_ends(sz, ref, ends_at, count) for ref in messages]
    matched_rows(sz, jnp.logical_not(first_seg), ends, matches, found)
    for t in range(hours):
        spread[t] = sz.share * exact_product(duals[t], onehots[t], NN)
    if first:
        tail = map_in.shape[0] - SUBLANES
        map_row = map_in[tail + 1 : tail + 2, :].astype(jnp.int32)
        earlier_onehot[...] = contract_onehot(map_row, sz.classes)

    state = (flow, pack, mass, momentum)
    resistance = friction[last:segs, :]
    write_edges(sz, seg_message, first, first_seg, state, cost, resistance, spread, found)
    at = sz.seg_tail[first]
    seg_message[at:, :] = jnp.zeros((seg_message.shape[0] - at, sz.pipes), jnp.float32)
    if not first:
        seg_message[at : at + 1, : 2 * LANES] = scalars[0:1, :]
    tail = earlier_in.shape[0] - SUBLANES
    seg_message[at + 1 : at + 2, :] = jnp.where(
        first_seg, earlier_in[tail : tail + 1, :], later_in[0:1, :]
    )


def write_squares(squares, dual_sq, scalars):
    total = tree_sum(squares)
    scalars[...] = jnp.zeros(scalars.shape, jnp.float32)
    scalars[0:1, :LANES] = total[0:1]
    scalars[0:1, LANES:] = total[1:2] + jnp.sum(dual_sq, axis=0, keepdims=True)


def new_weight(weight, total):
    primal = jnp.sum(total[:, :LANES], axis=1, keepdims=True)
    dual = jnp.sum(total[:, LANES : 2 * LANES], axis=1, keepdims=True)
    return jnp.sqrt(weight * jnp.sqrt((dual + NORM_EPS) / (primal + NORM_EPS)))


def step(sz, block, hour, first_seg, weight, state, data, halo, spread_of, outs, message, kept):
    flow, pack, mass, momentum = state
    cost, injection, resistance, target = data
    flow_out, pack_out, mass_out, momentum_out = outs
    edge_flow_out, edge_pack_out, earlier_pack_out = kept
    hours, segs, pipes = sz.hours, sz.segs, sz.pipes
    last, end = segs - 1, hours - 1
    has_earlier = hour > 0
    has_later = hour < sz.hour_parts - 1
    primal_step = STEP_SCALE / weight
    dual_step = STEP_SCALE * weight

    row_index = lax.broadcasted_iota(jnp.int32, (segs, pipes), 0)
    top, bottom = row_index == 0, row_index == last

    def from_above(values, row):
        return jnp.where(top, row, pltpu.roll(values, 1, 0))

    def from_below(values, row):
        return jnp.where(bottom, row, pltpu.roll(values, segs - 1, 0))

    def seg_row(slot, t):
        at = slot * hours + t
        return halo["seg"][at : at + 1, :]

    def new_flow(start, gap):
        return jnp.clip(start - primal_step * gap, -FLOW_CAP, FLOW_CAP)

    def new_pack(start, gradient):
        return jnp.clip(start + primal_step * gradient, 0.0, PACK_CAP)

    corner = halo["corner"]
    earlier_pack = halo["earlier_pack"]
    earlier_gradient = (
        halo["earlier"][0:segs, :]
        + halo["earlier_spread"]
        + jnp.where(top, jnp.where(first_seg, 0.0, corner), 0.0)
        - mass[0]
    )
    earlier_next = new_pack(earlier_pack, earlier_gradient)
    earlier_bar = jnp.where(has_earlier, 2.0 * earlier_next - earlier_pack, 0.0)
    if earlier_pack_out is not None:
        earlier_pack_out[...] = earlier_next
    later_mass = jnp.where(has_later, halo["later"][0:segs, :], 0.0)
    later_corner = jnp.where(has_later, corner, 0.0)
    primal_sq = jnp.zeros((SUBLANES, LANES), jnp.float32)
    dual_sq = jnp.zeros((SUBLANES, LANES), jnp.float32)
    for t in range(hours):
        mass_now, momentum_now = mass[t], momentum[t]
        flow_now, pack_now = flow[t], pack[t]
        spread, onehot = spread_of(t)
        below_mass = seg_row(0, t)
        next_mass = mass[t + 1] if t < end else later_mass
        gap = cost[t] - (
            mass_now - from_below(mass_now, below_mass) + resistance * momentum_now
        )
        flow_next = new_flow(flow_now, gap)
        above_momentum = jnp.where(first_seg, 0.0, seg_row(1, t))
        gradient = (
            mass_now
            - next_mass
            - momentum_now
            + from_above(momentum_now, above_momentum)
            + spread
        )
        pack_next = new_pack(pack_now, gradient)
        flow_bar = 2.0 * flow_next - flow_now
        pack_bar = 2.0 * pack_next - pack_now

        edge_flow, edge_pack = halo["edges"](t)
        edge_gap = seg_row(2, t) + mass_now[0:1, :]
        edge_flow_next = new_flow(edge_flow, edge_gap)
        edge_flow_bar = 2.0 * edge_flow_next - edge_flow
        edge_later = seg_row(0, t + 1) if t < end else later_corner
        edge_gradient = seg_row(1, t) + momentum_now[last : last + 1, :] - edge_later
        edge_pack_next = new_pack(edge_pack, edge_gradient)
        edge_pack_bar = jnp.where(first_seg, 2.0 * edge_pack_next - edge_pack, 0.0)
        if edge_flow_out is not None:
            edge_flow_out[t : t + 1, :] = edge_flow_next
            edge_pack_out[t : t + 1, :] = edge_pack_next

        mass_rows = pack_bar - earlier_bar + flow_bar - from_above(flow_bar, edge_flow_bar)
        momentum_rows = resistance * flow_bar - (pack_bar - from_below(pack_bar, edge_pack_bar))
        mass_change = dual_step * (injection[t] - mass_rows)
        momentum_change = dual_step * momentum_rows
        flow_out[t] = flow_next
        pack_out[t] = pack_next
        mass_out[t] = mass_now + mass_change
        momentum_out[t] = momentum_now - momentum_change
        flow_change, pack_change = flow_next - flow_now, pack_next - pack_now
        primal_sq = primal_sq + folded(flow_change * flow_change + pack_change * pack_change)
        dual_sq = dual_sq + folded(
            mass_change * mass_change + momentum_change * momentum_change
        )
        message[t * segs : (t + 1) * segs, :] = sz.share * exact_product(pack_bar, onehot, NT)
        rows = pl.ds(pl.multiple_of(t * segs + block * sz.chunk, sz.chunk), sz.chunk)
        message[rows, :] = message[rows, :] - target[t]
        earlier_bar = pack_bar

    at = message.shape[0] - SUBLANES
    message[at:, :] = jnp.zeros((SUBLANES, LANES), jnp.float32)
    message[at : at + 1, :] = jnp.sum(primal_sq, axis=0, keepdims=True)
    message[at + 1 : at + 2, :] = jnp.sum(dual_sq, axis=0, keepdims=True)


def write_next(sz, hour, first_seg, outs, cost, resistance, message, hour_messages):
    flow, pack, mass, momentum = outs
    last = sz.segs - 1
    firsts = [mass[t, 0:1, :] for t in range(sz.hours)]
    gaps = [
        cost[t, last : last + 1, :]
        - mass[t, last : last + 1, :]
        - resistance[last : last + 1, :] * momentum[t, last : last + 1, :]
        for t in range(sz.hours)
    ]
    rows = [jnp.where(first_seg, a, b) for a, b in zip(firsts, gaps)]
    write_ends(sz, message, sz.sums, rows)
    end = sz.hours - 1
    write_layers(sz, hour_messages, hour == 0, None, mass[end], momentum[end], mass[0])


def step_kernel(sz, iteration, final, *refs):
    take = taker(refs)
    first = iteration == 0
    state, data = take(4), take(2)
    friction, onehots, earlier_onehot, target, spread = take(5)
    corner_scalars = take(1) if sz.paired and not first else []
    seg_in, hours_in, duals_in = take(1)[0], take(1 if sz.paired else 2), take(1)[0]
    known = [] if first else take(3)
    old_weight = take(1)[0][0:1, 0:1] if iteration > 1 else 1.0
    scalars = [] if first else take(1)
    outs, message = take(4), take(1)[0]
    weight_out = [] if first else take(1)
    kept = [None] * 3 if final else take(3)
    hour_messages = [] if final else take(1 if sz.paired else 2)
    block, hour, first_seg = places()
    hours, segs = sz.hours, sz.segs
    weight = jnp.ones((1, 1), jnp.float32)
    if not first:
        total = scalars[0][0:1, :]
        if sz.paired:


            def sums_of(ref):
                parts = [ref[segs + part : segs + part + 1, :LANES] for part in (0, 1)]
                return jnp.concatenate(parts, axis=1)

            total = tree_sum(
                [
                    total,
                    seg_in[sz.seg_tail[False] : sz.seg_tail[False] + 1, : 2 * LANES],
                    sums_of(duals_in),
                sums_of(corner_scalars[0]),
                ]
            )
        weight = new_weight(old_weight, total)
        weight_out[0][...] = jnp.broadcast_to(weight, weight_out[0].shape)
    earlier_spread = sz.share * exact_product(duals_in[0:segs, :], earlier_onehot[...], NN)

    def spread_of(t):
        return spread[t], onehots[t]

    def edges(t):
        if not first:
            return known[0][t : t + 1, :], known[1][t : t + 1, :]
        shared, matched = [slot * hours + t for slot in (3, 4)]
        sent = seg_in[shared : shared + 1, :]
        return jnp.where(first_seg, seg_in[matched : matched + 1, :], sent), sent

    at = sz.seg_tail[first] + 1
    halo = {
        "seg": seg_in,
        "corner": seg_in[at : at + 1, :],
        "earlier": hours_in[0],
        "earlier_pack": hours_in[0][segs : 2 * segs, :] if first else known[2][...],
        "edges": edges,
        "later": hours_in[-1],
        "earlier_spread": earlier_spread,
    }
    resistance = friction[...]
    data = [*data, resistance, target]
    step(sz, block, hour, first_seg, weight, state, data, halo, spread_of, outs, message, kept)
    if not final:
        write_next(sz, hour, first_seg, outs, data[0], resistance, message, hour_messages)


def close_kernel(sz, *refs):
    take = taker(refs)
    messages = take_messages(sz, ITERS, take)
    old_duals, weight, written, duals, scalars = take(5)
    block, hour, first_seg = places()
    segs = sz.segs
    dual_step = STEP_SCALE * weight[0:1, 0:1]
    dual_sq = jnp.zeros((SUBLANES, LANES), jnp.float32)
    start = block * sz.chunk
    for t in range(sz.hours):
        totals = tree_sum([ref[t * segs : (t + 1) * segs, :] for ref in messages])
        change = dual_step * totals
        dual_sq = dual_sq + folded(change * change)
        own = pl.ds(pl.multiple_of(start, sz.chunk), sz.chunk)
        rows = pl.ds(pl.multiple_of(t * segs + start, sz.chunk), sz.chunk)
        own_totals = tree_sum([ref[rows, :] for ref in messages])
        duals[t] = old_duals[t, own, :] - dual_step * own_totals
    squares = [ref[sz.sums : sz.sums + SUBLANES, :] for ref in messages]
    write_squares(squares, dual_sq, scalars)


def written_out(state):
    count = len(state)

    def body(*refs):
        sources, targets, token, done = refs[:count], refs[count:-2], refs[-2], refs[-1]
        copies = [
            pltpu.make_async_copy(source, target, done.at[index])
            for index, (source, target) in enumerate(zip(sources, targets))
        ]
        for copy in copies:
            copy.start()
        token[...] = jnp.zeros(token.shape, jnp.float32)
        for copy in copies:
            copy.wait()

    return pl.pallas_call(
        body,
        out_shape=[pltpu.HBM(array.shape, array.dtype) for array in state]
        + [pltpu.VMEM((SUBLANES, LANES), jnp.float32)],
        in_specs=[pl.BlockSpec(memory_space=pltpu.VMEM) for _ in state],
        out_specs=[pl.BlockSpec(memory_space=pltpu.HBM) for _ in state]
        + [pl.BlockSpec(memory_space=pltpu.VMEM)],
        scratch_shapes=[pltpu.SemaphoreType.DMA((count,))],
        compiler_params=pltpu.CompilerParams(vmem_limit_bytes=VMEM_LIMIT),
    )(*state)


def weight_kernel(weight, *refs):
    *scalars, result = refs
    if len(scalars) == 4:
        own, *received = scalars
        by_distance = dict(zip(CORNER_ORDER, received))
        scalars = [own, by_distance[1], by_distance[2], by_distance[3]]
    result[...] = new_weight(weight[0:1, 0:1], tree_sum([ref[0:1, :] for ref in scalars]))


def gathered(sz, phase, message):
    return [message] + [swapped(message, "pipe", k) for k in sz.pipe_order(phase)]


def layers_exchanged(sz, hour_messages):
    if sz.paired:
        return [swapped(hour_messages[0], "hour", 1)]
    steps = range(sz.hour_parts - 1)
    return [
        lax.ppermute(hour_messages[0], "hour", [(i, i + 1) for i in steps]),
        lax.ppermute(hour_messages[1], "hour", [(i + 1, i) for i in steps]),
    ]


def on_device(
    segment_flow,
    linepack,
    mass_dual,
    momentum_dual,
    contract_dual,
    flow_cost,
    injection,
    contract_target,
    friction_table,
    friction_class,
    matching,
    contract_map,
):
    hours, segs, pipes = segment_flow.shape
    chunk, classes = contract_dual.shape[2:]
    sz = Sizes(hours, segs, pipes, chunk, classes, friction_table.shape[0])
    duals_now = contract_dual.reshape(hours, chunk, classes)
    target_now = contract_target.reshape(hours, chunk, classes)
    matching = matching.reshape(1, matching.shape[0])
    cells, contracts = (hours, segs, pipes), (hours, segs, classes)
    layer_shapes = [(segs + SUBLANES, pipes)]
    if not sz.paired:
        layer_shapes.append((segs, pipes))
    known_shapes = [(rounded_up(hours), pipes)] * 2 + [(segs, pipes)]
    scalars_shape = (SUBLANES, 2 * LANES)

    state = [segment_flow, linepack, mass_dual, momentum_dual]
    raw = [segment_flow, mass_dual, momentum_dual, flow_cost, friction_class, duals_now]
    raw += [friction_table, matching]
    message, matching = local_call(
        functools.partial(start_kernel, sz),
        [
            (sz.first_ends + sz.ends_packed(True), classes),
            matching.shape,
        ],
        [("hbm", array) for array in raw],
        kept=True,
        scratch=start_scratch(sz),
        kinds={1: jnp.int32},
    )
    hour_messages = local_call(
        functools.partial(layers_kernel, sz),
        [(2 * segs + SUBLANES, pipes), *layer_shapes[1:]],
        vmem(linepack, mass_dual, momentum_dual, contract_map, matching),
        kept=True,
    )
    onehots, matches, friction = local_call(
        functools.partial(prepare_kernel, sz),
        [(hours, classes, pipes), (sz.blocks, pipes, pipes), (segs, pipes)],
        [("hbm", array) for array in (contract_map, friction_class, friction_table)]
        + vmem(matching),
        kept=True,
        scratch=prepare_scratch(sz),
        cost=pl.CostEstimate(flops=PREP_FLOPS, bytes_accessed=1 << 20, transcendentals=0),
        kinds={0: jnp.bfloat16, 1: jnp.bfloat16},
    )
    duals, weight, known, earlier_onehot = [], [], [], None
    for iteration in range(ITERS):
        first, final = iteration == 0, iteration == ITERS - 1
        messages = gathered(sz, iteration, message)
        hours_in = layers_exchanged(sz, hour_messages)
        seg_rows = rounded_up(sz.seg_tail[first] + 2)
        duals_rows = segs
        if sz.paired:
            duals_rows = max(segs + SUBLANES, seg_rows * sz.halves + SUBLANES)
        full_duals, duals_message, *scalars = local_call(
            functools.partial(duals_kernel, sz, iteration),
            [contracts, (duals_rows, classes)] + ([] if first else [scalars_shape]),
            vmem(*messages, friction, *duals, *weight),
            kept=True,
        )
        duals = [full_duals]
        args = vmem(*state, flow_cost, friction, onehots, matches)
        args += vmem(*messages, *hours_in, *duals, *scalars, *(hours_in[:1] if first else []))
        seg_message, spread, *built = local_call(
            functools.partial(spread_kernel, sz, iteration),
            [(seg_rows, pipes), cells] + ([(classes, pipes)] if first else []),
            args,
            kept=True,
            scratch=[pltpu.VMEM((sz.end_rows[first], pipes), jnp.float32)],
            kinds={2: jnp.bfloat16},
        )
        earlier_onehot = built[0] if first else earlier_onehot
        seg_in = swapped(seg_message, "seg", 1)
        if sz.paired:
            duals_in = swapped(duals_message, "hour", 1)
            corner_in = [swapped(duals_message, ("hour", "seg"), 3) for part in scalars]
        else:
            steps = range(sz.hour_parts - 1)
            duals_in = lax.ppermute(duals_message, "hour", [(i, i + 1) for i in steps])
            scalars = [lax.psum(part, ("hour", "seg")) for part in scalars]
            corner_in = []
        args = vmem(
            *state, flow_cost, injection, friction, onehots, earlier_onehot, target_now, spread
        )
        args += vmem(*corner_in, seg_in, *hours_in, duals_in, *known, *weight, *scalars)
        message_rows = sz.sums + SUBLANES + (0 if final else sz.ends_packed(False))
        outs = [cells] * 4 + [(message_rows, classes)]
        outs += [] if first else [(SUBLANES, LANES)]
        results = local_call(
            functools.partial(step_kernel, sz, iteration, final),
            outs + ([] if final else known_shapes + layer_shapes),
            args,
            kept=True,
        )
        state, message, rest = results[:4], results[4], results[5:]
        weight, rest = ([], rest) if first else (rest[:1], rest[1:])
        known, hour_messages = rest[:3], rest[3:]
    *state, written = written_out(state)
    contract_out, scalars = local_call(
        functools.partial(close_kernel, sz),
        [(hours, chunk, classes), scalars_shape],
        vmem(*gathered(sz, ITERS, message), *duals, *weight, written),
        kept=True,
    )
    if sz.paired:
        sums = [scalars] + [swapped(scalars, ("hour", "seg"), k) for k in CORNER_ORDER]
    else:
        sums = [lax.psum(scalars, ("hour", "seg"))]
    (weight,) = local_call(weight_kernel, [(1, 1)], vmem(*weight, *sums))
    return (
        *state,
        contract_out.reshape(contract_dual.shape),
        weight.reshape(1),
    )


def solution(mesh):
    cells = P(("groups", "hour"), "seg", "pipe")
    contracts = P(("groups", "hour"), "seg", "pipe", None)
    return jax.shard_map(
        on_device,
        mesh=mesh,
        in_specs=(
            cells,
            cells,
            cells,
            cells,
            contracts,
            cells,
            cells,
            contracts,
            P(),
            P("seg", ("groups", "pipe")),
            P("groups"),
            P(("groups", "hour"), None),
        ),
        out_specs=(cells, cells, cells, cells, contracts, P("groups")),
        check_vma=False,
    )
```

```python
import functools

import jax
import jax.numpy as jnp
from jax import lax
from jax.experimental import pallas as pl
from jax.experimental.pallas import tpu as pltpu
from jax.sharding import PartitionSpec as P

ITERS = 2

FLOW_CAP = 1.5
PACK_CAP = 2.5
STEP_SCALE = 0.25
NORM_EPS = 1e-06

LANES = 128
PREP_FLOPS = 1 << 30
SUBLANES = 8
VMEM_LIMIT = 8 * 1024 * 1024
CORNER_ORDER = (1, 2, 3)
PIPE_ORDERS = ((1, 3, 2), (2, 1, 3), (2, 1, 3))
NT = (((1,), (1,)), ((), ()))
NN = (((1,), (0,)), ((), ()))


def rounded_up(count):
    return -(-count // SUBLANES) * SUBLANES


def local_call(body, outs, args, kept=False, scratch=(), kinds={}, cost=None):
    spaces = {"smem": pltpu.SMEM, "vmem": pltpu.VMEM, "hbm": pltpu.HBM}
    shape_of = pltpu.VMEM if kept else jax.ShapeDtypeStruct
    arrays = [
        pltpu.with_memory_space_constraint(array, pltpu.HBM) if space == "hbm" else array
        for space, array in args
    ]
    results = pl.pallas_call(
        body,
        out_shape=[shape_of(shape, kinds.get(index, jnp.float32)) for index, shape in enumerate(outs)],
        in_specs=[pl.BlockSpec(memory_space=spaces[space]) for space, _ in args],
        out_specs=[pl.BlockSpec(memory_space=pltpu.VMEM) for _ in outs],
        scratch_shapes=scratch,
        compiler_params=pltpu.CompilerParams(vmem_limit_bytes=VMEM_LIMIT),
        cost_estimate=cost,
    )(*arrays)
    return list(results)


def vmem(*arrays):
    return [("vmem", array) for array in arrays]


def taker(refs):
    refs = list(refs)

    def take(count):
        return [refs.pop(0) for _ in range(count)]

    return take


def parts_of(values):
    high = values.astype(jnp.bfloat16).astype(jnp.float32)
    rest = values - high
    middle = rest.astype(jnp.bfloat16).astype(jnp.float32)
    return jnp.concatenate([high, middle, rest - middle], axis=0).astype(jnp.bfloat16)


def exact_product(values, onehot, dims):
    rows = values.shape[0]
    product = lax.dot_general(
        parts_of(values), onehot, dims, preferred_element_type=jnp.float32
    )
    return product[:rows] + product[rows : 2 * rows] + product[2 * rows :]


def as_onehot(mask):
    return jnp.where(mask, 1.0, 0.0).astype(jnp.bfloat16)


def contract_onehot(map_row, class_count):
    shape = (class_count, map_row.shape[1])
    return as_onehot(lax.broadcasted_iota(jnp.int32, shape, 0) == map_row)


def friction_of(classes, table_ref, levels):
    friction = jnp.zeros(classes.shape, jnp.float32)
    for level in range(levels):
        friction = jnp.where(classes == level, table_ref[level], friction)
    return friction


def folded(values):
    rows, width = values.shape
    total = values[:SUBLANES]
    for start in range(SUBLANES, rows, SUBLANES):
        total = total + values[start : start + SUBLANES]
    result = total[:, :LANES]
    for start in range(LANES, width, LANES):
        result = result + total[:, start : start + LANES]
    return result


def tree_sum(terms):
    while len(terms) > 1:
        terms = [a + b for a, b in zip(terms[0::2], terms[1::2])]
    return terms[0]


def swapped(message, axes, distance):
    count = lax.axis_size(axes)
    return lax.ppermute(message, axes, [(i, i ^ distance) for i in range(count)])


class Sizes:
    def __init__(self, hours, segs, pipes, chunk, classes, levels):
        self.hours, self.segs, self.pipes = hours, segs, pipes
        self.chunk, self.classes, self.levels = chunk, classes, levels
        self.blocks = lax.axis_size("pipe")
        self.hour_parts = lax.axis_size("hour")
        self.share = classes / (pipes * self.blocks)
        self.halves = pipes // LANES
        self.paired = self.hour_parts == 2
        self.end_rows = {True: 2 * hours, False: hours}
        self.sums = hours * segs
        self.first_ends = rounded_up(hours * chunk)
        self.seg_tail = {True: 5 * hours, False: 3 * hours}

    def owner(self, block, index):
        return lax.bitwise_xor(block, index)

    def pipe_order(self, phase):
        return PIPE_ORDERS[phase] if self.blocks == 4 else range(1, self.blocks)

    def ends_packed(self, first):
        return rounded_up(self.end_rows[first] * self.halves)

    def own_pipes(self, block):
        return pl.ds(pl.multiple_of(block * self.pipes, LANES), self.pipes)


def take_messages(sz, phase, take):
    own, *received = take(sz.blocks)
    by_distance = dict(zip(sz.pipe_order(phase), received))
    return [own] + [by_distance[distance] for distance in range(1, sz.blocks)]


def places():
    return lax.axis_index("pipe"), lax.axis_index("hour"), lax.axis_index("seg") == 0


def write_ends(sz, message, start, rows):
    for index, row in enumerate(rows):
        for half in range(sz.halves):
            at = start + half * len(rows) + index
            message[at : at + 1, :] = row[:, half * LANES : (half + 1) * LANES]


def read_ends(sz, message, start, count):
    pieces = [
        message[start + half * count : start + (half + 1) * count, :]
        for half in range(sz.halves)
    ]
    return jnp.concatenate(pieces, axis=1)


def write_edges(sz, message, first, first_seg, state, cost, resistance, spread, found):
    flow, pack, mass, momentum = state
    hours, last = sz.hours, sz.segs - 1
    top, bottom = slice(0, 1), slice(last, last + 1)
    for t in range(hours):
        gap = cost[t, bottom, :] - mass[t, bottom, :] - resistance * momentum[t, bottom, :]
        gradient = mass[t, top, :] - momentum[t, top, :] + spread[t, top, :]
        matched = found[t : t + 1, :]
        rows = [
            jnp.where(first_seg, matched, mass[t, top, :]),
            jnp.where(first_seg, momentum[t, bottom, :], gradient),
            jnp.where(first_seg, gap, matched),
        ]
        if first:
            rows.append(jnp.where(first_seg, flow[t, bottom, :], pack[t, top, :]))
            rows.append(found[hours + t : hours + t + 1, :])
        for slot, row in enumerate(rows):
            at = slot * hours + t
            message[at : at + 1, :] = row


def write_layers(sz, outs, first_hour, pack, mass, momentum, first_mass):
    segs = sz.segs
    top = lax.broadcasted_iota(jnp.int32, (segs, sz.pipes), 0) == 0
    gradient = mass - momentum + jnp.where(top, 0.0, pltpu.roll(momentum, 1, 0))
    if sz.paired:
        outs[0][0:segs, :] = jnp.where(first_hour, gradient, first_mass)
    else:
        outs[0][0:segs, :] = gradient
        outs[1][...] = first_mass
    if pack is not None:
        outs[0][segs : 2 * segs, :] = pack
    tail = outs[0].shape[0] - SUBLANES
    outs[0][tail:, :] = jnp.zeros((SUBLANES, sz.pipes), jnp.float32)
    outs[0][tail : tail + 1, :] = momentum[segs - 1 : segs, :]


def match_onehots(sz, block, inlet_side, matching, result):
    row = lax.broadcasted_iota(jnp.int32, (sz.pipes, sz.pipes), 0)

    @pl.when(inlet_side)
    def _():
        own = matching[0:1, sz.own_pipes(block)]
        for index in range(sz.blocks):
            result[index] = as_onehot(row + sz.owner(block, index) * sz.pipes == own)

    @pl.when(jnp.logical_not(inlet_side))
    def _():
        here = row + block * sz.pipes
        for index in range(sz.blocks):
            feeds = matching[0:1, sz.own_pipes(sz.owner(block, index))]
            result[index] = as_onehot(here == feeds)


def matched_rows(sz, inlet_side, ends, onehots, found):
    for side, dims in ((inlet_side, NN), (jnp.logical_not(inlet_side), NT)):

        @pl.when(side)
        def _(dims=dims):
            result = jnp.zeros(found.shape, jnp.float32)
            for index, values in enumerate(ends):
                result = result + exact_product(values, onehots[index], dims)
            found[...] = result


def prepare_kernel(sz, *refs):
    contract_map_in, classes_in, table_in, matching = refs[:4]
    onehots, matches, friction = refs[4:7]
    contract_map, classes, table, arrived = refs[7:]
    block, hour, first_seg = places()
    pairs = [
        (contract_map_in.at[:, sz.own_pipes(block)], contract_map),
        (classes_in, classes),
        (table_in, table),
    ]
    copies = [
        pltpu.make_async_copy(source, target, arrived.at[index])
        for index, (source, target) in enumerate(pairs)
    ]
    for copy in copies:
        copy.start()
    match_onehots(sz, block, jnp.logical_not(first_seg), matching, matches)
    for copy in copies:
        copy.wait()
    for t in range(sz.hours):
        onehots[t] = contract_onehot(contract_map[t : t + 1, :], sz.classes)
    friction[...] = friction_of(classes[...], table, sz.levels)


def prepare_scratch(sz):
    return [
        pltpu.VMEM((sz.hours, sz.pipes), jnp.int32),
        pltpu.VMEM((sz.segs, sz.pipes), jnp.int32),
        pltpu.SMEM((sz.levels,), jnp.float32),
        pltpu.SemaphoreType.DMA((3,)),
    ]


def start_kernel(sz, *refs):
    take = taker(refs)
    flow, mass, momentum, cost, classes_in, duals_in, table_in, matching_in = take(8)
    message, matching = take(2)
    flow_last, cost_last, mass_last, momentum_last, mass_first = take(5)
    duals, classes, table, arrived = take(4)
    block, hour, first_seg = places()
    hours, segs = sz.hours, sz.segs
    low, high = pl.ds(0, SUBLANES), pl.ds(segs - SUBLANES, SUBLANES)
    copies = [
        (flow.at[:, high], flow_last),
        (cost.at[:, high], cost_last),
        (mass.at[:, high], mass_last),
        (momentum.at[:, high], momentum_last),
        (mass.at[:, low], mass_first),
        (duals_in, duals),
        (classes_in.at[high], classes),
        (table_in, table),
        (matching_in, matching),
    ]
    copies = [
        pltpu.make_async_copy(source, target, arrived.at[index])
        for index, (source, target) in enumerate(copies)
    ]
    for copy in copies:
        copy.start()
    for copy in copies:
        copy.wait()
    end = SUBLANES - 1
    resistance = friction_of(classes[...], table, sz.levels)[end:]
    firsts = [mass_first[t, 0:1, :] for t in range(hours)]
    lasts = [flow_last[t, end : end + 1, :] for t in range(hours)]
    gaps = [
        cost_last[t, end : end + 1, :]
        - mass_last[t, end : end + 1, :]
        - resistance * momentum_last[t, end : end + 1, :]
        for t in range(hours)
    ]
    for t in range(hours):
        message[t * sz.chunk : (t + 1) * sz.chunk, :] = duals[t]
    rows = [jnp.where(first_seg, a, b) for a, b in zip(firsts + firsts, gaps + lasts)]
    write_ends(sz, message, sz.first_ends, rows)


def layers_kernel(sz, *refs):
    take = taker(refs)
    pack, mass, momentum, contract_map, started = take(5)
    block, hour, first_seg = places()
    end = sz.hours - 1
    write_layers(sz, refs[5:], hour == 0, pack[end], mass[end], momentum[end], mass[0])
    map_row = contract_map[end : end + 1, sz.own_pipes(block)].astype(jnp.float32)
    tail = refs[5].shape[0] - SUBLANES
    refs[5][tail + 1 : tail + 2, :] = map_row


def start_scratch(sz):
    ends = pltpu.VMEM((sz.hours, SUBLANES, sz.pipes), jnp.float32)
    return [ends] * 5 + [
        pltpu.VMEM((sz.hours, sz.chunk, sz.classes), jnp.float32),
        pltpu.VMEM((SUBLANES, sz.pipes), jnp.int32),
        pltpu.SMEM((sz.levels,), jnp.float32),
        pltpu.SemaphoreType.DMA((9,)),
    ]


def duals_kernel(sz, iteration, *refs):
    take = taker(refs)
    first = iteration == 0
    messages = take_messages(sz, iteration, take)
    prepared = take(1)
    old_duals = None if first else take(1)[0]
    old_weight = take(1)[0][0:1, 0:1] if iteration > 1 else 1.0
    duals, hour_message = take(2)
    scalars = None if first else take(1)[0]
    block = places()[0]
    hours, segs, chunk = sz.hours, sz.segs, sz.chunk
    if first:
        for index, ref in enumerate(messages):
            owner = sz.owner(block, index)
            rows = pl.ds(pl.multiple_of(owner * chunk, chunk), chunk)
            for t in range(hours):
                duals[t, rows, :] = ref[t * chunk : (t + 1) * chunk, :]
    else:
        dual_step = STEP_SCALE * old_weight
        dual_sq = jnp.zeros((SUBLANES, LANES), jnp.float32)
        for t in range(hours):
            totals = tree_sum([ref[t * segs : (t + 1) * segs, :] for ref in messages])
            change = dual_step * totals
            duals[t] = old_duals[t] - change
            dual_sq = dual_sq + folded(change * change)
        at = sz.sums + sz.ends_packed(False)
        write_squares([ref[at : at + SUBLANES, :] for ref in messages], dual_sq, scalars)
    hour_message[0:segs, :] = duals[hours - 1]
    if sz.paired:
        rest = (hour_message.shape[0] - segs, sz.classes)
        hour_message[segs:, :] = jnp.zeros(rest, jnp.float32)
    if sz.paired and not first:
        for part in (0, 1):
            at = segs + part
            hour_message[at : at + 1, :LANES] = scalars[0:1, part * LANES : (part + 1) * LANES]


def spread_kernel(sz, iteration, *refs):
    take = taker(refs)
    first = iteration == 0
    flow, pack, mass, momentum, cost, friction, onehots, matches = take(8)
    messages = take_messages(sz, iteration, take)
    hours_in = take(1 if sz.paired else 2)
    duals = take(1)[0]
    scalars = None if first else take(1)[0]
    map_in = take(1)[0] if first else None
    seg_message, spread = take(2)
    earlier_onehot = take(1)[0] if first else None
    found = take(1)[0]
    earlier_in, later_in = hours_in[0], hours_in[-1]
    block, hour, first_seg = places()
    hours, segs = sz.hours, sz.segs
    last = segs - 1

    ends_at, count = sz.first_ends if first else sz.sums, sz.end_rows[first]
    ends = [read_ends(sz, ref, ends_at, count) for ref in messages]
    matched_rows(sz, jnp.logical_not(first_seg), ends, matches, found)
    for t in range(hours):
        spread[t] = sz.share * exact_product(duals[t], onehots[t], NN)
    if first:
        tail = map_in.shape[0] - SUBLANES
        map_row = map_in[tail + 1 : tail + 2, :].astype(jnp.int32)
        earlier_onehot[...] = contract_onehot(map_row, sz.classes)

    state = (flow, pack, mass, momentum)
    resistance = friction[last:segs, :]
    write_edges(sz, seg_message, first, first_seg, state, cost, resistance, spread, found)
    at = sz.seg_tail[first]
    seg_message[at:, :] = jnp.zeros((seg_message.shape[0] - at, sz.pipes), jnp.float32)
    if not first:
        seg_message[at : at + 1, : 2 * LANES] = scalars[0:1, :]
    tail = earlier_in.shape[0] - SUBLANES
    seg_message[at + 1 : at + 2, :] = jnp.where(
        first_seg, earlier_in[tail : tail + 1, :], later_in[0:1, :]
    )


def write_squares(squares, dual_sq, scalars):
    total = tree_sum(squares)
    scalars[...] = jnp.zeros(scalars.shape, jnp.float32)
    scalars[0:1, :LANES] = total[0:1]
    scalars[0:1, LANES:] = total[1:2] + jnp.sum(dual_sq, axis=0, keepdims=True)


def new_weight(weight, total):
    primal = jnp.sum(total[:, :LANES], axis=1, keepdims=True)
    dual = jnp.sum(total[:, LANES : 2 * LANES], axis=1, keepdims=True)
    return jnp.sqrt(weight * jnp.sqrt((dual + NORM_EPS) / (primal + NORM_EPS)))


def step(sz, block, hour, first_seg, weight, state, data, halo, spread_of, outs, message, kept):
    flow, pack, mass, momentum = state
    cost, injection, resistance, target = data
    flow_out, pack_out, mass_out, momentum_out = outs
    edge_flow_out, edge_pack_out, earlier_pack_out = kept
    hours, segs, pipes = sz.hours, sz.segs, sz.pipes
    last, end = segs - 1, hours - 1
    has_earlier = hour > 0
    has_later = hour < sz.hour_parts - 1
    primal_step = STEP_SCALE / weight
    dual_step = STEP_SCALE * weight

    row_index = lax.broadcasted_iota(jnp.int32, (segs, pipes), 0)
    top, bottom = row_index == 0, row_index == last

    def from_above(values, row):
        return jnp.where(top, row, pltpu.roll(values, 1, 0))

    def from_below(values, row):
        return jnp.where(bottom, row, pltpu.roll(values, segs - 1, 0))

    def seg_row(slot, t):
        at = slot * hours + t
        return halo["seg"][at : at + 1, :]

    def new_flow(start, gap):
        return jnp.clip(start - primal_step * gap, -FLOW_CAP, FLOW_CAP)

    def new_pack(start, gradient):
        return jnp.clip(start + primal_step * gradient, 0.0, PACK_CAP)

    corner = halo["corner"]
    earlier_pack = halo["earlier_pack"]
    earlier_gradient = (
        halo["earlier"][0:segs, :]
        + halo["earlier_spread"]
        + jnp.where(top, jnp.where(first_seg, 0.0, corner), 0.0)
        - mass[0]
    )
    earlier_next = new_pack(earlier_pack, earlier_gradient)
    earlier_bar = jnp.where(has_earlier, 2.0 * earlier_next - earlier_pack, 0.0)
    if earlier_pack_out is not None:
        earlier_pack_out[...] = earlier_next
    later_mass = jnp.where(has_later, halo["later"][0:segs, :], 0.0)
    later_corner = jnp.where(has_later, corner, 0.0)
    primal_sq = jnp.zeros((SUBLANES, LANES), jnp.float32)
    dual_sq = jnp.zeros((SUBLANES, LANES), jnp.float32)
    for t in range(hours):
        mass_now, momentum_now = mass[t], momentum[t]
        flow_now, pack_now = flow[t], pack[t]
        spread, onehot = spread_of(t)
        below_mass = seg_row(0, t)
        next_mass = mass[t + 1] if t < end else later_mass
        gap = cost[t] - (
            mass_now - from_below(mass_now, below_mass) + resistance * momentum_now
        )
        flow_next = new_flow(flow_now, gap)
        above_momentum = jnp.where(first_seg, 0.0, seg_row(1, t))
        gradient = (
            mass_now
            - next_mass
            - momentum_now
            + from_above(momentum_now, above_momentum)
            + spread
        )
        pack_next = new_pack(pack_now, gradient)
        flow_bar = 2.0 * flow_next - flow_now
        pack_bar = 2.0 * pack_next - pack_now

        edge_flow, edge_pack = halo["edges"](t)
        edge_gap = seg_row(2, t) + mass_now[0:1, :]
        edge_flow_next = new_flow(edge_flow, edge_gap)
        edge_flow_bar = 2.0 * edge_flow_next - edge_flow
        edge_later = seg_row(0, t + 1) if t < end else later_corner
        edge_gradient = seg_row(1, t) + momentum_now[last : last + 1, :] - edge_later
        edge_pack_next = new_pack(edge_pack, edge_gradient)
        edge_pack_bar = jnp.where(first_seg, 2.0 * edge_pack_next - edge_pack, 0.0)
        if edge_flow_out is not None:
            edge_flow_out[t : t + 1, :] = edge_flow_next
            edge_pack_out[t : t + 1, :] = edge_pack_next

        mass_rows = pack_bar - earlier_bar + flow_bar - from_above(flow_bar, edge_flow_bar)
        momentum_rows = resistance * flow_bar - (pack_bar - from_below(pack_bar, edge_pack_bar))
        mass_change = dual_step * (injection[t] - mass_rows)
        momentum_change = dual_step * momentum_rows
        flow_out[t] = flow_next
        pack_out[t] = pack_next
        mass_out[t] = mass_now + mass_change
        momentum_out[t] = momentum_now - momentum_change
        flow_change, pack_change = flow_next - flow_now, pack_next - pack_now
        primal_sq = primal_sq + folded(flow_change * flow_change + pack_change * pack_change)
        dual_sq = dual_sq + folded(
            mass_change * mass_change + momentum_change * momentum_change
        )
        message[t * segs : (t + 1) * segs, :] = sz.share * exact_product(pack_bar, onehot, NT)
        rows = pl.ds(pl.multiple_of(t * segs + block * sz.chunk, sz.chunk), sz.chunk)
        message[rows, :] = message[rows, :] - target[t]
        earlier_bar = pack_bar

    at = message.shape[0] - SUBLANES
    message[at:, :] = jnp.zeros((SUBLANES, LANES), jnp.float32)
    message[at : at + 1, :] = jnp.sum(primal_sq, axis=0, keepdims=True)
    message[at + 1 : at + 2, :] = jnp.sum(dual_sq, axis=0, keepdims=True)


def write_next(sz, hour, first_seg, outs, cost, resistance, message, hour_messages):
    flow, pack, mass, momentum = outs
    last = sz.segs - 1
    firsts = [mass[t, 0:1, :] for t in range(sz.hours)]
    gaps = [
        cost[t, last : last + 1, :]
        - mass[t, last : last + 1, :]
        - resistance[last : last + 1, :] * momentum[t, last : last + 1, :]
        for t in range(sz.hours)
    ]
    rows = [jnp.where(first_seg, a, b) for a, b in zip(firsts, gaps)]
    write_ends(sz, message, sz.sums, rows)
    end = sz.hours - 1
    write_layers(sz, hour_messages, hour == 0, None, mass[end], momentum[end], mass[0])


def step_kernel(sz, iteration, final, *refs):
    take = taker(refs)
    first = iteration == 0
    state, data = take(4), take(2)
    friction, onehots, earlier_onehot, target, spread = take(5)
    corner_scalars = take(1) if sz.paired and not first else []
    seg_in, hours_in, duals_in = take(1)[0], take(1 if sz.paired else 2), take(1)[0]
    known = [] if first else take(3)
    old_weight = take(1)[0][0:1, 0:1] if iteration > 1 else 1.0
    scalars = [] if first else take(1)
    outs, message = take(4), take(1)[0]
    weight_out = [] if first else take(1)
    kept = [None] * 3 if final else take(3)
    hour_messages = [] if final else take(1 if sz.paired else 2)
    block, hour, first_seg = places()
    hours, segs = sz.hours, sz.segs
    weight = jnp.ones((1, 1), jnp.float32)
    if not first:
        total = scalars[0][0:1, :]
        if sz.paired:


            def sums_of(ref):
                parts = [ref[segs + part : segs + part + 1, :LANES] for part in (0, 1)]
                return jnp.concatenate(parts, axis=1)

            total = tree_sum(
                [
                    total,
                    seg_in[sz.seg_tail[False] : sz.seg_tail[False] + 1, : 2 * LANES],
                    sums_of(duals_in),
                sums_of(corner_scalars[0]),
                ]
            )
        weight = new_weight(old_weight, total)
        weight_out[0][...] = jnp.broadcast_to(weight, weight_out[0].shape)
    earlier_spread = sz.share * exact_product(duals_in[0:segs, :], earlier_onehot[...], NN)

    def spread_of(t):
        return spread[t], onehots[t]

    def edges(t):
        if not first:
            return known[0][t : t + 1, :], known[1][t : t + 1, :]
        shared, matched = [slot * hours + t for slot in (3, 4)]
        sent = seg_in[shared : shared + 1, :]
        return jnp.where(first_seg, seg_in[matched : matched + 1, :], sent), sent

    at = sz.seg_tail[first] + 1
    halo = {
        "seg": seg_in,
        "corner": seg_in[at : at + 1, :],
        "earlier": hours_in[0],
        "earlier_pack": hours_in[0][segs : 2 * segs, :] if first else known[2][...],
        "edges": edges,
        "later": hours_in[-1],
        "earlier_spread": earlier_spread,
    }
    resistance = friction[...]
    data = [*data, resistance, target]
    step(sz, block, hour, first_seg, weight, state, data, halo, spread_of, outs, message, kept)
    if not final:
        write_next(sz, hour, first_seg, outs, data[0], resistance, message, hour_messages)


def close_kernel(sz, *refs):
    take = taker(refs)
    messages = take_messages(sz, ITERS, take)
    old_duals, weight, written, duals, scalars = take(5)
    block, hour, first_seg = places()
    segs = sz.segs
    dual_step = STEP_SCALE * weight[0:1, 0:1]
    dual_sq = jnp.zeros((SUBLANES, LANES), jnp.float32)
    start = block * sz.chunk
    for t in range(sz.hours):
        totals = tree_sum([ref[t * segs : (t + 1) * segs, :] for ref in messages])
        change = dual_step * totals
        dual_sq = dual_sq + folded(change * change)
        own = pl.ds(pl.multiple_of(start, sz.chunk), sz.chunk)
        rows = pl.ds(pl.multiple_of(t * segs + start, sz.chunk), sz.chunk)
        own_totals = tree_sum([ref[rows, :] for ref in messages])
        duals[t] = old_duals[t, own, :] - dual_step * own_totals
    total = tree_sum([ref[sz.sums : sz.sums + SUBLANES, :] for ref in messages])
    scalars[...] = jnp.zeros(scalars.shape, jnp.float32)
    scalars[0:1, :] = total[0:1]
    scalars[1:2, :] = total[1:2] + jnp.sum(dual_sq, axis=0, keepdims=True)


def written_out(state):
    count = len(state)

    def body(*refs):
        sources, targets, token, done = refs[:count], refs[count:-2], refs[-2], refs[-1]
        copies = [
            pltpu.make_async_copy(source, target, done.at[index])
            for index, (source, target) in enumerate(zip(sources, targets))
        ]
        for copy in copies:
            copy.start()
        token[...] = jnp.zeros(token.shape, jnp.float32)
        for copy in copies:
            copy.wait()

    return pl.pallas_call(
        body,
        out_shape=[pltpu.HBM(array.shape, array.dtype) for array in state]
        + [pltpu.VMEM((SUBLANES, LANES), jnp.float32)],
        in_specs=[pl.BlockSpec(memory_space=pltpu.VMEM) for _ in state],
        out_specs=[pl.BlockSpec(memory_space=pltpu.HBM) for _ in state]
        + [pl.BlockSpec(memory_space=pltpu.VMEM)],
        scratch_shapes=[pltpu.SemaphoreType.DMA((count,))],
        compiler_params=pltpu.CompilerParams(vmem_limit_bytes=VMEM_LIMIT),
    )(*state)


def side_by_side(rows):
    return jnp.concatenate([rows[0:1], rows[1:2]], axis=1)


def weight_kernel(weight, *refs):
    *scalars, result = refs
    if len(scalars) == 4:
        own, *received = scalars
        by_distance = dict(zip(CORNER_ORDER, received))
        scalars = [own, by_distance[1], by_distance[2], by_distance[3]]
    result[...] = new_weight(weight[0:1, 0:1], side_by_side(tree_sum([ref[0:2, :] for ref in scalars])))


def gathered(sz, phase, message):
    return [message] + [swapped(message, "pipe", k) for k in sz.pipe_order(phase)]


def layers_exchanged(sz, hour_messages):
    if sz.paired:
        return [swapped(hour_messages[0], "hour", 1)]
    steps = range(sz.hour_parts - 1)
    return [
        lax.ppermute(hour_messages[0], "hour", [(i, i + 1) for i in steps]),
        lax.ppermute(hour_messages[1], "hour", [(i + 1, i) for i in steps]),
    ]


def on_device(
    segment_flow,
    linepack,
    mass_dual,
    momentum_dual,
    contract_dual,
    flow_cost,
    injection,
    contract_target,
    friction_table,
    friction_class,
    matching,
    contract_map,
):
    hours, segs, pipes = segment_flow.shape
    chunk, classes = contract_dual.shape[2:]
    sz = Sizes(hours, segs, pipes, chunk, classes, friction_table.shape[0])
    duals_now = contract_dual.reshape(hours, chunk, classes)
    target_now = contract_target.reshape(hours, chunk, classes)
    matching = matching.reshape(1, matching.shape[0])
    cells, contracts = (hours, segs, pipes), (hours, segs, classes)
    layer_shapes = [(segs + SUBLANES, pipes)]
    if not sz.paired:
        layer_shapes.append((segs, pipes))
    known_shapes = [(rounded_up(hours), pipes)] * 2 + [(segs, pipes)]
    scalars_shape = (SUBLANES, 2 * LANES)

    state = [segment_flow, linepack, mass_dual, momentum_dual]
    raw = [segment_flow, mass_dual, momentum_dual, flow_cost, friction_class, duals_now]
    raw += [friction_table, matching]
    message, matching = local_call(
        functools.partial(start_kernel, sz),
        [
            (sz.first_ends + sz.ends_packed(True), classes),
            matching.shape,
        ],
        [("hbm", array) for array in raw],
        kept=True,
        scratch=start_scratch(sz),
        kinds={1: jnp.int32},
    )
    hour_messages = local_call(
        functools.partial(layers_kernel, sz),
        [(2 * segs + SUBLANES, pipes), *layer_shapes[1:]],
        vmem(linepack, mass_dual, momentum_dual, contract_map, matching),
        kept=True,
    )
    onehots, matches, friction = local_call(
        functools.partial(prepare_kernel, sz),
        [(hours, classes, pipes), (sz.blocks, pipes, pipes), (segs, pipes)],
        [("hbm", array) for array in (contract_map, friction_class, friction_table)]
        + vmem(matching),
        kept=True,
        scratch=prepare_scratch(sz),
        cost=pl.CostEstimate(flops=PREP_FLOPS, bytes_accessed=1 << 20, transcendentals=0),
        kinds={0: jnp.bfloat16, 1: jnp.bfloat16},
    )
    duals, weight, known, earlier_onehot = [], [], [], None
    for iteration in range(ITERS):
        first, final = iteration == 0, iteration == ITERS - 1
        messages = gathered(sz, iteration, message)
        hours_in = layers_exchanged(sz, hour_messages)
        seg_rows = rounded_up(sz.seg_tail[first] + 2)
        duals_rows = segs
        if sz.paired:
            duals_rows = max(segs + SUBLANES, seg_rows * sz.halves + SUBLANES)
        full_duals, duals_message, *scalars = local_call(
            functools.partial(duals_kernel, sz, iteration),
            [contracts, (duals_rows, classes)] + ([] if first else [scalars_shape]),
            vmem(*messages, friction, *duals, *weight),
            kept=True,
        )
        duals = [full_duals]
        args = vmem(*state, flow_cost, friction, onehots, matches)
        args += vmem(*messages, *hours_in, *duals, *scalars, *(hours_in[:1] if first else []))
        seg_message, spread, *built = local_call(
            functools.partial(spread_kernel, sz, iteration),
            [(seg_rows, pipes), cells] + ([(classes, pipes)] if first else []),
            args,
            kept=True,
            scratch=[pltpu.VMEM((sz.end_rows[first], pipes), jnp.float32)],
            kinds={2: jnp.bfloat16},
        )
        earlier_onehot = built[0] if first else earlier_onehot
        seg_in = swapped(seg_message, "seg", 1)
        if sz.paired:
            duals_in = swapped(duals_message, "hour", 1)
            corner_in = [swapped(duals_message, ("hour", "seg"), 3) for part in scalars]
        else:
            steps = range(sz.hour_parts - 1)
            duals_in = lax.ppermute(duals_message, "hour", [(i, i + 1) for i in steps])
            scalars = [lax.psum(part, ("hour", "seg")) for part in scalars]
            corner_in = []
        args = vmem(
            *state, flow_cost, injection, friction, onehots, earlier_onehot, target_now, spread
        )
        args += vmem(*corner_in, seg_in, *hours_in, duals_in, *known, *weight, *scalars)
        message_rows = sz.sums + SUBLANES + (0 if final else sz.ends_packed(False))
        outs = [cells] * 4 + [(message_rows, classes)]
        outs += [] if first else [(SUBLANES, LANES)]
        results = local_call(
            functools.partial(step_kernel, sz, iteration, final),
            outs + ([] if final else known_shapes + layer_shapes),
            args,
            kept=True,
        )
        state, message, rest = results[:4], results[4], results[5:]
        weight, rest = ([], rest) if first else (rest[:1], rest[1:])
        known, hour_messages = rest[:3], rest[3:]
    *state, written = written_out(state)
    contract_out, scalars = local_call(
        functools.partial(close_kernel, sz),
        [(hours, chunk, classes), (SUBLANES, LANES)],
        vmem(*gathered(sz, ITERS, message), *duals, *weight, written),
        kept=True,
    )
    if sz.paired:
        sums = [scalars] + [swapped(scalars, ("hour", "seg"), k) for k in CORNER_ORDER]
    else:
        sums = [lax.psum(scalars, ("hour", "seg"))]
    (weight,) = local_call(weight_kernel, [(1, 1)], vmem(*weight, *sums))
    return (
        *state,
        contract_out.reshape(contract_dual.shape),
        weight.reshape(1),
    )


def solution(mesh):
    cells = P(("groups", "hour"), "seg", "pipe")
    contracts = P(("groups", "hour"), "seg", "pipe", None)
    return jax.shard_map(
        on_device,
        mesh=mesh,
        in_specs=(
            cells,
            cells,
            cells,
            cells,
            contracts,
            cells,
            cells,
            contracts,
            P(),
            P("seg", ("groups", "pipe")),
            P("groups"),
            P(("groups", "hour"), None),
        ),
        out_specs=(cells, cells, cells, cells, contracts, P("groups")),
        check_vma=False,
    )
```
